32 devices in a mesh: dp: 8 (over y, x, core), tensor: 4 (over z).
Axes of the slice: x: 2, y: 2, z: 4, core: 2. Of those that a mesh axis runs over, the one named last changes fastest.
Arguments:
- inputs: bfloat16 [16384, 1536], P('dp'), may hold values from -6 to 6
- gain_attn: float32 [1536], replicated, may hold values from 0.5 to 1.5
- w_query: bfloat16 [1536, 1536], P(None, 'tensor'), may hold values from -0.15625 to 0.15625
- w_key: bfloat16 [1536, 1536], P(None, 'tensor'), may hold values from -0.15625 to 0.15625
- w_value: bfloat16 [1536, 1536], P(None, 'tensor'), may hold values from -0.15625 to 0.15625
- w_outgate: bfloat16 [1536, 1536], P(None, 'tensor'), may hold values from -0.15625 to 0.15625
- w_forget: bfloat16 [1536, 24], P(None, 'tensor'), may hold values from -0.15625 to 0.15625
- forget_bias: float32 [24], P('tensor'), may hold values from 2 to 8
- w_out: bfloat16 [1536, 1536], P(None, 'tensor'), may hold values from -0.625 to 0.625
- gain_mlp: float32 [1536], replicated, may hold values from 0.5 to 1.5
- w_gate: bfloat16 [1536, 4096], P(None, 'tensor'), may hold values from -0.15625 to 0.15625
- w_up: bfloat16 [1536, 4096], P(None, 'tensor'), may hold values from -0.15625 to 0.15625
- w_down: bfloat16 [1536, 4096], P(None, 'tensor'), may hold values from -0.09375 to 0.09375
- segment_ids: int32 [16, 1024], P('dp'), may hold values from 0 to 2, never falling along the last dimension, each value on 1 to 768 neighbouring positions
- cotangent: bfloat16 [16384, 1536], P('dp'), may hold values from -6 to 6
Outputs:
- output: float32 [16384, 1536], P(('dp', 'tensor'))
- grad_inputs: float32 [16384, 1536], P(('dp', 'tensor'))
- grad_gain_attn: float32 [1536], replicated
- grad_w_query: float32 [1536, 1536], P('dp', 'tensor')
- grad_w_key: float32 [1536, 1536], P('dp', 'tensor')
- grad_w_value: float32 [1536, 1536], P('dp', 'tensor')
- grad_w_outgate: float32 [1536, 1536], P('dp', 'tensor')
- grad_w_forget: float32 [1536, 24], P('dp', 'tensor')
- grad_forget_bias: float32 [24], P('tensor')
- grad_w_out: float32 [1536, 1536], P('dp', 'tensor')
- grad_gain_mlp: float32 [1536], replicated
- grad_w_gate: float32 [1536, 4096], P('dp', 'tensor')
- grad_w_up: float32 [1536, 4096], P('dp', 'tensor')
- grad_w_down: float32 [1536, 4096], P('dp', 'tensor')
The draws below stay inside these ranges and needn't reach their ends.
Inputs may be any that keep to these rules, and one draw needn't show every extreme that they name: `segment_ids`: within each packed row the document numbers never fall; attention stays inside a document.
All inputs are finite; a program needn't handle non-finite values.
Results may differ from the reference program's by a relative error of at most 0.035.
Values may be sent and summed in bfloat16 or wider, within the bound.
No kernel may reach another device: no remote copies, remote signals or barrier semaphores. Data moves between devices by JAX's collectives and lax.ppermute only.
A program may use at most 320 MiB of HBM per device.

```python
import math
from functools import partial
import jax
import jax.numpy as jnp
import numpy as np
from jax import lax

D = 1536
HEADS = 24
FF = 4096
SEQ = 1024
HD = 1536
PACKS = 16
TOKENS = 16384
N_TENSOR = 4


def levels(own_key, dims, shards, smallest, top_value):
    def one(dim, blocks):
        steps = jax.random.uniform(jax.random.fold_in(jax.random.fold_in(own_key, 6), dim), (blocks,), jnp.float32, smallest / len(shards), top_value / len(shards))
        return jnp.repeat(jnp.exp(steps), dims[dim] // blocks).reshape((-1,) + (1,) * (len(dims) - dim - 1))

    gain = one(*shards[0])
    for cut in shards[1:]:
        gain = gain * one(*cut)
    return gain


def split_up(amount, total, most, slope):
    weights = [(1 << 20) // math.isqrt(standing ** slope) + 1 for standing in range(2, amount + 1)]
    rest, counts = total - most - (amount - 1), [1] * (amount - 1)
    while rest > 0:
        free = [i for i in range(amount - 1) if counts[i] < most]
        mass, budget = sum([weights[i] for i in free]), rest
        for i in free:
            more = min(most - counts[i], max(1, budget * weights[i] // mass), rest)
            counts[i] = counts[i] + more
            rest = rest - more
    return np.array([most] + counts)


def uneven_parts(own_key, number_of, total, limit, slope):
    if number_of == 2:
        one = jax.random.randint(own_key, (), max(1, total - limit), min(limit, total - 1) + 1)
        return jnp.stack([one, total - one])
    tallies = jnp.asarray(split_up(number_of, total, limit, slope), jnp.int32)
    pairs = (number_of - 1) // 2
    giver, receiver = tallies[1:1 + 2 * pairs:2], tallies[2:2 + 2 * pairs:2]
    slack = jnp.minimum(giver - 1, limit - receiver)
    moved = jax.random.randint(jax.random.fold_in(own_key, 1), (pairs,), 0, 1 << 20) % (slack + 1)
    tallies = tallies.at[1:1 + 2 * pairs:2].set(giver - moved).at[2:2 + 2 * pairs:2].set(receiver + moved)
    return tallies[jax.random.permutation(jax.random.fold_in(own_key, 2), number_of)]


def normal_values(stream_key, dims, scale, limit, cuts=(), dtype=jnp.bfloat16):
    factor_of = levels(stream_key, dims, cuts, -0.22, 0.18) if cuts else 1.0
    values = jax.random.normal(stream_key, dims, jnp.float32) * scale * factor_of
    return jnp.minimum(jnp.maximum(values, -limit), limit).astype(dtype)


def setup_inputs(seed: int = 0) -> dict:
    streams_of = jax.random.split(jax.random.key(seed), 16)
    inputs = normal_values(streams_of[0], (TOKENS, D), 1.0, 6.0, ((0, 8),))
    gain_attn = jnp.clip(1.0 + 0.1 * jax.random.normal(streams_of[1], (D,), jnp.float32), 0.5, 1.5)
    w_query = normal_values(streams_of[2], (D, HD), D ** -0.5, 0.15625, ((1, 4),))
    w_key = normal_values(streams_of[3], (D, HD), D ** -0.5, 0.15625, ((1, 4),))
    w_value = normal_values(streams_of[4], (D, HD), D ** -0.5, 0.15625, ((1, 4),))
    w_outgate = normal_values(streams_of[5], (D, HD), D ** -0.5, 0.15625, ((1, 4),))
    w_forget = normal_values(streams_of[6], (D, HEADS), D ** -0.5, 0.15625, ((1, 4),))
    forget_bias = jnp.clip(2.0 + 6.0 * jax.random.uniform(streams_of[7], (HEADS,), jnp.float32) ** levels(streams_of[7], (HEADS,), ((0, 4),), -0.2, 0.2), 2.0, 8.0)
    w_out = normal_values(streams_of[8], (D, HD), (HD // 16) ** -0.5, 0.625, ((1, 4),))
    gain_mlp = jnp.clip(1.0 + 0.1 * jax.random.normal(streams_of[9], (D,), jnp.float32), 0.5, 1.5)
    w_gate = normal_values(streams_of[10], (D, FF), D ** -0.5, 0.15625, ((1, 4),))
    w_up = normal_values(streams_of[11], (D, FF), D ** -0.5, 0.15625, ((1, 4),))
    w_down = normal_values(streams_of[12], (D, FF), FF ** -0.5, 0.09375, ((1, 4),))
    segment_ids = jax.vmap(lambda own: jnp.searchsorted(jnp.cumsum(uneven_parts(own, 3, SEQ, 3 * SEQ // 4, 0)), jnp.arange(SEQ), side="right"))(jax.random.split(streams_of[13], PACKS)).reshape((PACKS, SEQ)).astype(jnp.int32)
    cotangent = normal_values(streams_of[14], (TOKENS, D), 1.0, 6.0, ((0, 8),))
    return {"inputs": inputs, "gain_attn": gain_attn, "w_query": w_query, "w_key": w_key, "w_value": w_value, "w_outgate": w_outgate, "w_forget": w_forget, "forget_bias": forget_bias, "w_out": w_out, "gain_mlp": gain_mlp, "w_gate": w_gate, "w_up": w_up, "w_down": w_down, "segment_ids": segment_ids, "cotangent": cotangent}


@jax.custom_vjp
def low(v):
    return lax.optimization_barrier(v.astype(jnp.bfloat16)).astype(jnp.float32)

@jax.custom_vjp
def low_back(v):
    return v

def low_keep(v):
    return (low(v), None)

def low_pass(kept, grad):
    return (grad,)

def back_keep(v):
    return (v, None)

def back_low(kept, grad):
    return (low(grad),)
low.defvjp(low_keep, low_pass)
low_back.defvjp(back_keep, back_low)
eps = 1e-06
top_precision = lax.Precision.HIGHEST

def project(left, right):
    return jnp.dot(left, right, precision=top_precision)

def normalize(values, scale_gain):
    return values * lax.rsqrt(lax.optimization_barrier(jnp.mean(values * values, axis=-1, keepdims=True)) + eps) * scale_gain

def grouped_sum(left, right):
    token_count = left.shape[0]
    split_left = left.reshape(token_count, N_TENSOR, left.shape[1] // N_TENSOR)
    split_right = right.reshape(right.shape[0], N_TENSOR, right.shape[1] // N_TENSOR)
    partials = jnp.einsum('tgk,dgk->gtd', split_left, split_right, precision=top_precision)
    return lax.optimization_barrier(jnp.sum(low(partials), axis=0))

def log_keep(values):
    return jnp.minimum(values, 0.0) - jnp.log1p(jnp.exp(-jnp.abs(values)))

def attend_row(pieces):
    queries, key_rows, value_rows, log_rates, segment = pieces
    length = queries.shape[0]
    running = jnp.cumsum(log_rates, axis=0)
    content = low_back(jnp.einsum('qhd,khd->hqk', queries, key_rows, precision=top_precision) * queries.shape[-1] ** (-0.5))
    scores = content + running.T[:, :, None] - running.T[:, None, :]
    causal = jnp.arange(length)[:, None] >= jnp.arange(length)[None, :]
    allowed = causal & (segment[:, None] == segment[None, :])
    scores = jnp.where(allowed[None], scores, -1e+30)
    row_peak = lax.optimization_barrier(jnp.max(scores, axis=-1, keepdims=True))
    numerators = jnp.exp(scores - row_peak)
    attn_weights = low(numerators / lax.optimization_barrier(jnp.sum(numerators, axis=-1, keepdims=True)))
    return low_back(jnp.einsum('hqk,khd->qhd', attn_weights, value_rows, precision=top_precision))

def layer(segment_ids, inputs, gain_attn, w_query, w_key, w_value, w_outgate, w_forget, forget_bias, w_out, gain_mlp, w_gate, w_up, w_down):
    row_count, length = segment_ids.shape
    token_count = inputs.shape[0]
    head_count = w_forget.shape[1]
    normed = low(normalize(inputs, gain_attn))
    queries = low(low_back(project(normed, w_query)))
    key_rows = low(low_back(project(normed, w_key)))
    value_rows = low(low_back(project(normed, w_value)))
    outgate = low_back(project(normed, w_outgate))
    forget = low_back(project(normed, w_forget) + forget_bias)
    log_rates = log_keep(forget)
    row_shape = (row_count, length, head_count, -1)
    attended = lax.map(jax.checkpoint(attend_row), (queries.reshape(row_shape), key_rows.reshape(row_shape), value_rows.reshape(row_shape), log_rates.reshape(row_count, length, head_count), segment_ids))
    attended = attended.reshape(token_count, -1)
    gated = low(attended * jax.nn.sigmoid(outgate))
    hidden_state = inputs + low_back(grouped_sum(gated, w_out))
    normed_mlp = low(normalize(hidden_state, gain_mlp))
    gate_pre = low_back(project(normed_mlp, w_gate))
    up_pre = low_back(project(normed_mlp, w_up))
    hidden = low(gate_pre * jax.nn.sigmoid(gate_pre) * up_pre)
    return hidden_state + low_back(grouped_sum(hidden, w_down))

def reference(inputs, gain_attn, w_query, w_key, w_value, w_outgate, w_forget, forget_bias, w_out, gain_mlp, w_gate, w_up, w_down, segment_ids, cotangent):
    params = (inputs, gain_attn, w_query, w_key, w_value, w_outgate, w_forget, forget_bias, w_out, gain_mlp, w_gate, w_up, w_down)
    floats = tuple((p.astype(jnp.float32) for p in params))
    output, pullback = jax.vjp(partial(layer, segment_ids), *floats)
    grads = pullback(cotangent.astype(jnp.float32))
    return (output, grads[0], grads[1], grads[2], grads[3], grads[4], grads[5], grads[6], grads[7], grads[8], grads[9], grads[10], grads[11], grads[12])
```

```python
import jax
import jax.numpy as jnp
from jax import lax
from jax.sharding import PartitionSpec as P
from jax.experimental import pallas as pl
from jax.experimental.pallas import tpu as pltpu

LOG2E = 1.4426950408889634
LN2 = 0.6931471805599453
HEAD = 64
BLK = 256

def last(a, b):
    return lax.dot_general(a, b, (((1,), (1,)), ((), ())), preferred_element_type=jnp.float32)
def first(a, b):
    return lax.dot_general(a, b, (((0,), (0,)), ((), ())), preferred_element_type=jnp.float32)
def mm(a, b):
    return jnp.dot(a, b, preferred_element_type=jnp.float32)

def fwd_kernel(q_ref, k_ref, v_ref, g_ref, crow_ref, scol_ref, srow_ref, z_ref, o_ref, lse_ref):
    length, width = q_ref.shape
    hp = width // HEAD
    lane = lax.broadcasted_iota(jnp.int32, (1, width), 1) // HEAD
    tri = lax.broadcasted_iota(jnp.int32, (BLK, BLK), 0) >= lax.broadcasted_iota(jnp.int32, (BLK, BLK), 1)
    for i in range(length // BLK):
        rows = pl.ds(i * BLK, BLK)
        reach = (i + 1) * BLK
        q = q_ref[rows, :]
        same = scol_ref[rows, :] == srow_ref[:, :reach]
        if i:
            allowed = jnp.concatenate([same[:, :reach - BLK], same[:, reach - BLK:] & tri], axis=1)
        else:
            allowed = same & tri
        out = jnp.zeros((BLK, width), jnp.float32)
        stats = jnp.zeros((BLK, 128), jnp.float32)
        for h in range(hp):
            s = last(jnp.where(lane == h, q, 0), k_ref[:reach, :])
            s = jnp.where(allowed, s - crow_ref[0, h:h + 1, :reach], -1e30)
            top = jnp.max(s, axis=1, keepdims=True)
            e = jnp.exp2(s - top)
            total = jnp.sum(e, axis=1, keepdims=True)
            part = mm(e.astype(jnp.bfloat16), v_ref[:reach, :])
            out = jnp.where(lane == h, part * (1.0 / total), out)
            stats = jnp.where(lax.broadcasted_iota(jnp.int32, (BLK, 128), 1) == h, top + jnp.log2(total), stats)
        g = g_ref[rows, :].astype(jnp.float32)
        z_ref[rows, :] = (out * jax.nn.sigmoid(g)).astype(jnp.bfloat16)
        o_ref[rows, :] = out.astype(jnp.bfloat16)
        lse_ref[0, :, i * BLK:(i + 1) * BLK] = stats.T[:hp, :]

def attend_forward(q, k, v, g, crow, scol, srow):
    length, n = q.shape
    heads = n // HEAD
    hp = 2 if heads % 2 == 0 else heads
    steps = heads // hp
    width = hp * HEAD
    blk = pl.BlockSpec((length, width), lambda i: (0, i))
    return pl.pallas_call(
        fwd_kernel,
        grid=(steps,),
        in_specs=[blk] * 4 + [pl.BlockSpec((1, hp, length), lambda i: (i, 0, 0)),
                  pl.BlockSpec((length, 1), lambda i: (0, 0)), pl.BlockSpec((1, length), lambda i: (0, 0))],
        out_specs=[blk, blk, pl.BlockSpec((1, hp, length), lambda i: (i, 0, 0))],
        out_shape=[jax.ShapeDtypeStruct((length, n), jnp.bfloat16), jax.ShapeDtypeStruct((length, n), jnp.bfloat16),
                   jax.ShapeDtypeStruct((steps, hp, length), jnp.float32)],
        compiler_params=pltpu.CompilerParams(vmem_limit_bytes=40 << 20),
        cost_estimate=pl.CostEstimate(flops=heads * length * length * 512, bytes_accessed=12 * length * n, transcendentals=heads * length * length // 2),
        name="attend_forward",
    )(q, k, v, g, crow.reshape(steps, hp, length), scol, srow)

def bwd_kernel(q_ref, k_ref, v_ref, g_ref, o_ref, dz_ref, lse_ref, ccol_ref, scol_ref, srow_ref,
               dq_ref, dk_ref, dv_ref, dg_ref, dc_ref, dqacc):
    length, width = q_ref.shape
    hp = width // HEAD
    lane = lax.broadcasted_iota(jnp.int32, (1, width), 1) // HEAD
    tri = lax.broadcasted_iota(jnp.int32, (BLK, BLK), 1) >= lax.broadcasted_iota(jnp.int32, (BLK, BLK), 0)
    blocks = length // BLK
    sig = jax.nn.sigmoid(g_ref[...].astype(jnp.float32))
    dz = dz_ref[...].astype(jnp.float32)
    out = o_ref[...].astype(jnp.float32)
    dout = (dz * sig).astype(jnp.bfloat16)
    dg_ref[...] = (dz * out * sig * (1.0 - sig)).astype(jnp.bfloat16)
    prod = (dout.astype(jnp.float32) * out)
    prod_hi = prod.astype(jnp.bfloat16)
    prod_lo = (prod - prod_hi.astype(jnp.float32)).astype(jnp.bfloat16)
    dqs = [None] * blocks
    for h in range(hp):
        head = lane == h
        ones = jnp.broadcast_to(jnp.where(head, 1.0, 0.0).astype(jnp.bfloat16), (8, width))
        centre = (last(ones, prod_hi) + last(ones, prod_lo))[0:1, :]
        q_one = jnp.where(head, q_ref[...], 1.0)
        q_zero = jnp.where(head, q_ref[...], 0.0)
        k_one = jnp.where(head, k_ref[...], 1.0)
        d_zero = jnp.where(head, dout, 0.0)
        dqacc[...] = jnp.zeros_like(dqacc)
        for j in range(blocks):
            keys = pl.ds(j * BLK, BLK)
            lo = j * BLK
            s = last(k_ref[keys, :], q_zero[lo:, :])
            s = s - ccol_ref[0, keys, h:h + 1] - lse_ref[0, h:h + 1, lo:]
            same = scol_ref[keys, :] == srow_ref[:, lo:]
            if j < blocks - 1:
                allowed = jnp.concatenate([same[:, :BLK] & tri, same[:, BLK:]], axis=1)
            else:
                allowed = same & tri
            p = jnp.where(allowed, jnp.exp2(s), 0.0)
            dp = last(v_ref[keys, :], d_zero[lo:, :])
            ds = (p * (dp - centre[:, lo:])).astype(jnp.bfloat16)
            dv = mm(p.astype(jnp.bfloat16), dout[lo:, :])
            dk = mm(ds, q_one[lo:, :])
            dqacc[lo:, :] += first(ds, k_one[lo:lo + BLK, :])
            if h == 0:
                dk_ref[keys, :] = (dk * LN2).astype(jnp.bfloat16)
                dv_ref[keys, :] = dv.astype(jnp.bfloat16)
                dc_ref[0, keys, :] = -dk
            else:
                dk_ref[keys, :] = jnp.where(head, (dk * LN2).astype(jnp.bfloat16), dk_ref[keys, :])
                dv_ref[keys, :] = jnp.where(head, dv.astype(jnp.bfloat16), dv_ref[keys, :])
                dc_ref[0, keys, :] = jnp.where(lane == 0, -dk, dc_ref[0, keys, :]) if h == 1 else jnp.where(lane == h - 1, -dk, dc_ref[0, keys, :])
        dq = dqacc[...]
        if h == 0:
            dq_ref[...] = (dq * 0.125).astype(jnp.bfloat16)
            dc_ref[0] = dc_ref[0] + dq
        else:
            dq_ref[...] = jnp.where(head, (dq * 0.125).astype(jnp.bfloat16), dq_ref[...])
            dc_ref[0] = jnp.where(lane == h - 1, dc_ref[0] + dq, dc_ref[0])

def attend_backward(q, k, v, g, o, dz, lse, ccol, scol, srow):
    length, n = q.shape
    heads = n // HEAD
    hp = 2 if heads % 2 == 0 else heads
    steps = heads // hp
    width = hp * HEAD
    blk = pl.BlockSpec((length, width), lambda i: (0, i))
    low = jax.ShapeDtypeStruct((length, n), jnp.bfloat16)
    return pl.pallas_call(
        bwd_kernel,
        grid=(steps,),
        in_specs=[blk] * 6 + [pl.BlockSpec((1, hp, length), lambda i: (i, 0, 0)),
                  pl.BlockSpec((1, length, hp), lambda i: (i, 0, 0)),
                  pl.BlockSpec((length, 1), lambda i: (0, 0)), pl.BlockSpec((1, length), lambda i: (0, 0))],
        out_specs=[blk] * 4 + [pl.BlockSpec((1, length, width), lambda i: (i, 0, 0))],
        out_shape=[low] * 4 + [jax.ShapeDtypeStruct((steps, length, width), jnp.float32)],
        scratch_shapes=[pltpu.VMEM((length, width), jnp.float32)],
        compiler_params=pltpu.CompilerParams(vmem_limit_bytes=48 << 20),
        cost_estimate=pl.CostEstimate(flops=heads * length * length * 1280, bytes_accessed=24 * length * n, transcendentals=heads * length * length // 2),
        name="attend_backward",
    )(q, k, v, g, o, dz, lse, ccol.reshape(length, steps, hp).transpose(1, 0, 2), scol, srow)
eps = 1e-06


def normalize(values, scale_gain):
    inverse = lax.rsqrt(jnp.mean(values * values, axis=-1, keepdims=True) + eps)
    return values * inverse * scale_gain, inverse


def norm_back(values, inverse, scale_gain, upstream):
    unit_rows = values * inverse
    scaled = upstream * scale_gain
    return inverse * (scaled - unit_rows * jnp.mean(scaled * unit_rows, axis=-1, keepdims=True))


def log_keep(values):
    return jnp.minimum(values, 0.0) - jnp.log1p(jnp.exp(-jnp.abs(values)))


def low(values):
    return values.astype(jnp.bfloat16)


def bits_of(size):
    return [1 << b for b in range(size.bit_length() - 1)]


class Place:
    def __init__(self, rows):
        self.tensor = lax.axis_size("tensor")
        self.dp = lax.axis_size("dp")
        self.rows = rows
        self.group = self.tensor // rows
        self.at = lax.axis_index("tensor")
        self.dp_at = lax.axis_index("dp")
        self.row = self.at // self.group
        self.member = self.at % self.group

    def slot_owner(self, at, step, turn):
        row, member = at // self.group, at % self.group
        return ((row + turn) % self.rows) * self.group + (member + step) % self.group

    def from_slot(self, value, step, turn):
        pairs = [(self.slot_owner(i, step, turn), i) for i in range(self.tensor)]
        return lax.ppermute(value, "tensor", pairs)

    def to_slot(self, value, step, turn):
        pairs = [(i, self.slot_owner(i, step, turn)) for i in range(self.tensor)]
        return lax.ppermute(value, "tensor", pairs)

    def swap(self, value, bit):
        return lax.ppermute(value, "dp", [(i, i ^ bit) for i in range(self.dp)])

    def has(self, bit):
        return (self.dp_at // bit) % 2

    def piece(self, shard):
        count = shard.shape[0] // self.dp
        return lax.dynamic_slice_in_dim(shard, self.dp_at * count, count, 0)

    def gather(self, piece, flip):
        bits = bits_of(self.dp)
        order = bits[1:] if flip else bits[:0:-1]
        held = piece
        done = []
        for bit in order + bits[:1]:
            other = self.swap(held, bit)
            axis = sum(1 for b in done if b > bit)
            mine_high = self.has(bit) == 1
            first_half = jnp.where(mine_high, other, held)
            second_half = jnp.where(mine_high, held, other)
            held = jnp.stack([first_half, second_half], axis)
            done.append(bit)
        return held.reshape((-1, piece.shape[-1]))

    def scatter(self, partial, flip):
        bits = bits_of(self.dp)
        rows, width = partial.shape
        held = partial.reshape((2,) * len(bits) + (rows // self.dp, width))
        order = bits[:1] + (bits[1:] if flip else bits[:0:-1])
        left = bits[::-1]
        for bit in order:
            axis = left.index(bit)
            mine = self.has(bit)
            keep = lax.dynamic_index_in_dim(held, mine, axis, keepdims=False)
            send = lax.dynamic_index_in_dim(held, 1 - mine, axis, keepdims=False)
            got = self.swap(send, bit)
            held = low(keep.astype(jnp.float32) + got.astype(jnp.float32))
            left = [b for b in left if b != bit]
        return held

    def sum_all(self, value):
        for bit in bits_of(self.dp):
            value = value + self.swap(value, bit)
        for bit in bits_of(self.tensor):
            value = value + lax.ppermute(value, "tensor", [(i, i ^ bit) for i in range(self.tensor)])
        return value

    def shares(self, make):
        total = make(self.member)
        for step in range(1, self.group):
            theirs = low(make((self.member + step) % self.group))
            pairs = [(i, (i // self.group) * self.group + (i % self.group + step) % self.group) for i in range(self.tensor)]
            total = total + lax.ppermute(theirs, "tensor", pairs).astype(jnp.float32)
        return total


def on_device(
    inputs, gain_attn, w_query, w_key, w_value, w_outgate, w_forget, forget_bias, w_out,
    gain_mlp, w_gate, w_up, w_down, segment_ids, cotangent,
):
    rows, length = segment_ids.shape
    here = Place(rows)
    head_local = w_forget.shape[1]
    width = w_query.shape[1]
    hidden = w_gate.shape[1]
    model = inputs.shape[1]
    own_count = length // here.group
    slots = [(s, j) for s in range(here.group) for j in range(rows)]

    def own_row(array):
        return lax.dynamic_slice_in_dim(array, here.row * length, length, 0)

    def share(array, member):
        return lax.dynamic_slice_in_dim(array, member * own_count, own_count, 0)

    attn_own = jnp.concatenate([w_query, w_key, w_value, w_outgate, w_forget], axis=1)
    attn_piece = here.piece(attn_own)
    attn_w = [attn_own] + [here.gather(here.from_slot(attn_piece, 0, j), False) for j in range(1, rows)]
    bias = [forget_bias] + [here.from_slot(forget_bias, 0, j) for j in range(1, rows)]
    out_piece = here.piece(w_out)
    out_rest = here.gather(
        jnp.concatenate([here.from_slot(out_piece, s, j) for s, j in slots[1:]], axis=1), True
    )
    out_w = jnp.concatenate([w_out, out_rest], axis=1)
    gate_piece = here.piece(jnp.concatenate([w_gate, w_up], axis=1))
    down_piece = here.piece(w_down)
    gate_w, up_w, down_w = [w_gate], [w_up], [w_down]
    for j in range(1, rows):
        both = here.gather(here.from_slot(gate_piece, 0, j), False)
        gate_w.append(both[:, :hidden])
        up_w.append(both[:, hidden:])
        down_w.append(here.gather(here.from_slot(down_piece, 0, j), True))

    inputs_row = own_row(inputs).astype(jnp.float32)
    normed, inverse_attn = normalize(inputs_row, gain_attn)
    normed_low = low(normed)
    segment = lax.dynamic_index_in_dim(segment_ids, here.row, 0, keepdims=False)
    scol, srow = segment[:, None], segment[None, :]
    below = (
        lax.broadcasted_iota(jnp.int32, (length, length), 0)
        >= lax.broadcasted_iota(jnp.int32, (length, length), 1)
    ).astype(jnp.float32)
    kept = []
    gated = []
    for j in range(rows):
        mixed = mm(normed_low, attn_w[j])
        queries = low(mixed[:, :width] * (HEAD ** -0.5 * LOG2E))
        key_rows = low(mixed[:, width:2 * width])
        value_rows = low(mixed[:, 2 * width:3 * width])
        outgate = low(mixed[:, 3 * width:4 * width])
        forget = mixed[:, 4 * width:] + bias[j]
        running = jnp.dot(below, log_keep(forget) * LOG2E, precision=lax.Precision.HIGHEST)
        z, attended, log_total = attend_forward(
            queries, key_rows, value_rows, outgate, running.T, scol, srow
        )
        kept.append((queries, key_rows, value_rows, outgate, forget, running, attended, log_total))
        gated.append(z)
    gated_full = list(gated)
    for s in range(1, here.group):
        gated_full += [here.from_slot(z, s, 0) for z in gated]
    gated_full = jnp.concatenate(gated_full, axis=1)
    hidden_row = inputs_row + last(gated_full, out_w)

    mlp_normed, inverse_mlp = normalize(hidden_row, gain_mlp)
    mlp_low = low(mlp_normed)
    cotangent_row = own_row(cotangent)
    middle, grad_gate, grad_up = [], [], []
    for j in range(rows):
        gate_pre = mm(mlp_low, gate_w[j])
        up_pre = mm(mlp_low, up_w[j])
        grad_middle = mm(cotangent_row, down_w[j])
        sig = jax.nn.sigmoid(gate_pre)
        middle.append(low(gate_pre * sig * up_pre))
        grad_gate.append(low(grad_middle * up_pre * sig * (1.0 + gate_pre * (1.0 - sig))))
        grad_up.append(low(grad_middle * gate_pre * sig))

    def mlp_back(member):
        total = 0.0
        for j in range(rows):
            total = total + last(share(grad_gate[j], member), gate_w[j]) + last(share(grad_up[j], member), up_w[j])
        return total

    def mlp_out(member):
        return sum(last(share(middle[j], member), down_w[j]) for j in range(rows))

    hidden_own = share(hidden_row, here.member)
    inverse_own = share(inverse_mlp, here.member)
    mlp_grad = here.shares(mlp_back)
    dh_own = share(cotangent_row, here.member).astype(jnp.float32) + norm_back(
        hidden_own, inverse_own, gain_mlp, mlp_grad
    )
    gain_mlp_part = jnp.sum(mlp_grad * (hidden_own * inverse_own), axis=0)
    dh_low = low(dh_own)
    output = hidden_own + here.shares(mlp_out)

    def settle(parts, flip):
        total = 0.0
        for j, part in enumerate(parts):
            mine = here.scatter(low(part), flip)
            if j:
                mine = here.to_slot(mine, 0, j)
            total = total + mine.astype(jnp.float32)
        return total

    grad_down_w = settle([first(cotangent_row, m) for m in middle], True)
    grad_gate_w = settle([first(mlp_low, g) for g in grad_gate], False)
    grad_up_w = settle([first(mlp_low, g) for g in grad_up], True)

    block = rows * width
    dz_own = low(mm(dh_low, out_w))
    dz = jnp.zeros((length, block), jnp.bfloat16)
    dz = lax.dynamic_update_slice_in_dim(dz, dz_own[:, :block], here.member * own_count, 0)
    for s in range(1, here.group):
        back = here.group - s
        got = here.from_slot(dz_own[:, back * block:(back + 1) * block], s, 0)
        dz = lax.dynamic_update_slice_in_dim(dz, got, (here.member + s) % here.group * own_count, 0)
    out_part = here.scatter(low(first(dh_low, share(gated_full, here.member))), False)
    grad_out_w = 0.0
    for i, (s, j) in enumerate(slots):
        mine = out_part[:, i * width:(i + 1) * width]
        if i:
            mine = here.to_slot(mine, s, j)
        grad_out_w = grad_out_w + mine.astype(jnp.float32)

    mixed_back = [None] * rows
    attn_parts = [None] * rows
    bias_parts = [None] * rows
    for j in reversed(range(rows)):
        queries, key_rows, value_rows, outgate, forget, running, attended, log_total = kept[j]
        dq, dk, dv, dg, dc = attend_backward(
            queries, key_rows, value_rows, outgate, attended,
            dz[:, j * width:(j + 1) * width], log_total, running, scol, srow,
        )
        per_step = dc.shape[2] // HEAD
        columns = [dc[i, :, (HEAD if h == 0 else (h - 1) * HEAD)] for i in range(dc.shape[0]) for h in range(per_step)]
        rate_back = lax.dot_general(
            below, jnp.stack(columns, axis=1), (((0,), (0,)), ((), ())), precision=lax.Precision.HIGHEST
        )
        grad_forget = low(rate_back * jax.nn.sigmoid(-forget))
        bias_parts[j] = jnp.sum(grad_forget.astype(jnp.float32), axis=0)
        mixed_back[j] = jnp.concatenate([dq, dk, dv, dg, grad_forget], axis=1)
        attn_parts[j] = first(normed_low, mixed_back[j])

    def attn_back(member):
        return sum(last(share(mixed_back[j], member), attn_w[j]) for j in range(rows))

    attn_grad = here.shares(attn_back)
    inputs_own = share(inputs_row, here.member)
    inverse_own_attn = share(inverse_attn, here.member)
    grad_inputs = dh_own + norm_back(inputs_own, inverse_own_attn, gain_attn, attn_grad)
    gain_attn_part = jnp.sum(attn_grad * (inputs_own * inverse_own_attn), axis=0)
    grad_attn = settle(attn_parts, False)

    bias_full = jnp.zeros((here.tensor, head_local), jnp.float32)
    for j in range(rows):
        owner = here.slot_owner(here.at, 0, j)
        bias_full = lax.dynamic_update_slice(bias_full, bias_parts[j][None], (owner, 0))
    small = jnp.concatenate([gain_attn_part, gain_mlp_part, bias_full.reshape(-1)])[None]
    small = here.sum_all(small)[0]
    bias_own = lax.dynamic_slice_in_dim(small[2 * model:], here.at * head_local, head_local, 0)

    return (
        output,
        grad_inputs,
        small[:model],
        grad_attn[:, :width],
        grad_attn[:, width:2 * width],
        grad_attn[:, 2 * width:3 * width],
        grad_attn[:, 3 * width:4 * width],
        grad_attn[:, 4 * width:],
        bias_own,
        grad_out_w,
        small[model:2 * model],
        grad_gate_w,
        grad_up_w,
        grad_down_w,
    )


def solution(mesh):
    placed = (
        P("dp", None), P(), P(None, "tensor"), P(None, "tensor"), P(None, "tensor"),
        P(None, "tensor"), P(None, "tensor"), P("tensor"), P(None, "tensor"), P(),
        P(None, "tensor"), P(None, "tensor"), P(None, "tensor"), P("dp", None), P("dp", None),
    )
    weight = P("dp", "tensor")
    tokens = P(("dp", "tensor"), None)
    return jax.shard_map(
        on_device,
        mesh=mesh,
        in_specs=placed,
        out_specs=(
            tokens, tokens, P(), weight, weight, weight, weight, weight, P("tensor"),
            weight, P(), weight, weight, weight,
        ),
        check_vma=False,
    )
```

```python
import jax
import jax.numpy as jnp
from jax import lax
from jax.sharding import PartitionSpec as P
from jax.experimental import pallas as pl
from jax.experimental.pallas import tpu as pltpu

LOG2E = 1.4426950408889634
LN2 = 0.6931471805599453
HEAD = 64
BLK = 256
EPS = 1e-06
ROW, MEMBER, CORE, CHIP, PIECE = 0, 1, 2, 3, 4
f32 = jnp.float32
bf16 = jnp.bfloat16


def last(a, b):
    return lax.dot_general(a, b, (((1,), (1,)), ((), ())), preferred_element_type=f32)


def first(a, b):
    return lax.dot_general(a, b, (((0,), (0,)), ((), ())), preferred_element_type=f32)


def mm(a, b):
    return jnp.dot(a, b, preferred_element_type=f32)


def low(values):
    return values.astype(bf16)


def shape(dims, dtype):
    return jax.ShapeDtypeStruct(dims, dtype)


def run(name, body, where, grid, ins, outs, scratch=(), after=(), flops=0, vmem=56):
    count, extra, made = len(ins), len(after), len(outs)

    def kernel(where_ref, *refs):
        body(where_ref, refs[:count], refs[count + extra:count + extra + made], refs[count + extra + made:])

    return pl.pallas_call(
        kernel,
        grid_spec=pltpu.PrefetchScalarGridSpec(
            num_scalar_prefetch=1,
            grid=grid,
            in_specs=[pl.BlockSpec(b, m) for _, b, m in ins]
            + [pl.BlockSpec(memory_space=pl.ANY)] * extra,
            out_specs=[pl.BlockSpec(b, m) for _, b, m in outs],
            scratch_shapes=list(scratch),
        ),
        out_shape=[s for s, _, _ in outs],
        compiler_params=pltpu.CompilerParams(vmem_limit_bytes=vmem << 20),
        cost_estimate=pl.CostEstimate(flops=int(flops) + 10 ** 9, bytes_accessed=1, transcendentals=0),
        name=name,
    )(where, *[a for a, _, _ in ins], *after)


def fixed(array):
    return (array, array.shape, lambda i, w: (0,) * array.ndim)


def fixed_out(dims, dtype):
    return (shape(dims, dtype), dims, lambda i, w: (0,) * len(dims))


def halves(values, pieces, core):
    count = values.shape[1] // pieces
    even = jnp.concatenate([values[:, p * count:(p + 1) * count] for p in range(0, pieces, 2)], axis=1)
    odd = jnp.concatenate([values[:, p * count:(p + 1) * count] for p in range(1, pieces, 2)], axis=1)
    return jnp.where(core == 0, odd, even), jnp.where(core == 0, even, odd)


def three(values):
    top = low(values)
    rest = values - top.astype(f32)
    middle = low(rest)
    return top, middle, low(rest - middle.astype(f32))


def log_keep(values):
    return jnp.minimum(values, 0.0) - jnp.log1p(jnp.exp(-jnp.abs(values)))


def lower(flip=False):
    r = lax.broadcasted_iota(jnp.int32, (BLK, BLK), 0)
    c = lax.broadcasted_iota(jnp.int32, (BLK, BLK), 1)
    return jnp.where(r <= c if flip else r >= c, 1.0, 0.0).astype(bf16)


TOK = 512


def project_tail(i, mixed, width, bias, outs, carry):
    q_ref, k_ref, v_ref, g_ref, f_ref, ccol_ref, crow_ref = outs
    q_ref[...] = low(mixed[:, :width] * (HEAD ** -0.5 * LOG2E))
    for p, ref in ((1, k_ref), (2, v_ref), (3, g_ref)):
        ref[...] = low(mixed[:, p * width:(p + 1) * width])
    heads = f_ref.shape[1]
    forget = mixed[:, 4 * width:4 * width + heads] + bias
    f_ref[...] = forget

    @pl.when(i == 0)
    def _():
        carry[...] = jnp.zeros_like(carry)

    mask = lower()
    hp = crow_ref.shape[1]
    tokens = forget.shape[0]
    for t in range(tokens // BLK):
        rows = slice(t * BLK, (t + 1) * BLK)
        wide = jnp.concatenate([log_keep(forget[rows]) * LOG2E, jnp.zeros((BLK, 128 - heads), f32)], axis=1)
        sums = sum(mm(mask, part) for part in three(wide)) + carry[0:1, :]
        carry[0:1, :] = sums[BLK - 1:BLK, :]
        ccol_ref[rows, :] = sums[:, :heads]
        flat = sums.T
        for s in range(crow_ref.shape[0]):
            crow_ref[s, :, rows] = flat[s * hp:(s + 1) * hp, :]


def together(heads):
    return 2 if heads % 2 == 0 else heads


def project_outs(length, width, heads):
    tokens = lambda i, w: (i, 0)
    return [(shape((length, width), bf16), (TOK, width), tokens) for _ in range(4)] + [
        (shape((length, heads), f32), (TOK, heads), tokens),
        (shape((length, heads), f32), (TOK, heads), tokens),
        (shape((heads // together(heads), together(heads), length), f32),
         (heads // together(heads), together(heads), TOK), lambda i, w: (0, 0, i)),
    ]


def project_own(where, length, pieces, inputs, gain, weights, bias, after=()):
    model = inputs.shape[1]
    width, heads = weights[0].shape[1], weights[4].shape[1]
    half = model // 2

    def body(w, ins, outs, scratch):
        x_ref, gain_ref, wq, wk, wv, wg, wf, b_ref = ins
        a_ref, send_ref, keep_ref, inv_ref = outs[:4]
        x = x_ref[...].astype(f32)
        inverse = lax.rsqrt(jnp.mean(x * x, axis=1, keepdims=True) + EPS)
        a = low(x * inverse * gain_ref[...])
        a_ref[...] = a
        inv_ref[...] = inverse
        send_ref[...], keep_ref[...] = halves(a, pieces, w[CORE])
        mixed = mm(a, jnp.concatenate([r[...] for r in (wq, wk, wv, wg, wf)], axis=1))
        project_tail(pl.program_id(0), mixed, width, b_ref[...], outs[4:], scratch[0])

    blocks = length // TOK
    tokens = lambda i, w: (i, 0)
    return run(
        "project_own", body, where, (blocks,),
        [(inputs, (TOK, model), lambda i, w: (w[ROW] * blocks + i, 0)), fixed(gain)]
        + [fixed(a) for a in weights] + [fixed(bias)],
        [(shape((length, model), bf16), (TOK, model), tokens),
         (shape((length, half), bf16), (TOK, half), tokens), (shape((length, half), bf16), (TOK, half), tokens),
         (shape((length, 1), f32), (TOK, 1), tokens)]
        + project_outs(length, width, heads),
        [pltpu.VMEM((8, 128), f32)], after, 2 * length * model * (4 * width + heads),
    )


def core_halves(ref, w, half):
    return (ref[:, pl.ds(pl.multiple_of(w[CORE] * half, 128), half)],
            ref[:, pl.ds(pl.multiple_of((1 - w[CORE]) * half, 128), half)])


def project_other(where, normed, mine, theirs, width, heads, bias, after=()):
    length, model = normed.shape
    half = model // 2

    def body(w, ins, outs, scratch):
        a_ref, m_ref, t_ref, b_ref = ins
        am, at = core_halves(a_ref, w, half)
        mixed = mm(am, m_ref[...]) + mm(at, t_ref[...])
        project_tail(pl.program_id(0), mixed, width, b_ref[...], outs, scratch[0])

    return run(
        "project_other", body, where, (length // TOK,),
        [(normed, (TOK, model), lambda i, w: (i, 0)), fixed(mine), fixed(theirs), fixed(bias)],
        project_outs(length, width, heads),
        [pltpu.VMEM((8, 128), f32)], after, 2 * length * model * (4 * width + heads),
    )


def attend_forward(where, q, k, v, g, crow, scol, srow, after=()):
    length, n = q.shape
    heads = n // HEAD
    hp = together(heads)
    width = hp * HEAD

    def body(w, ins, outs, scratch):
        q_ref, k_ref, v_ref, g_ref, crow_ref, scol_ref, srow_ref = ins
        z_ref, lse_ref = outs
        lane = lax.broadcasted_iota(jnp.int32, (1, width), 1) // HEAD
        lane1 = lax.broadcasted_iota(jnp.int32, (BLK, 128), 1)
        tri = lax.broadcasted_iota(jnp.int32, (BLK, BLK), 0) >= lax.broadcasted_iota(jnp.int32, (BLK, BLK), 1)
        crows = crow_ref[0]
        for i in range(length // BLK):
            rows = pl.ds(i * BLK, BLK)
            reach = (i + 1) * BLK
            q = q_ref[rows, :]
            same = scol_ref[rows, :] == srow_ref[:, :reach]
            if i:
                allowed = jnp.concatenate([same[:, :reach - BLK], same[:, reach - BLK:] & tri], axis=1)
            else:
                allowed = same & tri
            out = jnp.zeros((BLK, width), f32)
            stats = jnp.zeros((BLK, 128), f32)
            for h in range(hp):
                s = last(jnp.where(lane == h, q, 0), k_ref[:reach, :])
                s = jnp.where(allowed, s - crows[h:h + 1, :reach], -1e30)
                top = jnp.max(s, axis=1, keepdims=True)
                e = jnp.exp2(s - top)
                total = jnp.sum(e, axis=1, keepdims=True)
                part = mm(low(e), v_ref[:reach, :])
                out = jnp.where(lane == h, part * (1.0 / total), out)
                stats = jnp.where(lane1 == h, top + jnp.log2(total), stats)
            z_ref[rows, :] = low(out * jax.nn.sigmoid(g_ref[rows, :].astype(f32)))
            lse_ref[0, :, i * BLK:(i + 1) * BLK] = stats.T[:hp, :]

    tokens = lambda i, w: (0, i)
    return run(
        "attend_forward", body, where, (heads // hp,),
        [(a, (length, width), tokens) for a in (q, k, v, g)]
        + [(crow, (1, hp, length), lambda i, w: (i, 0, 0)), fixed(scol), fixed(srow)],
        [(shape((length, n), bf16), (length, width), tokens),
         (shape((heads // hp, hp, length), f32), (1, hp, length), lambda i, w: (i, 0, 0))],
        (), after, heads * length * length * 1100,
    )


def attend_backward(where, q, k, v, g, z, dz_parts, lse, ccol, forget, scol, srow, after=()):
    length, n = q.shape
    heads = n // HEAD
    hp = together(heads)
    width = hp * HEAD
    steps = heads // hp
    group = len(dz_parts)
    share = length // group

    def body(w, ins, outs, scratch):
        q_ref, k_ref, v_ref, g_ref, z_ref = ins[:5]
        dz_refs = ins[5:5 + group]
        lse_ref, ccol_ref, f_ref, scol_ref, srow_ref = ins[5 + group:]
        dq_ref, dk_ref, dv_ref, dg_ref, df_ref, db_ref = outs
        dqacc, dkacc, rates, dzfull = scratch
        step = pl.program_id(0)
        lane = lax.broadcasted_iota(jnp.int32, (1, width), 1) // HEAD
        lane1 = lax.broadcasted_iota(jnp.int32, (1, 128), 1)
        tri = lax.broadcasted_iota(jnp.int32, (BLK, BLK), 1) >= lax.broadcasted_iota(jnp.int32, (BLK, BLK), 0)
        blocks = length // BLK

        @pl.when(step == 0)
        def _():
            rates[...] = jnp.zeros_like(rates)

        for s in range(group):
            at = lax.rem(w[MEMBER] + s, group) * share
            dzfull[pl.ds(pl.multiple_of(at, share), share), :] = dz_refs[s][...]
        sig = jax.nn.sigmoid(g_ref[...].astype(f32))
        dz = dzfull[...].astype(f32)
        prod = dz * z_ref[...].astype(f32)
        dout = low(dz * sig)
        dg_ref[...] = low(prod * (1.0 - sig))
        prod_hi = low(prod)
        prod_lo = low(prod - prod_hi.astype(f32))
        lses = lse_ref[0]
        for h in range(hp):
            head = lane == h
            index = step * hp + h
            decay = jnp.sum(jnp.where(lane1[:, :heads] == index, ccol_ref[...], 0.0), axis=1, keepdims=True)
            ones = jnp.broadcast_to(jnp.where(head, 1.0, 0.0).astype(bf16), (8, width))
            centre = (last(ones, prod_hi) + last(ones, prod_lo))[0:1, :]
            q_one = jnp.where(head, q_ref[...], 1.0)
            q_zero = jnp.where(head, q_ref[...], 0.0)
            k_one = jnp.where(head, k_ref[...], 1.0)
            d_zero = jnp.where(head, dout, 0.0)
            dqacc[...] = jnp.zeros_like(dqacc)
            for j in range(blocks):
                keys = pl.ds(j * BLK, BLK)
                lo = j * BLK
                s = last(k_ref[keys, :], q_zero[lo:, :])
                s = s - decay[lo:lo + BLK, :] - lses[h:h + 1, lo:]
                same = scol_ref[keys, :] == srow_ref[:, lo:]
                if j < blocks - 1:
                    allowed = jnp.concatenate([same[:, :BLK] & tri, same[:, BLK:]], axis=1)
                else:
                    allowed = same & tri
                p = jnp.exp2(jnp.where(allowed, s, -1e30))
                dp = last(v_ref[keys, :], d_zero[lo:, :])
                ds = low(p * (dp - centre[:, lo:]))
                dv = mm(low(p), dout[lo:, :])
                dk = mm(ds, q_one[lo:, :])
                dqacc[lo:, :] += first(ds, k_one[lo:lo + BLK, :])
                dkacc[keys, :] = dk
                if h == 0:
                    dk_ref[keys, :] = low(dk * LN2)
                    dv_ref[keys, :] = low(dv)
                else:
                    dk_ref[keys, :] = jnp.where(head, low(dk * LN2), dk_ref[keys, :])
                    dv_ref[keys, :] = jnp.where(head, low(dv), dv_ref[keys, :])
            dq = dqacc[...]
            if h == 0:
                dq_ref[...] = low(dq * HEAD ** -0.5)
            else:
                dq_ref[...] = jnp.where(head, low(dq * HEAD ** -0.5), dq_ref[...])
            spare = HEAD if h == 0 else 0
            rate = (dq - dkacc[...])[:, spare:spare + 1]
            rates[...] = jnp.where(lane1 == index, rate, rates[...])

        @pl.when(step == steps - 1)
        def _():
            mask = lower(True)
            carry = jnp.zeros((1, 128), f32)
            bias = jnp.zeros((1, heads), f32)
            for b in reversed(range(blocks)):
                rows = pl.ds(b * BLK, BLK)
                sums = sum(mm(mask, part) for part in three(rates[rows, :])) + carry
                carry = sums[0:1, :]
                df = low(sums[:, :heads] * jax.nn.sigmoid(-f_ref[rows, :]))
                df_ref[rows, :] = df
                bias = bias + jnp.sum(df.astype(f32), axis=0, keepdims=True)
            db_ref[...] = bias

    tokens = lambda i, w: (0, i)
    wide = (shape((length, n), bf16), (length, width), tokens)
    return run(
        "attend_backward", body, where, (steps,),
        [(a, (length, width), tokens) for a in (q, k, v, g, z)]
        + [(a, (share, width), lambda i, w, off=off: (0, off + i)) for a, off in dz_parts]
        + [(lse, (1, hp, length), lambda i, w: (i, 0, 0))] + [fixed(a) for a in (ccol, forget, scol, srow)],
        [wide] * 4 + [fixed_out((length, heads), bf16), fixed_out((1, heads), f32)],
        [pltpu.VMEM((length, width), f32), pltpu.VMEM((length, width), f32), pltpu.VMEM((length, 128), f32),
         pltpu.VMEM((length, width), bf16)],
        after, heads * length * length * 1500,
    )


def close_attention(where, length, pieces, inputs, gated, out_own, out_mine, out_theirs, gain, after=()):
    model = inputs.shape[1]
    half = model // 2
    width = out_own.shape[1]

    def body(w, ins, outs, scratch):
        x_ref, own_ref, m_ref, t_ref, gain_ref = ins[:5]
        z = jnp.concatenate([r[...] for r in ins[5:]], axis=1)
        h_ref, a_ref, send_ref, keep_ref, inv_ref = outs
        for ref, core in ((m_ref, w[CORE]), (t_ref, 1 - w[CORE])):
            at = pl.ds(pl.multiple_of(core * half, 128), half)
            own = own_ref[pl.ds(pl.multiple_of(core * half, 128), half), :]
            rest = ref[:, :(len(gated) - 1) * width]
            h_ref[:, at] = x_ref[:, at].astype(f32) + last(z, jnp.concatenate([own, rest], axis=1))
        h = h_ref[...]
        inverse = lax.rsqrt(jnp.mean(h * h, axis=1, keepdims=True) + EPS)
        a = low(h * inverse * gain_ref[...])
        a_ref[...] = a
        inv_ref[...] = inverse
        send_ref[...], keep_ref[...] = halves(a, pieces, w[CORE])

    blocks = length // TOK
    tokens = lambda i, w: (i, 0)
    side = (shape((length, half), bf16), (TOK, half), tokens)
    return run(
        "close_attention", body, where, (blocks,),
        [(inputs, (TOK, model), lambda i, w: (w[ROW] * blocks + i, 0))]
        + [fixed(a) for a in (out_own, out_mine, out_theirs, gain)]
        + [(z, (TOK, width), tokens) for z in gated],
        [(shape((length, model), f32), (TOK, model), tokens), (shape((length, model), bf16), (TOK, model), tokens),
         side, side, (shape((length, 1), f32), (TOK, 1), tokens)],
        (), after, 2 * length * model * width * len(gated),
    )


def split_rows(where, length, pieces, array, after=()):
    model = array.shape[1]
    half = model // 2
    blocks = length // BLK

    def body(w, ins, outs, scratch):
        outs[0][...], outs[1][...] = halves(ins[0][...], pieces, w[CORE])

    side = (shape((length, half), bf16), (BLK, half), lambda i, w: (i, 0))
    return run(
        "split_rows", body, where, (blocks,),
        [(array, (BLK, model), lambda i, w: (w[ROW] * blocks + i, 0))], [side, side], (), after,
    )


def feed_forward(where, normed, cotangent, weights, hidden, after=()):
    length, model = normed.shape
    half = model // 2
    wide = BLK if hidden % BLK == 0 else hidden
    steps = hidden // wide
    own = len(weights) == 3

    def body(w, ins, outs, scratch):
        a_ref, e_ref = ins[:2]
        m_ref, du_ref, dw_ref = outs
        if not own:
            core = pl.ds(pl.multiple_of(w[CORE] * half, 128), half)
            other = pl.ds(pl.multiple_of((1 - w[CORE]) * half, 128), half)
        for t in range(length // TOK):
            rows = pl.ds(t * TOK, TOK)
            if own:
                gate, up = mm(a_ref[rows, :], ins[2][...]), mm(a_ref[rows, :], ins[3][...])
                dm = mm(e_ref[rows, :], ins[4][...])
            else:
                both = lambda ref, p: mm(ref[rows, core], ins[2 + p][...]) + mm(ref[rows, other], ins[5 + p][...])
                gate, up, dm = both(a_ref, 0), both(a_ref, 1), both(e_ref, 2)
            sig = jax.nn.sigmoid(gate)
            act = gate * sig
            m_ref[rows, :] = low(act * up)
            dw_ref[rows, :] = low(dm * act)
            du_ref[rows, :] = low(dm * up * (sig * (1.0 + gate * (1.0 - sig))))

    if own:
        parts = [(a, (model, wide), lambda i, w: (0, i)) for a in weights]
    else:
        gm, gt, dm, dt = weights
        parts = [
            (a, (half, wide), lambda i, w, p=p: (0, p * steps + i))
            for a, p in ((gm, 0), (gm, 1), (dm, 0), (gt, 0), (gt, 1), (dt, 0))
        ]
    result = (shape((length, hidden), bf16), (length, wide), lambda i, w: (0, i))
    return run(
        "feed_forward", body, where, (steps,),
        [fixed(normed), (cotangent, (length, model), lambda i, w: (w[ROW], 0))] + parts,
        [result] * 3, (), after, 6 * length * model * hidden,
    )


def weight_grads(name, where, sides, groups, rows_of=False, after=()):
    length, half = sides[0][0].shape
    widths = [sum(r.shape[1] for r in rights) for _, rights in groups]
    padded = [-(-n // 256) * 256 for n in widths]
    several = len(groups) > 1
    tall = half if several else half // 2
    count = 2 * len(sides)

    def body(w, ins, outs, scratch):
        at = count
        for k, (s, rights) in enumerate(groups):
            for which in (0, 1):
                @pl.when((pl.program_id(0) == (k if several else which)) & (pl.program_id(1) == which)
                         if several else pl.program_id(0) == which)
                def _(k=k, s=s, at=at, n=len(rights), which=which):
                    right = [ins[at + c][...] for c in range(n)]
                    value = first(ins[2 * s + which][...], right[0] if n == 1 else jnp.concatenate(right, axis=1))
                    outs[which][:, :widths[k]] = low(value)
                    if widths[k] < padded[k]:
                        outs[which][:, widths[k]:] = jnp.zeros((tall, padded[k] - widths[k]), bf16)
            at += len(rights)

    pick = (lambda i, c, w: (w[MEMBER], 0)) if rows_of else (lambda i, c, w: (0, 0))
    if several:
        grid = (len(groups), 2)
        left_at = [lambda i, c, w: (0, 0)] * 2
        out_at = [lambda i, c, w: (0, i)] * 2
    else:
        grid = (2, 2)
        left_at = [lambda i, c, w: (0, jnp.where(i == 0, c, 1)), lambda i, c, w: (0, jnp.where(i == 0, 0, c))]
        out_at = [lambda i, c, w: (jnp.where(i == 0, c, 1), 0), lambda i, c, w: (jnp.where(i == 0, 0, c), 0)]
    return run(
        name, body, where, grid,
        [(a, (length, tall), left_at[which]) for pair in sides for which, a in enumerate(pair)]
        + [(r, (length, r.shape[1]), pick) for _, rights in groups for r in rights],
        [(shape((half, sum(padded)), bf16), (tall, padded[0]), out_at[which]) for which in (0, 1)],
        (), after, 4 * half * length * sum(padded),
    )


def fold(where, entries, after=()):
    keep, _, bits, _, _, width = entries[0]
    rows = keep.shape[0]
    count = len(bits)
    pieces = 1 << count
    piece = rows // pieces
    wide = next(n for n in (768, 512, 384, width) if width % n == 0)
    across = width // wide
    block = (piece, wide)
    ins, outs = [], []
    for keep, got, bits, bit_at, col, _ in entries:
        place = count - 1 - bits.index(bit_at)

        def index(mine, place=place, bit_at=bit_at, col=col):
            def at(i, c, w):
                own = lax.rem(w[CHIP] // (bit_at >> 1), 2)
                bit = own if mine else 1 - own
                low_part = lax.rem(i, 1 << place)
                high = i // (1 << place)
                return ((high * 2 + bit) * (1 << place) + low_part, col * across + c)
            return at

        for mine in (False, True):
            ins += [(keep, block, index(mine)), (got, block, index(mine))]
            outs.append((shape((rows // 2, width), bf16), block, lambda i, c, w: (i, c)))

    def body(w, ins_, outs_, scratch):
        for k, out in enumerate(outs_):
            out[...] = low(ins_[2 * k][...].astype(f32) + ins_[2 * k + 1][...].astype(f32))

    return run("fold", body, where, (pieces // 2, across), ins, outs, (), after, 10 ** 9)


def assemble(where, pieces, masks, after=()):
    count, extra = len(pieces), len(after)
    rows, width = pieces[0].shape

    def kernel(w, *refs):
        out, sems = refs[count + extra], refs[count + extra + 1]
        copies = []
        for k in range(count):
            at = pl.multiple_of(jnp.bitwise_xor(w[CHIP], masks[k]) * rows, rows)
            copies.append(pltpu.make_async_copy(refs[k], out.at[pl.ds(at, rows), :], sems.at[k]))
        for c in copies:
            c.start()
        for c in copies:
            c.wait()

    return pl.pallas_call(
        kernel,
        grid_spec=pltpu.PrefetchScalarGridSpec(
            num_scalar_prefetch=1, grid=(),
            in_specs=[pl.BlockSpec(memory_space=pl.ANY)] * (count + extra),
            out_specs=pl.BlockSpec(memory_space=pl.ANY),
            scratch_shapes=[pltpu.SemaphoreType.DMA((count,))],
        ),
        out_shape=shape((count * rows, width), bf16),
        compiler_params=pltpu.CompilerParams(vmem_limit_bytes=4 << 20),
        cost_estimate=pl.CostEstimate(flops=10 ** 9, bytes_accessed=1, transcendentals=0),
        name="assemble",
    )(where, *pieces, *after)


def back_rows(name, where, steps, group, share, own_terms, pair_terms, model, dtypes, adds=(), unit=None, after=()):
    half = model // 2
    count = len(steps)
    turn = lambda m: sum(jnp.where(m == k, s, 0) for k, s in enumerate(steps))
    member = lambda m, w: lax.rem(w[MEMBER] + turn(m), group)
    side = lambda i, w: lax.rem(w[CORE] + i, 2)
    ins = []

    def put(array, block, at):
        ins.append((array, block, at))
        return len(ins) - 1

    rows_at = lambda i, m, w: (member(m, w), 0)
    own_plan = [
        ([put(x, (share, x.shape[1]), rows_at) for x in xs],
         [put(a, (half, a.shape[1]), lambda i, m, w: (side(i, w), 0)) for a in weights])
        for xs, weights in own_terms
    ]
    known = {}
    pair_plan = []
    for xs, mine, theirs, lo in pair_terms:
        for a in (mine, theirs):
            if id(a) not in known:
                known[id(a)] = put(a, a.shape, lambda i, m, w: (0, 0))
        pair_plan.append(([put(x, (share, x.shape[1]), rows_at) for x in xs],
                          known[id(mine)], known[id(theirs)], lo, sum(x.shape[1] for x in xs)))
    first_add = len(ins)
    for a, kind in adds:
        ins.append((a, (share, half), (lambda i, m, w: (w[MEMBER], side(i, w))) if kind == "row"
                    else (lambda i, m, w: (0, side(i, w)))))
    if unit is not None:
        values, base, inverse = unit
        ins.append((values, (share, half), lambda i, m, w: (w[ROW] * base + member(m, w), side(i, w))))
        ins.append((inverse, (share, 1), rows_at))

    def body(w, ins_, outs, scratch):
        wide = lambda refs: ins_[refs[0]][...] if len(refs) == 1 else jnp.concatenate([ins_[r][...] for r in refs], axis=1)
        at = pl.program_id(1)
        total = 0.0
        for xs, weights in own_plan:
            total = total + last(wide(xs), wide(weights))
        scratch[0][...] = total
        for which in (0, 1):
            @pl.when(pl.program_id(0) == which)
            def _():
                part = 0.0
                for xs, mine, theirs, lo, n in pair_plan:
                    part = part + last(wide(xs), ins_[(mine, theirs)[which]][:, lo:lo + n])
                scratch[0][...] += part
        if unit is not None:
            u = ins_[-2][...].astype(f32) * ins_[-1][...]
            gained = jnp.sum(scratch[0][...] * u, axis=0, keepdims=True)
            outs[count][...] = jnp.where(at == 0, 0.0, outs[count][...]) + gained
        for k in range(count):
            @pl.when(at == k)
            def _():
                total = scratch[0][...]
                if k == count - 1:
                    for a in range(len(adds)):
                        total = total + ins_[first_add + a][...].astype(f32)
                outs[k][...] = total.astype(dtypes[k])

    outs = [(shape((share, model), d), (share, half), lambda i, m, w: (0, side(i, w))) for d in dtypes]
    if unit is not None:
        outs.append((shape((1, model), f32), (1, half), lambda i, m, w: (0, side(i, w))))
    flops = 2 * share * model * count * sum(x.shape[1] for t in tuple(own_terms) + tuple(pair_terms) for x in t[0])
    return run(name, body, where, (2, count), ins, outs, [pltpu.VMEM((share, half), f32)], after, flops)


def close_feed_forward(where, share, group, pieces, part, got, hidden_row, inverse, gain, cotangent,
                       out_own, out_mine, out_theirs, after=()):
    model = part.shape[1]
    half = model // 2
    width = out_own.shape[1]
    filled = width + out_mine.shape[1]
    own_slots = filled // group

    def body(w, ins, outs, scratch):
        p_ref, h_ref, i_ref, gain_ref, e_ref, own_ref, m_ref, t_ref = ins[:8]
        dh_ref, send_ref, keep_ref, mine_out, peer_out = outs
        total = p_ref[...]
        for r in ins[8:]:
            total = total + r[...].astype(f32)
        unit = h_ref[...] * i_ref[...]
        scaled = total * gain_ref[...]
        dh = e_ref[...].astype(f32) + i_ref[...] * (scaled - unit * jnp.mean(scaled * unit, axis=1, keepdims=True))
        dh_ref[...] = dh
        d = low(dh)
        send_ref[...], keep_ref[...] = halves(d, pieces, w[CORE])
        scratch[0][...] = d
        dz = 0.0
        for d_half, ref, core in zip(core_halves(scratch[0], w, half), (m_ref, t_ref), (w[CORE], 1 - w[CORE])):
            own = own_ref[pl.ds(pl.multiple_of(core * half, 128), half), :]
            dz = dz + mm(d_half, jnp.concatenate([own, ref[...]], axis=1))
        mine_out[...] = low(dz[:, :own_slots])
        peer_out[...] = low(dz[:, own_slots:])

    whole = lambda i, w: (0, 0)
    mine = lambda i, w: (w[MEMBER], 0)
    side = (shape((share, half), bf16), (share, half), whole)
    return run(
        "close_feed_forward", body, where, (1,),
        [fixed(part), (hidden_row, (share, model), mine), (inverse, (share, 1), mine), fixed(gain),
         (cotangent, (share, model), lambda i, w: (w[ROW] * group + w[MEMBER], 0)),
         fixed(out_own), fixed(out_mine), fixed(out_theirs)] + [fixed(a) for a in got],
        [(shape((share, model), f32), (share, model), whole), side, side,
         (shape((share, own_slots), bf16), (share, own_slots), whole),
         (shape((share, filled - own_slots), bf16), (share, filled - own_slots), whole)],
        [pltpu.VMEM((share, model), bf16)], after, 2 * share * model * filled,
    )


def close_block(where, share, group, part, got, inputs, inverse, gain, dh, after=()):
    model = part.shape[1]
    step_rows = min(BLK, share)
    blocks = share // step_rows
    row_blocks = group * blocks

    def body(w, ins, outs, scratch):
        p_ref, x_ref, i_ref, gain_ref, dh_ref = ins[:5]
        total = p_ref[...]
        for r in ins[5:]:
            total = total + r[...].astype(f32)
        unit = x_ref[...].astype(f32) * i_ref[...]
        scaled = total * gain_ref[...]
        outs[0][...] = dh_ref[...] + i_ref[...] * (scaled - unit * jnp.mean(scaled * unit, axis=1, keepdims=True))

    tokens = lambda i, w: (i, 0)
    return run(
        "close_block", body, where, (blocks,),
        [(part, (step_rows, model), tokens),
         (inputs, (step_rows, model), lambda i, w: (w[ROW] * row_blocks + w[MEMBER] * blocks + i, 0)),
         (inverse, (step_rows, 1), lambda i, w: (w[MEMBER] * blocks + i, 0)), fixed(gain),
         (dh, (step_rows, model), tokens)] + [(a, (step_rows, model), tokens) for a in got],
        [(shape((share, model), f32), (step_rows, model), tokens)], (), after,
    )[0]


def collect(where, arrays, pieces, unit=1, after=()):
    count = arrays[0].shape[0] // pieces
    filled = sum(a.shape[1] for a in arrays)
    total = -(-filled // unit) * unit

    def body(w, ins, outs, scratch):
        at = 0
        for r in ins:
            n = r.shape[1]
            outs[0][:, at:at + n] = r[...]
            at += n
        if at < total:
            outs[0][:, at:] = jnp.zeros((count, total - at), bf16)

    return run(
        "collect", body, where, (1,),
        [(a, (count, a.shape[1]), lambda i, w: (w[PIECE], 0)) for a in arrays],
        [(shape((count, total), bf16), (count, total), lambda i, w: (0, 0))], (), after,
    )[0]


class Place:
    def __init__(self, rows):
        self.tensor = lax.axis_size("tensor")
        self.dp = lax.axis_size("dp")
        self.rows = rows
        self.group = self.tensor // rows
        self.at = lax.axis_index("tensor")
        self.dp_at = lax.axis_index("dp")
        self.bits = [1 << b for b in reversed(range(1, self.dp.bit_length() - 1))]

    def owner(self, at, step, turn):
        row, member = at // self.group, at % self.group
        return ((row + turn) % self.rows) * self.group + (member + step) % self.group

    def fetch(self, value, step, turn):
        pairs = [(self.owner(i, step, turn), i) for i in range(self.tensor)]
        return lax.ppermute(value, "tensor", pairs)

    def deliver(self, value, step, turn):
        pairs = [(i, self.owner(i, step, turn)) for i in range(self.tensor)]
        return lax.ppermute(value, "tensor", pairs)

    def swap(self, value, bit):
        return lax.ppermute(value, "dp", [(i, i ^ bit) for i in range(self.dp)])

    def sum_rest(self, value):
        for bit in self.bits[1:]:
            value = value + self.swap(value, bit)
        for bit in [1 << b for b in range(self.tensor.bit_length() - 1)]:
            value = value + lax.ppermute(value, "tensor", [(i, i ^ bit) for i in range(self.tensor)])
        return value


class Chain:
    def __init__(self, where):
        self.where = where
        self.behind = ()

    def __call__(self, make, *args, extra=(), **keys):
        made = make(self.where, *args, after=self.behind + tuple(extra), **keys)
        outs = made if isinstance(made, (list, tuple)) else [made]
        self.behind = (min(outs, key=lambda a: a.size),)
        return made

    def sync(self, *values):
        out = lax.optimization_barrier((*values, *self.behind))
        self.behind = tuple(out[len(values):])
        return out[:len(values)]


def on_device(
    inputs, gain_attn, w_query, w_key, w_value, w_outgate, w_forget, forget_bias, w_out,
    gain_mlp, w_gate, w_up, w_down, segment_ids, cotangent,
):
    rows, length = segment_ids.shape
    here = Place(rows)
    group, pieces = here.group, here.dp
    heads, width, hidden = w_forget.shape[1], w_query.shape[1], w_gate.shape[1]
    model = inputs.shape[1]
    share = length // group
    row, member = here.at // group, here.at % group
    core, chip = here.dp_at % 2, here.dp_at // 2
    where = jnp.stack([row, member, core, chip, core * (pieces // 2) + chip]).astype(jnp.int32)
    go = Chain(where)
    gain_attn, gain_mlp = gain_attn[None], gain_mlp[None]
    segment = lax.dynamic_index_in_dim(segment_ids, row, 0, keepdims=False)
    scol, srow = segment[:, None], segment[None, :]
    turns = range(1, rows)
    slots = [(s, j) for s in range(group) for j in range(rows)]

    def to_member(value, step):
        return lax.ppermute(value, "tensor", [
            (i, (i // group) * group + (i % group + step) % group) for i in range(here.tensor)])

    class Gather:
        def __init__(self, piece, flip):
            self.held, self.masks = [piece], [0]
            self.left = here.bits[::-1] if flip else list(here.bits)
            self.sent = {}
            self.send()

        def send(self):
            for bit in self.left:
                for i, p in enumerate(self.held):
                    if (bit, i) not in self.sent:
                        self.sent[bit, i] = here.swap(p, bit)

        def hop(self):
            bit = self.left.pop(0)
            got = go.sync(*[self.sent[bit, i] for i in range(len(self.held))])
            self.masks = self.masks + [k ^ (bit >> 1) for k in self.masks]
            self.held = self.held + list(got)
            self.send()

        def close(self):
            while self.left:
                self.hop()
            self.mine = go(assemble, self.held, self.masks)
            self.theirs = here.swap(self.mine, 1)
            return self.mine, self.theirs

    class Reduce:
        def __init__(self, send, keep, orders):
            self.parts = None
            self.keep, self.got, self.orders = keep, here.swap(send, 1), orders

        def hop(self):
            if self.parts is None:
                n = self.keep.shape[1]
                split = len(self.orders) if n % (128 * len(self.orders)) == 0 else 1
                entries = [(self.keep, self.got, list(here.bits), self.orders[c][0], c, n // split) for c in range(split)]
                orders = [order[1:] for order in self.orders[:split]]
            else:
                entries = [(kept, got, left, order[0], 0, kept.shape[1]) for kept, got, left, order in self.parts]
                orders = [order[1:] for _, _, _, order in self.parts]
            outs = go(fold, entries)
            self.parts = [
                [outs[2 * c + 1], here.swap(outs[2 * c], e[3]), [b for b in e[2] if b != e[3]], orders[c]]
                for c, e in enumerate(entries)
            ]

        def close(self):
            while self.parts is None or self.parts[0][3]:
                self.hop()
            sums = [kept.astype(f32) + got.astype(f32) for kept, got, _, _ in self.parts]
            return sums[0] if len(sums) == 1 else jnp.concatenate(sums, axis=1)

        def wait(self):
            got = go.sync(*([self.got] if self.parts is None else [p[1] for p in self.parts]))
            if self.parts is None:
                self.got = got[0]
            else:
                for p, g in zip(self.parts, got):
                    p[1] = g

    both_ways = [here.bits, here.bits[::-1]]

    attn_piece = go(collect, [w_query, w_key, w_value, w_outgate, w_forget], pieces, 256)
    attn_got = [here.fetch(attn_piece, 0, j) for j in turns]
    bias_got = [here.fetch(forget_bias, 0, j) for j in turns]
    own = go(project_own, length, pieces, inputs, gain_attn,
             [w_query, w_key, w_value, w_outgate, w_forget], forget_bias[None])
    normed, norm_send, norm_keep, inverse_attn = own[:4]
    mixed = {0: own[4:]}
    gated = {}
    logs = {}

    def attend(j):
        q, k, v, g, _, _, crow = mixed[j]
        z, logs[j] = go(attend_forward, q, k, v, g, crow, scol, srow)
        gated[0, j] = z
        for s in range(1, group):
            gated[s, j] = here.fetch(z, s, 0)

    attend(0)
    arrived = go.sync(*attn_got, *bias_got)
    attn_got, bias_got = arrived[:rows - 1], arrived[rows - 1:]
    attn_gather = [Gather(p, False) for p in attn_got]
    out_piece = go(collect, [w_out], pieces)
    out_got = [here.fetch(out_piece, 0, j) for j in turns]
    gate_piece = go(collect, [w_gate, w_up], pieces)
    gate_got = [here.fetch(gate_piece, 0, j) for j in turns]
    cot_sides = go(split_rows, length, pieces, cotangent)
    for gather in attn_gather:
        gather.hop()
    out_got = go.sync(*out_got)
    out_own = jnp.concatenate([out_piece, *out_got], axis=1)
    out_peers = [here.fetch(out_own, s, 0) for s in range(1, group)]
    attn_w = [gather.close() for gather in attn_gather]
    out_peers = go.sync(*out_peers)
    out_gather = Gather(jnp.concatenate([*out_got, *out_peers], axis=1), True)
    for j in turns:
        mixed[j] = go(project_other, normed, *attn_w[j - 1], width, heads, bias_got[j - 1][None])
    down_piece = go(collect, [w_down], pieces)
    gate_got = go.sync(*gate_got)
    gate_gather = [Gather(p, False) for p in gate_got]
    for j in turns:
        attend(j)
    down_got = [here.fetch(down_piece, 0, j) for j in turns]
    out_gather.hop()
    for gather in gate_gather:
        gather.hop()
    out_mine, out_theirs = out_gather.close()
    gate_w = [gather.close() for gather in gate_gather]
    hidden_row, mlp_normed, mlp_send, mlp_keep, inverse_mlp = go(
        close_attention, length, pieces, inputs, [gated[slot] for slot in slots], w_out, out_mine, out_theirs, gain_mlp
    )
    down_got = go.sync(*down_got)
    down_gather = [Gather(p, True) for p in down_got]

    ffn = {0: go(feed_forward, mlp_normed, cotangent, [w_gate, w_up, w_down], hidden)}
    for gather in down_gather:
        gather.hop()

    def mlp_grads(j):
        m, du, dw = ffn[j]
        sides = [(mlp_send, mlp_keep), cot_sides]
        send, keep = go(lambda w, after: weight_grads(
            "mlp_grads", w, sides, [(0, [du]), (0, [dw]), (1, [m])], after=after))
        return Reduce(send, keep, both_ways)

    mlp_sums = {0: mlp_grads(0)}
    mlp_w = {}
    for j in turns:
        mlp_w[j] = gate_w[j - 1] + down_gather[j - 1].close()
        gm, gt, dm, dt = mlp_w[j]
        ffn[j] = go(feed_forward, mlp_normed, cotangent, [gm, gt, dm, dt], hidden)
    peers = list(range(1, group))
    own_terms = [([ffn[0][1]], [w_gate]), ([ffn[0][2]], [w_up])]
    pair_terms = [([ffn[j][1], ffn[j][2]], *mlp_w[j][:2], 0) for j in turns]
    made = go(lambda w, after: back_rows(
        "mlp_back", w, peers + [0], group, share, own_terms, pair_terms, model, [bf16] * len(peers) + [f32],
        (), (hidden_row, 0, inverse_mlp), after))
    part, gain_mlp_part = made[-2:]
    got = [to_member(v, s) for v, s in zip(made, peers)]
    mlp_sums[0].hop()
    for j in turns:
        mlp_sums[j] = mlp_grads(j)
    mlp_sums[0].hop()
    for j in turns:
        mlp_sums[j].hop()
    dh, dh_send, dh_keep, dz_mine, dz_peers = go(
        close_feed_forward, share, group, pieces, part, got, hidden_row, inverse_mlp, gain_mlp, cotangent,
        w_out, out_mine, out_theirs,
    )
    dz_parts = [dz_mine]
    own_slots = rows * width
    for s in peers:
        lo = (group - s - 1) * own_slots
        dz_parts.append(here.fetch(dz_peers if group == 2 else dz_peers[:, lo:lo + own_slots], s, 0))

    def mlp_out(steps, dtypes, adds):
        own_terms = [([ffn[0][0]], [w_down])]
        pair_terms = [([ffn[j][0]], *mlp_w[j][2:], 0) for j in turns]
        return go(lambda w, after: back_rows(
            "mlp_out", w, steps, group, share, own_terms, pair_terms, model, dtypes, adds, None, after))

    out_send = mlp_out(peers, [bf16] * len(peers), ())
    out_sum = Reduce(*go(lambda w, after: weight_grads(
        "out_grads", w, [(dh_send, dh_keep)], [(0, [gated[slot] for slot in slots])], True, after)), both_ways)
    for j in turns:
        mlp_sums[j].hop()
    mlp_own = mlp_sums[0].close()

    back = {}
    attn_sums = {}
    per_step = together(heads) * HEAD

    def attend_back(j):
        q, k, v, g, forget, ccol, _ = mixed[j]
        parts = [(d, j * width // per_step) for d in dz_parts]
        if width % 128:
            parts = [(a[:, o * per_step:(o + 1) * per_step], 0) for a, o in parts]
        back[j] = go(attend_backward, q, k, v, g, gated[0, j], parts, logs[j], ccol, forget, scol, srow)

    def attn_grads(j):
        attn_sums[j] = Reduce(*go(lambda w, after: weight_grads(
            "attn_grads", w, [(norm_send, norm_keep)], [(0, back[j][:5])], False, after)), both_ways)

    dz_parts[1:] = go.sync(*dz_parts[1:])
    out_got = [to_member(v, s) for v, s in zip(out_send, peers)]
    for j in turns:
        attend_back(j)
    out_sum.hop()
    for j in turns:
        mlp_sums[j].wait()
    mlp_other = [here.deliver(low(mlp_sums[j].close()), 0, j) for j in turns]
    for j in turns:
        attn_grads(j)
    out_got = go.sync(*out_got)
    attend_back(0)
    out_sum.hop()
    for j in turns:
        attn_sums[j].hop()
    attn_grads(0)
    mlp_other = go.sync(*mlp_other)
    own_terms = [(back[0][:5], [w_query, w_key, w_value, w_outgate, w_forget])]
    pair_terms = [(back[j][:5], *attn_w[j - 1], 0) for j in turns]
    made = go(lambda w, after: back_rows(
        "attn_back", w, peers + [0], group, share, own_terms, pair_terms, model, [bf16] * len(peers) + [f32],
        (), (inputs, group, inverse_attn), after))
    part, gain_attn_part = made[-2:]
    got = [to_member(v, s) for v, s in zip(made, peers)]
    bias_full = jnp.zeros((here.tensor, heads), f32)
    for j in range(rows):
        bias_full = lax.dynamic_update_slice(bias_full, back[j][5], (here.owner(here.at, 0, j), 0))
    small = jnp.concatenate([gain_attn_part, gain_mlp_part, bias_full.reshape(1, -1)], axis=1)
    small = go.sync(small + here.swap(small, 1))[0]
    attn_sums[0].hop()
    small = small + here.swap(small, here.bits[0])
    for j in turns:
        attn_sums[j].hop()
    small = go.sync(small)[0]
    small = here.sum_rest(small)
    out_sum.wait()
    out_part = out_sum.close()
    grad_out = out_part[:, :width]
    out_rest = [here.deliver(low(out_part[:, (i + 1) * width:(i + 2) * width]), s, j) for i, (s, j) in enumerate(slots[1:])]
    attn_other = [here.deliver(low(attn_sums[j].close()), 0, j) for j in turns]
    output = mlp_out([0], [f32], [(hidden_row, "row")] + [(v, "own") for v in out_got])[0]
    attn_sums[0].hop()
    grad_inputs = go(close_block, share, group, part, got, inputs, inverse_attn, gain_attn, dh)
    mlp = mlp_own
    for v in mlp_other:
        mlp = mlp + v.astype(f32)
    for v in out_rest:
        grad_out = grad_out + v.astype(f32)
    attn = attn_sums[0].close()
    for v in attn_other:
        attn = attn + v.astype(f32)
    bias_own = lax.dynamic_slice_in_dim(small[0, 2 * model:], here.at * heads, heads, 0)
    return (
        output,
        grad_inputs,
        small[0, :model],
        attn[:, :width],
        attn[:, width:2 * width],
        attn[:, 2 * width:3 * width],
        attn[:, 3 * width:4 * width],
        attn[:, 4 * width:4 * width + heads],
        bias_own,
        grad_out,
        small[0, model:2 * model],
        mlp[:, :hidden],
        mlp[:, hidden:2 * hidden],
        mlp[:, 2 * hidden:],
    )


def solution(mesh):
    placed = (
        P("dp", None), P(), P(None, "tensor"), P(None, "tensor"), P(None, "tensor"),
        P(None, "tensor"), P(None, "tensor"), P("tensor"), P(None, "tensor"), P(),
        P(None, "tensor"), P(None, "tensor"), P(None, "tensor"), P("dp", None), P("dp", None),
    )
    weight = P("dp", "tensor")
    tokens = P(("dp", "tensor"), None)
    return jax.shard_map(
        on_device,
        mesh=mesh,
        in_specs=placed,
        out_specs=(
            tokens, tokens, P(), weight, weight, weight, weight, weight, P("tensor"),
            weight, P(), weight, weight, weight,
        ),
        check_vma=False,
    )
```

```python
import jax
import jax.numpy as jnp
from jax import lax
from jax.sharding import PartitionSpec as P
from jax.experimental import pallas as pl
from jax.experimental.pallas import tpu as pltpu

LOG2E = 1.4426950408889634
LN2 = 0.6931471805599453
HEAD = 64
BLK = 256
EPS = 1e-06
STEP = 115 * 10 ** 9
ROW, MEMBER, CORE, CHIP, PIECE = 0, 1, 2, 3, 4
f32 = jnp.float32
bf16 = jnp.bfloat16


def last(a, b):
    return lax.dot_general(a, b, (((1,), (1,)), ((), ())), preferred_element_type=f32)


def first(a, b):
    return lax.dot_general(a, b, (((0,), (0,)), ((), ())), preferred_element_type=f32)


def mm(a, b):
    return jnp.dot(a, b, preferred_element_type=f32)


def low(values):
    return values.astype(bf16)


def shape(dims, dtype):
    return jax.ShapeDtypeStruct(dims, dtype)


def spec(block, at, mode=None):
    if block is None:
        return pl.BlockSpec(memory_space=pl.ANY)
    return pl.BlockSpec(block, at) if mode is None else pl.BlockSpec(block, at, pipeline_mode=mode)


def run(name, body, where, grid, ins, outs, scratch=(), after=(), flops=0, vmem=56):
    count, extra, made = len(ins), len(after), len(outs)

    def kernel(where_ref, *refs):
        body(where_ref, refs[:count], refs[count + extra:count + extra + made], refs[count + extra + made:])

    return pl.pallas_call(
        kernel,
        grid_spec=pltpu.PrefetchScalarGridSpec(
            num_scalar_prefetch=1,
            grid=grid,
            in_specs=[spec(*entry[1:]) for entry in ins] + [pl.BlockSpec(memory_space=pl.ANY)] * extra,
            out_specs=[spec(*entry[1:]) for entry in outs],
            scratch_shapes=list(scratch),
        ),
        out_shape=[entry[0] for entry in outs],
        compiler_params=pltpu.CompilerParams(vmem_limit_bytes=vmem << 20),
        cost_estimate=pl.CostEstimate(flops=STEP, bytes_accessed=1, transcendentals=0),
        name=name,
    )(where, *[entry[0] for entry in ins], *after)


class Part:
    def __init__(self, array, rows=None, row_at=None, cols=None, col_at=None):
        self.array = array
        self.rows = array.shape[0] if rows is None else rows
        self.cols = array.shape[1] if cols is None else cols
        self.row_at, self.col_at = row_at, col_at

    def view(self, ref, w):
        if self.row_at is None and self.col_at is None:
            return ref
        row = 0 if self.row_at is None else pl.multiple_of(self.row_at(w), self.rows)
        col = 0 if self.col_at is None else pl.multiple_of(self.col_at(w), self.cols)
        return ref.at[pl.ds(row, self.rows), pl.ds(col, self.cols)]


def stream(name, body, where, parts, outs, scratch=(), after=()):
    count, extra, made = len(parts), len(after), len(outs)
    chunks = 16

    def kernel(w, *refs):
        sources = refs[:count]
        targets = refs[count + extra:count + extra + made]
        at = count + extra + made
        held = refs[at:at + count]
        ready = refs[at + count:at + count + made]
        in_sems, out_sems = refs[at + count + made:at + count + made + 2]
        rest = refs[at + count + made + 2:]
        loads = []
        for k, part in enumerate(parts):
            copy = pltpu.make_async_copy(part.view(sources[k], w), held[k], in_sems.at[k])
            copy.start()
            loads.append(copy)
        waited = set()
        sent = []

        def get(k):
            if k not in waited:
                loads[k].wait()
                waited.add(k)
            return held[k]

        def put(k, row=None, rows=None, col=None, cols=None):
            spot = (pl.ds(0, outs[k].shape[0]) if row is None else pl.ds(row, rows),
                    pl.ds(0, outs[k].shape[1]) if col is None else pl.ds(col, cols))
            copy = pltpu.make_async_copy(ready[k].at[spot], targets[k].at[spot], out_sems.at[k, len([1 for i, _ in sent if i == k])])
            copy.start()
            sent.append((k, copy))

        body(w, get, ready, put, rest)
        for _, copy in sent:
            copy.wait()

    return pl.pallas_call(
        kernel,
        grid_spec=pltpu.PrefetchScalarGridSpec(
            num_scalar_prefetch=1, grid=(),
            in_specs=[pl.BlockSpec(memory_space=pl.ANY)] * (count + extra),
            out_specs=[pl.BlockSpec(memory_space=pl.ANY)] * made,
            scratch_shapes=[pltpu.VMEM((p.rows, p.cols), p.array.dtype) for p in parts]
            + [pltpu.VMEM(o.shape, o.dtype) for o in outs]
            + [pltpu.SemaphoreType.DMA((count,)), pltpu.SemaphoreType.DMA((made, chunks))] + list(scratch),
        ),
        out_shape=list(outs),
        compiler_params=pltpu.CompilerParams(vmem_limit_bytes=58 << 20),
        cost_estimate=pl.CostEstimate(flops=STEP, bytes_accessed=1, transcendentals=0),
        name=name,
    )(where, *[p.array for p in parts], *after)


def fixed(array):
    return (array, array.shape, lambda i, w: (0,) * array.ndim)


def fixed_out(dims, dtype):
    return (shape(dims, dtype), dims, lambda i, w: (0,) * len(dims))


def halves(values, pieces, core):
    count = values.shape[0] // pieces
    even = jnp.concatenate([values[p * count:(p + 1) * count] for p in range(0, pieces, 2)], axis=0)
    odd = jnp.concatenate([values[p * count:(p + 1) * count] for p in range(1, pieces, 2)], axis=0)
    return jnp.where(core == 0, odd, even), jnp.where(core == 0, even, odd)


def three(values):
    top = low(values)
    rest = values - top.astype(f32)
    middle = low(rest)
    return top, middle, low(rest - middle.astype(f32))


def log_keep(values):
    return jnp.minimum(values, 0.0) - jnp.log1p(jnp.exp(-jnp.abs(values)))


def lower(flip=False):
    r = lax.broadcasted_iota(jnp.int32, (BLK, BLK), 0)
    c = lax.broadcasted_iota(jnp.int32, (BLK, BLK), 1)
    return jnp.where(r <= c if flip else r >= c, 1.0, 0.0).astype(bf16)


TOK = 512


def project_tail(i, mixed, width, bias, outs, carry):
    q_ref, k_ref, v_ref, g_ref, f_ref, ccol_ref, crow_ref = outs
    q_ref[...] = low(mixed[:, :width] * (HEAD ** -0.5 * LOG2E))
    for p, ref in ((1, k_ref), (2, v_ref), (3, g_ref)):
        ref[...] = low(mixed[:, p * width:(p + 1) * width])
    heads = f_ref.shape[1]
    forget = mixed[:, 4 * width:4 * width + heads] + bias
    f_ref[...] = forget

    @pl.when(i == 0)
    def _():
        carry[...] = jnp.zeros_like(carry)

    mask = lower()
    hp = crow_ref.shape[1]
    tokens = forget.shape[0]
    for t in range(tokens // BLK):
        rows = slice(t * BLK, (t + 1) * BLK)
        wide = jnp.concatenate([log_keep(forget[rows]) * LOG2E, jnp.zeros((BLK, 128 - heads), f32)], axis=1)
        sums = sum(mm(mask, part) for part in three(wide)) + carry[0:1, :]
        carry[0:1, :] = sums[BLK - 1:BLK, :]
        ccol_ref[rows, :] = sums[:, :heads]
        flat = sums.T
        for s in range(crow_ref.shape[0]):
            crow_ref[s, :, rows] = flat[s * hp:(s + 1) * hp, :]


def together(heads):
    return 2 if heads % 2 == 0 else heads


def project_outs(length, width, heads):
    tokens = lambda i, w: (i, 0)
    return [(shape((length, width), bf16), (TOK, width), tokens) for _ in range(4)] + [
        (shape((length, heads), f32), (TOK, heads), tokens),
        (shape((length, heads), f32), (TOK, heads), tokens),
        (shape((heads // together(heads), together(heads), length), f32),
         (heads // together(heads), together(heads), TOK), lambda i, w: (0, 0, i)),
    ]


def project_own(where, length, inputs, gain, weights, bias, after=()):
    model = inputs.shape[1]
    width, heads = weights[0].shape[1], weights[4].shape[1]

    def body(w, ins, outs, scratch):
        x_ref, gain_ref, wq, wk, wv, wg, wf, b_ref = ins
        a_ref, inv_ref = outs[:2]
        x = x_ref[...].astype(f32)
        inverse = lax.rsqrt(jnp.mean(x * x, axis=1, keepdims=True) + EPS)
        a = low(x * inverse * gain_ref[...])
        a_ref[...] = a
        inv_ref[...] = inverse
        mixed = mm(a, jnp.concatenate([r[...] for r in (wq, wk, wv, wg, wf)], axis=1))
        project_tail(pl.program_id(0), mixed, width, b_ref[...], outs[2:], scratch[0])

    blocks = length // TOK
    tokens = lambda i, w: (i, 0)
    return run(
        "project_own", body, where, (blocks,),
        [(inputs, (TOK, model), lambda i, w: (w[ROW] * blocks + i, 0)), fixed(gain)]
        + [fixed(a) for a in weights] + [fixed(bias)],
        [(shape((length, model), bf16), (TOK, model), tokens), (shape((length, 1), f32), (TOK, 1), tokens)]
        + project_outs(length, width, heads),
        [pltpu.VMEM((8, 128), f32)], after, 2 * length * model * (4 * width + heads),
    )


def core_halves(ref, w, half):
    return (ref[:, pl.ds(pl.multiple_of(w[CORE] * half, 128), half)],
            ref[:, pl.ds(pl.multiple_of((1 - w[CORE]) * half, 128), half)])


def project_other(where, normed, mine, theirs, width, heads, bias, after=()):
    length, model = normed.shape
    half = model // 2

    def body(w, ins, outs, scratch):
        a_ref, m_ref, t_ref, b_ref = ins
        am, at = core_halves(a_ref, w, half)
        mixed = mm(am, m_ref[...]) + mm(at, t_ref[...])
        project_tail(pl.program_id(0), mixed, width, b_ref[...], outs, scratch[0])

    return run(
        "project_other", body, where, (length // TOK,),
        [(normed, (TOK, model), lambda i, w: (i, 0)), fixed(mine), fixed(theirs), fixed(bias)],
        project_outs(length, width, heads),
        [pltpu.VMEM((8, 128), f32)], after, 2 * length * model * (4 * width + heads),
    )


def attend_forward(where, q, k, v, g, crow, scol, srow, after=()):
    length, n = q.shape
    heads = n // HEAD
    hp = together(heads)
    width = hp * HEAD

    def body(w, ins, outs, scratch):
        q_ref, k_ref, v_ref, g_ref, crow_ref, scol_ref, srow_ref = ins
        z_ref, lse_ref = outs
        lane = lax.broadcasted_iota(jnp.int32, (1, width), 1) // HEAD
        lane1 = lax.broadcasted_iota(jnp.int32, (BLK, 128), 1)
        tri = lax.broadcasted_iota(jnp.int32, (BLK, BLK), 0) >= lax.broadcasted_iota(jnp.int32, (BLK, BLK), 1)
        crows = crow_ref[0]
        for i in range(length // BLK):
            rows = pl.ds(i * BLK, BLK)
            reach = (i + 1) * BLK
            q = q_ref[rows, :]
            same = scol_ref[rows, :] == srow_ref[:, :reach]
            if i:
                allowed = jnp.concatenate([same[:, :reach - BLK], same[:, reach - BLK:] & tri], axis=1)
            else:
                allowed = same & tri
            out = jnp.zeros((BLK, width), f32)
            stats = jnp.zeros((BLK, 128), f32)
            for h in range(hp):
                s = last(jnp.where(lane == h, q, 0), k_ref[:reach, :])
                s = jnp.where(allowed, s - crows[h:h + 1, :reach], -1e30)
                top = jnp.max(s, axis=1, keepdims=True)
                e = jnp.exp2(s - top)
                total = jnp.sum(e, axis=1, keepdims=True)
                part = mm(low(e), v_ref[:reach, :])
                out = jnp.where(lane == h, part * (1.0 / total), out)
                stats = jnp.where(lane1 == h, top + jnp.log2(total), stats)
            z_ref[rows, :] = low(out * jax.nn.sigmoid(g_ref[rows, :].astype(f32)))
            lse_ref[0, :, i * BLK:(i + 1) * BLK] = stats.T[:hp, :]

    tokens = lambda i, w: (0, i)
    return run(
        "attend_forward", body, where, (heads // hp,),
        [(a, (length, width), tokens) for a in (q, k, v, g)]
        + [(crow, (1, hp, length), lambda i, w: (i, 0, 0)), fixed(scol), fixed(srow)],
        [(shape((length, n), bf16), (length, width), tokens),
         (shape((heads // hp, hp, length), f32), (1, hp, length), lambda i, w: (i, 0, 0))],
        (), after, heads * length * length * 1100,
    )


def attend_backward(where, q, k, v, g, z, dz_parts, lse, ccol, forget, scol, srow, after=()):
    length, n = q.shape
    heads = n // HEAD
    hp = together(heads)
    width = hp * HEAD
    steps = heads // hp
    group = len(dz_parts)
    share = length // group

    def body(w, ins, outs, scratch):
        q_ref, k_ref, v_ref, g_ref, z_ref = ins[:5]
        dz_refs = ins[5:5 + group]
        lse_ref, ccol_ref, f_ref, scol_ref, srow_ref = ins[5 + group:]
        dq_ref, dk_ref, dv_ref, dg_ref, df_ref, db_ref = outs
        dqacc, dkacc, rates, dzfull = scratch
        step = pl.program_id(0)
        lane = lax.broadcasted_iota(jnp.int32, (1, width), 1) // HEAD
        lane1 = lax.broadcasted_iota(jnp.int32, (1, 128), 1)
        tri = lax.broadcasted_iota(jnp.int32, (BLK, BLK), 1) >= lax.broadcasted_iota(jnp.int32, (BLK, BLK), 0)
        blocks = length // BLK

        @pl.when(step == 0)
        def _():
            rates[...] = jnp.zeros_like(rates)

        for s in range(group):
            at = lax.rem(w[MEMBER] + s, group) * share
            dzfull[pl.ds(pl.multiple_of(at, share), share), :] = dz_refs[s][...]
        sig = jax.nn.sigmoid(g_ref[...].astype(f32))
        dz = dzfull[...].astype(f32)
        prod = dz * z_ref[...].astype(f32)
        dout = low(dz * sig)
        dg_ref[...] = low(prod * (1.0 - sig))
        prod_hi = low(prod)
        prod_lo = low(prod - prod_hi.astype(f32))
        lses = lse_ref[0]
        for h in range(hp):
            head = lane == h
            index = step * hp + h
            decay = jnp.sum(jnp.where(lane1[:, :heads] == index, ccol_ref[...], 0.0), axis=1, keepdims=True)
            ones = jnp.broadcast_to(jnp.where(head, 1.0, 0.0).astype(bf16), (8, width))
            centre = (last(ones, prod_hi) + last(ones, prod_lo))[0:1, :]
            q_one = jnp.where(head, q_ref[...], 1.0)
            q_zero = jnp.where(head, q_ref[...], 0.0)
            k_one = jnp.where(head, k_ref[...], 1.0)
            d_zero = jnp.where(head, dout, 0.0)
            dqacc[...] = jnp.zeros_like(dqacc)
            for j in range(blocks):
                keys = pl.ds(j * BLK, BLK)
                lo = j * BLK
                s = last(k_ref[keys, :], q_zero[lo:, :])
                s = s - decay[lo:lo + BLK, :] - lses[h:h + 1, lo:]
                same = scol_ref[keys, :] == srow_ref[:, lo:]
                if j < blocks - 1:
                    allowed = jnp.concatenate([same[:, :BLK] & tri, same[:, BLK:]], axis=1)
                else:
                    allowed = same & tri
                p = jnp.exp2(jnp.where(allowed, s, -1e30))
                dp = last(v_ref[keys, :], d_zero[lo:, :])
                ds = low(p * (dp - centre[:, lo:]))
                dv = mm(low(p), dout[lo:, :])
                dk = mm(ds, q_one[lo:, :])
                dqacc[lo:, :] += first(ds, k_one[lo:lo + BLK, :])
                dkacc[keys, :] = dk
                if h == 0:
                    dk_ref[keys, :] = low(dk * LN2)
                    dv_ref[keys, :] = low(dv)
                else:
                    dk_ref[keys, :] = jnp.where(head, low(dk * LN2), dk_ref[keys, :])
                    dv_ref[keys, :] = jnp.where(head, low(dv), dv_ref[keys, :])
            dq = dqacc[...]
            if h == 0:
                dq_ref[...] = low(dq * HEAD ** -0.5)
            else:
                dq_ref[...] = jnp.where(head, low(dq * HEAD ** -0.5), dq_ref[...])
            spare = HEAD if h == 0 else 0
            rate = (dq - dkacc[...])[:, spare:spare + 1]
            rates[...] = jnp.where(lane1 == index, rate, rates[...])

        @pl.when(step == steps - 1)
        def _():
            mask = lower(True)
            carry = jnp.zeros((1, 128), f32)
            bias = jnp.zeros((1, heads), f32)
            for b in reversed(range(blocks)):
                rows = pl.ds(b * BLK, BLK)
                sums = sum(mm(mask, part) for part in three(rates[rows, :])) + carry
                carry = sums[0:1, :]
                df = low(sums[:, :heads] * jax.nn.sigmoid(-f_ref[rows, :]))
                df_ref[rows, :] = df
                bias = bias + jnp.sum(df.astype(f32), axis=0, keepdims=True)
            db_ref[...] = bias

    tokens = lambda i, w: (0, i)
    wide = (shape((length, n), bf16), (length, width), tokens)
    return run(
        "attend_backward", body, where, (steps,),
        [(a, (length, width), tokens) for a in (q, k, v, g, z)]
        + [(a, (share, width), lambda i, w, off=off: (0, off + i)) for a, off in dz_parts]
        + [(lse, (1, hp, length), lambda i, w: (i, 0, 0))] + [fixed(a) for a in (ccol, forget, scol, srow)],
        [wide] * 4 + [fixed_out((length, heads), bf16), fixed_out((1, heads), f32)],
        [pltpu.VMEM((length, width), f32), pltpu.VMEM((length, width), f32), pltpu.VMEM((length, 128), f32),
         pltpu.VMEM((length, width), bf16)],
        after, heads * length * length * 1500,
    )


def close_attention(where, length, inputs, gated, out_own, out_mine, out_theirs, gain, after=()):
    model = inputs.shape[1]
    half = model // 2
    width = out_own.shape[1]

    def body(w, ins, outs, scratch):
        x_ref, own_ref, m_ref, t_ref, gain_ref = ins[:5]
        z = jnp.concatenate([r[...] for r in ins[5:]], axis=1)
        h_ref, a_ref, inv_ref = outs
        for ref, core in ((m_ref, w[CORE]), (t_ref, 1 - w[CORE])):
            at = pl.ds(pl.multiple_of(core * half, 128), half)
            own = own_ref[pl.ds(pl.multiple_of(core * half, 128), half), :]
            rest = ref[:, :(len(gated) - 1) * width]
            h_ref[:, at] = x_ref[:, at].astype(f32) + last(z, jnp.concatenate([own, rest], axis=1))
        h = h_ref[...]
        inverse = lax.rsqrt(jnp.mean(h * h, axis=1, keepdims=True) + EPS)
        a = low(h * inverse * gain_ref[...])
        a_ref[...] = a
        inv_ref[...] = inverse

    blocks = length // TOK
    tokens = lambda i, w: (i, 0)
    return run(
        "close_attention", body, where, (blocks,),
        [(inputs, (TOK, model), lambda i, w: (w[ROW] * blocks + i, 0))]
        + [fixed(a) for a in (out_own, out_mine, out_theirs, gain)]
        + [(z, (TOK, width), tokens) for z in gated],
        [(shape((length, model), f32), (TOK, model), tokens), (shape((length, model), bf16), (TOK, model), tokens),
         (shape((length, 1), f32), (TOK, 1), tokens)],
        (), after, 2 * length * model * width * len(gated),
    )


def once(array_or_shape, block, at):
    return (array_or_shape, block, at, pl.Buffered(1))


def feed_forward(where, normed, cotangent, weights, hidden, gain, group, pieces, before, final, after=()):
    length, model = normed.shape
    half = model // 2
    share = length // group
    wide = BLK if hidden % BLK == 0 else hidden
    steps = hidden // wide
    own = len(weights) == 3
    tokens = length // TOK

    def body(w, ins, outs, scratch):
        a_ref, e_ref, gain_ref = ins[:3]
        blocks = ins[3:3 + (3 if own else 6)]
        rest = ins[3 + len(blocks):]
        back, out = scratch[:2]
        kept = scratch[2:5]
        step = pl.program_id(0)
        core = pl.ds(pl.multiple_of(w[CORE] * half, 128), half)
        other = pl.ds(pl.multiple_of((1 - w[CORE]) * half, 128), half)
        copies = [pltpu.make_async_copy(r, scratch[5 + k], scratch[5 + len(rest)].at[k]) for k, r in enumerate(rest)]

        @pl.when(step == 0)
        def _():
            for c in copies:
                c.start()
            back[...] = jnp.zeros_like(back)
            out[...] = jnp.zeros_like(out)

        for t in range(tokens):
            rows = pl.ds(t * TOK, TOK)
            if own:
                gate, up = mm(a_ref[rows, :], blocks[0][...]), mm(a_ref[rows, :], blocks[1][...])
                dm = mm(e_ref[rows, :], blocks[2][...])
            else:
                both = lambda ref, p: mm(ref[rows, core], blocks[p][...]) + mm(ref[rows, other], blocks[3 + p][...])
                gate, up, dm = both(a_ref, 0), both(a_ref, 1), both(e_ref, 2)
            sig = jax.nn.sigmoid(gate)
            act = gate * sig
            values = (low(dm * up * (sig * (1.0 + gate * (1.0 - sig)))), low(dm * act), low(act * up))
            for k, value in enumerate(values):
                kept[k][rows, :] = value
                if final:
                    outs[k][rows, :] = value
        du, dw, m = kept
        if own:
            back[...] += last(du[...], blocks[0][...]) + last(dw[...], blocks[1][...])
            out[...] += last(m[...], blocks[2][...])
        else:
            for where_to, p in ((core, 0), (other, 3)):
                back[:, where_to] += last(du[...], blocks[p][...]) + last(dw[...], blocks[p + 1][...])
                out[:, where_to] += last(m[...], blocks[p + 2][...])
        if not final:
            for k, left in enumerate((a_ref, a_ref, e_ref)):
                send, keep = halves(low(first(left[...], kept[k][...])), pieces, w[CORE])
                outs[0][:, k * wide:(k + 1) * wide] = send
                outs[1][:, k * wide:(k + 1) * wide] = keep

        @pl.when(step == steps - 1)
        def _():
            for c in copies:
                c.wait()
            if rest:
                back[...] += scratch[5][...].astype(f32)
                out[...] += scratch[6][...].astype(f32)
            if final:
                for k in range(group):
                    member = lax.rem(w[MEMBER] + (k + 1) % group, group)
                    rows = pl.ds(pl.multiple_of(member * share, share), share)
                    outs[3 + k][...] = low(back[rows, :])
                    outs[3 + group + k][...] = low(out[rows, :])
                outs[3 + 2 * group][...] = jnp.sum(back[...] * a_ref[...].astype(f32), axis=0, keepdims=True) / gain_ref[...]
            else:
                outs[2][...] = low(back[...])
                outs[3][...] = low(out[...])

    whole = lambda i, w: (0, 0)
    column = lambda i, w: (0, i)
    if own:
        parts = [(a, (model, wide), column) for a in weights]
    else:
        gm, gt, dm, dt = weights
        parts = [(a, (half, wide), lambda i, w, p=p: (0, p * steps + i))
                 for a, p in ((gm, 0), (gm, 1), (dm, 0), (gt, 0), (gt, 1), (dt, 0))]
    row_sum = once(shape((length, model), bf16), (length, model), whole)
    if final:
        outs = [(shape((length, hidden), bf16), (length, wide), column)] * 3
        outs += [once(shape((share, model), bf16), (share, model), whole)] * (2 * group)
        outs += [fixed_out((1, model), f32)]
    else:
        side = (shape((half, 3 * hidden), bf16), (half, 3 * wide), column)
        outs = [side, side, row_sum, row_sum]
    return run(
        "feed_forward", body, where, (steps,),
        [once(normed, (length, model), whole), once(cotangent, (length, model), lambda i, w: (w[ROW], 0)), fixed(gain)] + parts
        + [(a, None, None) for a in before],
        outs,
        [pltpu.VMEM((length, model), f32)] * 2 + [pltpu.VMEM((length, wide), bf16)] * 3
        + [pltpu.VMEM((length, model), bf16) for _ in before]
        + ([pltpu.SemaphoreType.DMA((len(before),))] if before else []),
        after,
    )


def weight_grads(name, where, lefts, groups, pieces, rows_of=False, row_of=(), mixed=0, after=()):
    length = groups[0][1][0].shape[0] if not rows_of else lefts[0].shape[0]
    half = lefts[0].shape[1] // 2
    widths = [sum(r.shape[1] for r in rights) for _, rights in groups]
    padded = [-(-n // 256) * 256 for n in widths]
    parts, plan, loaded = [], [], {}
    row_at = (lambda w: w[MEMBER] * length) if rows_of else None
    for k, (s, rights) in enumerate(groups):
        if s not in loaded:
            loaded[s] = len(parts)
            parts.append(Part(lefts[s], length, (lambda w: w[ROW] * length) if s in row_of else None))
        at = []
        for r in rights:
            at.append(len(parts))
            parts.append(Part(r, length, row_at, r.shape[1]))
        plan.append((loaded[s], at, sum(padded[:k]), widths[k], padded[k]))

    def body(w, get, ready, put, rest):
        for k, (left, at, col, n, full) in enumerate(plan):
            left = get(left)[...]
            right = [get(k)[...] for k in at]
            value = low(first(left, right[0] if len(right) == 1 else jnp.concatenate(right, axis=1)))
            for which, part in enumerate(halves(value, pieces, w[CORE])):
                if mixed:
                    for b in range(n // mixed):
                        spot = (b * len(plan) + k) * mixed
                        ready[which][:, spot:spot + mixed] = part[:, b * mixed:(b + 1) * mixed]
                        put(which, col=spot, cols=mixed)
                    continue
                ready[which][:, col:col + n] = part
                if n < full:
                    ready[which][:, col + n:col + full] = jnp.zeros((half, full - n), bf16)
                put(which, col=col, cols=full)

    return stream(name, body, where, parts, [shape((half, sum(padded)), bf16)] * 2, (), after)


def fold(where, entries, after=()):
    keep, _, bits, _, _, width = entries[0]
    rows = keep.shape[0]
    count = len(bits)
    pieces = 1 << count
    piece = rows // pieces
    wide = next(n for n in (768, 512, 384, width) if width % n == 0)
    across = width // wide
    block = (piece, wide)
    ins, outs = [], []
    for keep, got, bits, bit_at, col, _ in entries:
        place = count - 1 - bits.index(bit_at)

        def index(mine, place=place, bit_at=bit_at, col=col):
            def at(i, c, w):
                own = lax.rem(w[CHIP] // (bit_at >> 1), 2)
                bit = own if mine else 1 - own
                low_part = lax.rem(i, 1 << place)
                high = i // (1 << place)
                return ((high * 2 + bit) * (1 << place) + low_part, col * across + c)
            return at

        for mine in (False, True):
            ins += [(keep, block, index(mine)), (got, block, index(mine))]
            outs.append((shape((rows // 2, width), bf16), block, lambda i, c, w: (i, c)))

    def body(w, ins_, outs_, scratch):
        for k, out in enumerate(outs_):
            out[...] = ins_[2 * k][...] + ins_[2 * k + 1][...]

    return run("fold", body, where, (pieces // 2, across), ins, outs, (), after, 10 ** 9)


def assemble(where, pieces, masks, after=()):
    count, extra = len(pieces), len(after)
    rows, width = pieces[0].shape

    def kernel(w, *refs):
        out, sems = refs[count + extra], refs[count + extra + 1]
        copies = []
        for k in range(count):
            at = pl.multiple_of(jnp.bitwise_xor(w[CHIP], masks[k]) * rows, rows)
            copies.append(pltpu.make_async_copy(refs[k], out.at[pl.ds(at, rows), :], sems.at[k]))
        for c in copies:
            c.start()
        for c in copies:
            c.wait()

    return pl.pallas_call(
        kernel,
        grid_spec=pltpu.PrefetchScalarGridSpec(
            num_scalar_prefetch=1, grid=(1,),
            in_specs=[pl.BlockSpec(memory_space=pl.ANY)] * (count + extra),
            out_specs=pl.BlockSpec((count * rows, width), lambda i, w: (0, 0)),
            scratch_shapes=[pltpu.SemaphoreType.DMA((count,))],
        ),
        out_shape=shape((count * rows, width), bf16),
        compiler_params=pltpu.CompilerParams(vmem_limit_bytes=56 << 20),
        cost_estimate=pl.CostEstimate(flops=STEP, bytes_accessed=1, transcendentals=0),
        name="assemble",
    )(where, *pieces, *after)


def back_rows(name, where, steps, group, share, own_terms, pair_terms, model, dtypes, adds=(), unit=None, after=()):
    half = model // 2
    count = len(steps)
    member = lambda w, k: lax.rem(w[MEMBER] + steps[k], group)
    parts, xs_at, weights_at = [], {}, {}

    def x_parts(xs):
        for x in xs:
            for k in range(count):
                if (id(x), k) not in xs_at:
                    xs_at[id(x), k] = len(parts)
                    parts.append(Part(x, share, lambda w, k=k: member(w, k) * share))

    def w_part(a):
        if id(a) not in weights_at:
            weights_at[id(a)] = len(parts)
            parts.append(Part(a))

    for xs, weights in own_terms:
        x_parts(xs)
        for a in weights:
            w_part(a)
    for xs, mine, theirs, lo in pair_terms:
        x_parts(xs)
        w_part(mine)
    for xs, mine, theirs, lo in pair_terms:
        w_part(theirs)
    add_at = len(parts)
    for a, kind in adds:
        parts.append(Part(a, share, (lambda w: w[MEMBER] * share) if kind == "row" else None))
    unit_at = len(parts)
    if unit is not None:
        for k in range(count):
            parts.append(Part(unit[0], share, lambda w, k=k: member(w, k) * share))
        parts.append(Part(unit[1]))

    def body(w, get, ready, put, rest):
        wide = lambda xs, k: (get(xs_at[id(xs[0]), k])[...] if len(xs) == 1 else
                              jnp.concatenate([get(xs_at[id(x), k])[...] for x in xs], axis=1))
        for which in (0, 1):
            core = lax.rem(w[CORE] + which, 2)
            at = pl.multiple_of(core * half, 128)
            for k in range(count):
                total = 0.0
                for xs, weights in own_terms:
                    rows = [get(weights_at[id(a)])[pl.ds(at, half), :] for a in weights]
                    total = total + last(wide(xs, k), rows[0] if len(rows) == 1 else jnp.concatenate(rows, axis=1))
                for xs, mine, theirs, lo in pair_terms:
                    ref = get(weights_at[id((mine, theirs)[which])])
                    total = total + last(wide(xs, k), ref[:, lo:lo + sum(x.shape[1] for x in xs)])
                if unit is not None:
                    u = get(unit_at + k)[:, pl.ds(at, half)].astype(f32)
                    gained = jnp.sum(total * u, axis=0, keepdims=True) / get(unit_at + count)[:, pl.ds(at, half)]
                    gain = ready[count]
                    gain[:, pl.ds(at, half)] = gained if k == 0 else gain[:, pl.ds(at, half)] + gained
                if k == count - 1:
                    for a in range(len(adds)):
                        total = total + get(add_at + a)[:, pl.ds(at, half)].astype(f32)
                ready[k][:, pl.ds(at, half)] = total.astype(dtypes[k])
                put(k, col=at, cols=half)
        if unit is not None:
            put(count)

    outs = [shape((share, model), d) for d in dtypes]
    if unit is not None:
        outs.append(shape((1, model), f32))
    return stream(name, body, where, parts, outs, (), after)


def close_feed_forward(where, share, group, part, got, hidden_row, inverse, gain, cotangent,
                       out_own, out_mine, out_theirs, after=()):
    model = part.shape[1]
    half = model // 2
    width = out_own.shape[1]
    filled = width + out_mine.shape[1]
    own_slots = filled // group

    def body(w, ins, outs, scratch):
        p_ref, h_ref, i_ref, gain_ref, e_ref, own_ref, m_ref, t_ref = ins[:8]
        dh_ref, low_ref, mine_out, peer_out = outs
        total = p_ref[...].astype(f32)
        for r in ins[8:]:
            total = total + r[...].astype(f32)
        unit = h_ref[...] * i_ref[...]
        scaled = total * gain_ref[...]
        dh = e_ref[...].astype(f32) + i_ref[...] * (scaled - unit * jnp.mean(scaled * unit, axis=1, keepdims=True))
        dh_ref[...] = dh
        d = low(dh)
        low_ref[...] = d
        dz = 0.0
        for d_half, ref, core in zip(core_halves(low_ref, w, half), (m_ref, t_ref), (w[CORE], 1 - w[CORE])):
            own = own_ref[pl.ds(pl.multiple_of(core * half, 128), half), :]
            dz = dz + mm(d_half, jnp.concatenate([own, ref[...]], axis=1))
        mine_out[...] = low(dz[:, :own_slots])
        peer_out[...] = low(dz[:, own_slots:])

    whole = lambda i, w: (0, 0)
    mine = lambda i, w: (w[MEMBER], 0)
    return run(
        "close_feed_forward", body, where, (1,),
        [fixed(part), (hidden_row, (share, model), mine), (inverse, (share, 1), mine), fixed(gain),
         (cotangent, (share, model), lambda i, w: (w[ROW] * group + w[MEMBER], 0)),
         fixed(out_own), fixed(out_mine), fixed(out_theirs)] + [fixed(a) for a in got],
        [(shape((share, model), f32), (share, model), whole), (shape((share, model), bf16), (share, model), whole),
         (shape((share, own_slots), bf16), (share, own_slots), whole),
         (shape((share, filled - own_slots), bf16), (share, filled - own_slots), whole)],
        (), after, 2 * share * model * filled,
    )


def close_block(where, share, group, part, got, inputs, inverse, gain, dh, after=()):
    model = part.shape[1]
    step_rows = min(BLK, share)
    blocks = share // step_rows
    row_blocks = group * blocks

    def body(w, ins, outs, scratch):
        p_ref, x_ref, i_ref, gain_ref, dh_ref = ins[:5]
        total = p_ref[...].astype(f32)
        for r in ins[5:]:
            total = total + r[...].astype(f32)
        unit = x_ref[...].astype(f32) * i_ref[...]
        scaled = total * gain_ref[...]
        outs[0][...] = dh_ref[...] + i_ref[...] * (scaled - unit * jnp.mean(scaled * unit, axis=1, keepdims=True))

    tokens = lambda i, w: (i, 0)
    return run(
        "close_block", body, where, (blocks,),
        [(part, (step_rows, model), tokens),
         (inputs, (step_rows, model), lambda i, w: (w[ROW] * row_blocks + w[MEMBER] * blocks + i, 0)),
         (inverse, (step_rows, 1), lambda i, w: (w[MEMBER] * blocks + i, 0)), fixed(gain),
         (dh, (step_rows, model), tokens)] + [(a, (step_rows, model), tokens) for a in got],
        [(shape((share, model), f32), (step_rows, model), tokens)], (), after,
    )[0]


def collect(where, arrays, pieces, unit=1, after=()):
    count = arrays[0].shape[0] // pieces
    filled = sum(a.shape[1] for a in arrays)
    total = -(-filled // unit) * unit

    def body(w, ins, outs, scratch):
        at = 0
        for r in ins:
            n = r.shape[1]
            outs[0][:, at:at + n] = r[...]
            at += n
        if at < total:
            outs[0][:, at:] = jnp.zeros((count, total - at), bf16)

    return run(
        "collect", body, where, (1,),
        [(a, (count, a.shape[1]), lambda i, w: (w[PIECE], 0)) for a in arrays],
        [(shape((count, total), bf16), (count, total), lambda i, w: (0, 0))], (), after,
    )[0]


class Place:
    def __init__(self, rows):
        self.tensor = lax.axis_size("tensor")
        self.dp = lax.axis_size("dp")
        self.rows = rows
        self.group = self.tensor // rows
        self.at = lax.axis_index("tensor")
        self.dp_at = lax.axis_index("dp")
        self.bits = [1 << b for b in reversed(range(1, self.dp.bit_length() - 1))]

    def owner(self, at, step, turn):
        row, member = at // self.group, at % self.group
        return ((row + turn) % self.rows) * self.group + (member + step) % self.group

    def fetch(self, value, step, turn):
        pairs = [(self.owner(i, step, turn), i) for i in range(self.tensor)]
        return lax.ppermute(value, "tensor", pairs)

    def deliver(self, value, step, turn):
        pairs = [(i, self.owner(i, step, turn)) for i in range(self.tensor)]
        return lax.ppermute(value, "tensor", pairs)

    def swap(self, value, bit):
        return lax.ppermute(value, "dp", [(i, i ^ bit) for i in range(self.dp)])


class Chain:
    def __init__(self, where):
        self.where = where
        self.behind = ()

    def __call__(self, make, *args, extra=(), **keys):
        made = make(self.where, *args, after=self.behind + tuple(extra), **keys)
        outs = made if isinstance(made, (list, tuple)) else [made]
        self.behind = (min(outs, key=lambda a: a.size),)
        return made

    def sync(self, *values):
        out = lax.optimization_barrier((*values, *self.behind))
        self.behind = tuple(out[len(values):])
        return out[:len(values)]


def on_device(
    inputs, gain_attn, w_query, w_key, w_value, w_outgate, w_forget, forget_bias, w_out,
    gain_mlp, w_gate, w_up, w_down, segment_ids, cotangent,
):
    rows, length = segment_ids.shape
    here = Place(rows)
    group, pieces = here.group, here.dp
    heads, width, hidden = w_forget.shape[1], w_query.shape[1], w_gate.shape[1]
    model = inputs.shape[1]
    share = length // group
    row, member = here.at // group, here.at % group
    core, chip = here.dp_at % 2, here.dp_at // 2
    where = jnp.stack([row, member, core, chip, core * (pieces // 2) + chip]).astype(jnp.int32)
    go = Chain(where)
    gain_attn, gain_mlp = gain_attn[None], gain_mlp[None]
    segment = lax.dynamic_index_in_dim(segment_ids, row, 0, keepdims=False)
    scol, srow = segment[:, None], segment[None, :]
    turns = range(1, rows)
    slots = [(s, j) for s in range(group) for j in range(rows)]

    def to_member(value, step):
        return lax.ppermute(value, "tensor", [
            (i, (i // group) * group + (i % group + step) % group) for i in range(here.tensor)])

    class Gather:
        def __init__(self, piece, flip):
            self.held, self.masks = [piece], [0]
            self.left = here.bits[::-1] if flip else list(here.bits)
            self.sent = {}
            self.send()

        def send(self):
            for bit in self.left:
                for i, p in enumerate(self.held):
                    if (bit, i) not in self.sent:
                        self.sent[bit, i] = here.swap(p, bit)

        def hop(self):
            bit = self.left.pop(0)
            got = go.sync(*[self.sent[bit, i] for i in range(len(self.held))])
            self.masks = self.masks + [k ^ (bit >> 1) for k in self.masks]
            self.held = self.held + list(got)
            self.send()

        def close(self):
            while self.left:
                self.hop()
            self.mine = go(assemble, self.held, self.masks)
            self.theirs = here.swap(self.mine, 1)
            return self.mine, self.theirs

    class Reduce:
        def __init__(self, send, keep, orders):
            self.parts = None
            self.keep, self.got, self.orders = keep, here.swap(send, 1), orders

        def hop(self):
            if self.parts is None:
                n = self.keep.shape[1]
                split = len(self.orders) if n % (128 * len(self.orders)) == 0 else 1
                entries = [(self.keep, self.got, list(here.bits), self.orders[c][0], c, n // split) for c in range(split)]
                orders = [order[1:] for order in self.orders[:split]]
            else:
                entries = [(kept, got, left, order[0], 0, kept.shape[1]) for kept, got, left, order in self.parts]
                orders = [order[1:] for _, _, _, order in self.parts]
            outs = go(fold, entries)
            self.parts = [
                [outs[2 * c + 1], here.swap(outs[2 * c], e[3]), [b for b in e[2] if b != e[3]], orders[c]]
                for c, e in enumerate(entries)
            ]

        def close(self):
            while self.parts is None or self.parts[0][3]:
                self.hop()
            sums = [kept.astype(f32) + got.astype(f32) for kept, got, _, _ in self.parts]
            return sums[0] if len(sums) == 1 else jnp.concatenate(sums, axis=1)

        def wait(self):
            got = go.sync(*([self.got] if self.parts is None else [p[1] for p in self.parts]))
            if self.parts is None:
                self.got = got[0]
            else:
                for p, g in zip(self.parts, got):
                    p[1] = g

    both_ways = [here.bits, here.bits[::-1]]

    attn_piece = go(collect, [w_query, w_key, w_value, w_outgate, w_forget], pieces, 256)
    attn_got = [here.fetch(attn_piece, 0, j) for j in turns]
    bias_got = [here.fetch(forget_bias, 0, j) for j in turns]
    own = go(project_own, length, inputs, gain_attn,
             [w_query, w_key, w_value, w_outgate, w_forget], forget_bias[None])
    normed, inverse_attn = own[:2]
    mixed = {0: own[2:]}
    gated = {}
    logs = {}

    def attend(j):
        q, k, v, g, _, _, crow = mixed[j]
        z, logs[j] = go(attend_forward, q, k, v, g, crow, scol, srow)
        gated[0, j] = z
        for s in range(1, group):
            gated[s, j] = here.fetch(z, s, 0)

    def wait_gated(j):
        arrived = go.sync(*[gated[s, j] for s in range(1, group)])
        for s in range(1, group):
            gated[s, j] = arrived[s - 1]

    attend(0)
    arrived = go.sync(*attn_got, *bias_got)
    attn_got, bias_got = arrived[:rows - 1], arrived[rows - 1:]
    attn_gather = [Gather(p, False) for p in attn_got]
    out_piece = go(collect, [w_out], pieces)
    out_got = [here.fetch(out_piece, 0, j) for j in turns]
    wait_gated(0)
    for gather in attn_gather:
        gather.hop()
    out_got = go.sync(*out_got)
    out_own = jnp.concatenate([out_piece, *out_got], axis=1)
    out_peers = [here.fetch(out_own, s, 0) for s in range(1, group)]
    attn_w = [gather.close() for gather in attn_gather]
    out_peers = go.sync(*out_peers)
    out_gather = Gather(jnp.concatenate([*out_got, *out_peers], axis=1), True)
    gate_piece = go(collect, [w_gate, w_up], pieces)
    gate_got = [here.fetch(gate_piece, 0, j) for j in turns]
    for j in turns:
        mixed[j] = go(project_other, normed, *attn_w[j - 1], width, heads, bias_got[j - 1][None])
    out_gather.hop()
    for j in turns:
        attend(j)
    out_mine, out_theirs = out_gather.close()
    gate_got = go.sync(*gate_got)
    gate_gather = [Gather(p, False) for p in gate_got]
    for j in turns:
        wait_gated(j)
    down_piece = go(collect, [w_down], pieces)
    down_got = [here.fetch(down_piece, 0, j) for j in turns]
    out_theirs = go.sync(out_theirs)[0]
    for gather in gate_gather:
        gather.hop()
    hidden_row, mlp_normed, inverse_mlp = go(
        close_attention, length, inputs, [gated[slot] for slot in slots], w_out, out_mine, out_theirs, gain_mlp
    )
    down_got = go.sync(*down_got)
    down_gather = [Gather(p, True) for p in down_got]

    def ffn(weights, before, final):
        return go(feed_forward, mlp_normed, cotangent, weights, hidden, gain_mlp, group, pieces, before, final)

    wide = BLK if hidden % BLK == 0 else hidden
    mlp_sums = {}
    send, keep, *carried = ffn([w_gate, w_up, w_down], [], False)
    gate_w = [gather.close() for gather in gate_gather]
    for gather in down_gather:
        gather.hop()
    down_w = [gather.close() for gather in down_gather]
    mlp_sums[0] = Reduce(send, keep, both_ways)
    mlp_w = {}
    for j in turns:
        mlp_w[j] = gate_w[j - 1] + down_w[j - 1]
        if j < rows - 1:
            send, keep, *carried = ffn(mlp_w[j], carried, False)
            mlp_sums[j] = Reduce(send, keep, both_ways)
    mlp_sums[0].hop()
    du, dw, m, *made = ffn(mlp_w[rows - 1], carried, True)
    peers = list(range(1, group))
    part, out_part_own, gain_mlp_part = made[group - 1], made[2 * group - 1], made[2 * group]
    out_send = made[group:2 * group - 1]
    got = [to_member(v, s) for v, s in zip(made, peers)]
    mlp_sums[0].hop()
    mlp_sums[rows - 1] = Reduce(*go(lambda w, after: weight_grads(
        "mlp_grads", w, [mlp_normed, cotangent], [(0, [du]), (0, [dw]), (1, [m])], pieces, row_of=(1,), mixed=wide, after=after)), both_ways)
    dh, dh_low, dz_mine, dz_peers = go(
        close_feed_forward, share, group, part, got, hidden_row, inverse_mlp, gain_mlp, cotangent,
        w_out, out_mine, out_theirs,
    )
    dz_parts = [dz_mine]
    own_slots = rows * width
    for s in peers:
        lo = (group - s - 1) * own_slots
        dz_parts.append(here.fetch(dz_peers if group == 2 else dz_peers[:, lo:lo + own_slots], s, 0))
    mlp_sums[0].wait()
    mlp_own = mlp_sums[0].close()
    for j in turns:
        mlp_sums[j].hop()
    out_sum = Reduce(*go(lambda w, after: weight_grads(
        "out_grads", w, [dh_low], [(0, [gated[slot] for slot in slots])], pieces, True, after=after)), both_ways[:1])

    back = {}
    attn_sums = {}
    per_step = together(heads) * HEAD

    def attend_back(j):
        q, k, v, g, forget, ccol, _ = mixed[j]
        parts = [(d, j * width // per_step) for d in dz_parts]
        if width % 128:
            parts = [(a[:, o * per_step:(o + 1) * per_step], 0) for a, o in parts]
        back[j] = go(attend_backward, q, k, v, g, gated[0, j], parts, logs[j], ccol, forget, scol, srow)

    def attn_grads(j, orders):
        attn_sums[j] = Reduce(*go(lambda w, after: weight_grads(
            "attn_grads", w, [normed], [(0, back[j][:5])], pieces, after=after)), orders)

    arrived = go.sync(*dz_parts[1:], *out_send)
    dz_parts[1:], out_send = arrived[:group - 1], arrived[group - 1:]
    out_got = [to_member(v, s) for v, s in zip(out_send, peers)]
    for j in turns:
        attend_back(j)
        attn_grads(j, both_ways)
    for j in turns:
        mlp_sums[j].hop()
    out_sum.hop()
    out_got = go.sync(*out_got)
    for j in turns:
        attn_sums[j].hop()
    for j in turns:
        mlp_sums[j].wait()
    mlp_other = [here.deliver(low(mlp_sums[j].close()), 0, j) for j in turns]
    attend_back(0)
    out_sum.hop()
    for j in turns:
        attn_sums[j].hop()
    attn_grads(0, both_ways)
    mlp_other = go.sync(*mlp_other)
    for j in turns:
        attn_sums[j].wait()
    attn_other = [here.deliver(low(attn_sums[j].close()), 0, j) for j in turns]
    out_sum.wait()
    out_part = out_sum.close().reshape(-1, group, rows, width)
    out_turned = [here.deliver(low(out_part[:, :, j]).reshape(-1, group * width), 0, j) for j in turns]
    own_terms = [(back[0][:5], [w_query, w_key, w_value, w_outgate, w_forget])]
    pair_terms = [(back[j][:5], *attn_w[j - 1], 0) for j in turns]

    def attn_back(name, steps):
        return go(lambda w, after: back_rows(
            name, w, steps, group, share, own_terms, pair_terms, model, [bf16] * len(steps), (), (normed, gain_attn), after))

    made = attn_back("attn_back_send", peers)
    got = [to_member(v, s) for v, s in zip(made, peers)]
    arrived = go.sync(*attn_other, *out_turned)
    attn_other, out_turned = arrived[:rows - 1], arrived[rows - 1:]
    attn_sums[0].hop()
    part, gained = attn_back("attn_back_own", [0])
    bias_full = jnp.zeros((here.tensor, heads), f32)
    for j in range(rows):
        bias_full = lax.dynamic_update_slice(bias_full, back[j][5], (here.owner(here.at, 0, j), 0))
    small = jnp.concatenate([made[-1] + gained, gain_mlp_part, bias_full.reshape(1, -1)], axis=1)
    small_hops = [lambda v, b=b: here.swap(v, b) for b in [1] + here.bits] + [
        lambda v, b=b: lax.ppermute(v, "tensor", [(i, i ^ b) for i in range(here.tensor)])
        for b in [1 << k for k in range(here.tensor.bit_length() - 1)]]
    flying = small_hops.pop(0)(small)

    def small_step():
        arrived = go.sync(flying)[0]
        total = small + arrived
        return total, (small_hops.pop(0)(total) if small_hops else None)

    attn_sums[0].hop()
    small, flying = small_step()
    out_part = out_part[:, :, 0].reshape(-1, group * width) + sum(v.astype(f32) for v in out_turned)
    grad_out = out_part[:, :width]
    out_rest = [here.deliver(low(out_part[:, s * width:(s + 1) * width]), s, 0) for s in peers]
    out_own, *arrived = go.sync(out_part_own, *out_got)
    output = lax.dynamic_slice_in_dim(hidden_row, member * share, share, 0) + out_own.astype(f32)
    for v in arrived:
        output = output + v.astype(f32)
    small, flying = small_step()
    mlp_own, *mlp_other = go.sync(mlp_own, *mlp_other)
    attn_sums[0].wait()
    attn = attn_sums[0].close()
    while flying is not None:
        small, flying = small_step()
    out_rest = go.sync(*out_rest)
    grad_inputs = go(close_block, share, group, part, got, inputs, inverse_attn, gain_attn, dh)
    mlp = mlp_own
    for v in mlp_other:
        mlp = mlp + v.astype(f32)

    def columns(kind):
        return jnp.concatenate([mlp[:, b + kind * wide:b + (kind + 1) * wide] for b in range(0, 3 * hidden, 3 * wide)], axis=1)

    for v in out_rest:
        grad_out = grad_out + v.astype(f32)
    for v in attn_other:
        attn = attn + v.astype(f32)
    bias_own = lax.dynamic_slice_in_dim(small[0, 2 * model:], here.at * heads, heads, 0)
    return (
        output,
        grad_inputs,
        small[0, :model],
        attn[:, :width],
        attn[:, width:2 * width],
        attn[:, 2 * width:3 * width],
        attn[:, 3 * width:4 * width],
        attn[:, 4 * width:4 * width + heads],
        bias_own,
        grad_out,
        small[0, model:2 * model],
        columns(0),
        columns(1),
        columns(2),
    )


def solution(mesh):
    placed = (
        P("dp", None), P(), P(None, "tensor"), P(None, "tensor"), P(None, "tensor"),
        P(None, "tensor"), P(None, "tensor"), P("tensor"), P(None, "tensor"), P(),
        P(None, "tensor"), P(None, "tensor"), P(None, "tensor"), P("dp", None), P("dp", None),
    )
    weight = P("dp", "tensor")
    tokens = P(("dp", "tensor"), None)
    return jax.shard_map(
        on_device,
        mesh=mesh,
        in_specs=placed,
        out_specs=(
            tokens, tokens, P(), weight, weight, weight, weight, weight, P("tensor"),
            weight, P(), weight, weight, weight,
        ),
        check_vma=False,
    )
```

```python
import jax
import jax.numpy as jnp
from jax import lax
from jax.sharding import PartitionSpec as P
from jax.experimental import pallas as pl
from jax.experimental.pallas import tpu as pltpu

LOG2E = 1.4426950408889634
LN2 = 0.6931471805599453
HEAD = 64
BLK = 256
EPS = 1e-06
STEP = 115 * 10 ** 9
ROW, MEMBER, CORE, CHIP, PIECE = 0, 1, 2, 3, 4
f32 = jnp.float32
bf16 = jnp.bfloat16


def last(a, b):
    return lax.dot_general(a, b, (((1,), (1,)), ((), ())), preferred_element_type=f32)


def first(a, b):
    return lax.dot_general(a, b, (((0,), (0,)), ((), ())), preferred_element_type=f32)


def mm(a, b):
    return jnp.dot(a, b, preferred_element_type=f32)


def low(values):
    return values.astype(bf16)


def shape(dims, dtype):
    return jax.ShapeDtypeStruct(dims, dtype)


def spec(block, at, mode=None):
    if block is None:
        return pl.BlockSpec(memory_space=pl.ANY)
    return pl.BlockSpec(block, at) if mode is None else pl.BlockSpec(block, at, pipeline_mode=mode)


def run(name, body, where, grid, ins, outs, scratch=(), after=(), flops=0, vmem=56):
    count, extra, made = len(ins), len(after), len(outs)

    def kernel(where_ref, *refs):
        body(where_ref, refs[:count], refs[count + extra:count + extra + made], refs[count + extra + made:])

    return pl.pallas_call(
        kernel,
        grid_spec=pltpu.PrefetchScalarGridSpec(
            num_scalar_prefetch=1,
            grid=grid,
            in_specs=[spec(*entry[1:]) for entry in ins] + [pl.BlockSpec(memory_space=pl.ANY)] * extra,
            out_specs=[spec(*entry[1:]) for entry in outs],
            scratch_shapes=list(scratch),
        ),
        out_shape=[entry[0] for entry in outs],
        compiler_params=pltpu.CompilerParams(vmem_limit_bytes=vmem << 20),
        cost_estimate=pl.CostEstimate(flops=STEP, bytes_accessed=1, transcendentals=0),
        name=name,
    )(where, *[entry[0] for entry in ins], *after)


class Part:
    def __init__(self, array, rows=None, row_at=None, cols=None, col_at=None, into=None):
        self.array = array
        self.rows = array.shape[0] if rows is None else rows
        self.cols = array.shape[1] if cols is None else cols
        self.row_at, self.col_at = row_at, col_at
        self.into = into

    def view(self, ref, w):
        if self.row_at is None and self.col_at is None:
            return ref
        row = 0 if self.row_at is None else pl.multiple_of(self.row_at(w), self.rows)
        col = 0 if self.col_at is None else pl.multiple_of(self.col_at(w), self.cols)
        return ref.at[pl.ds(row, self.rows), pl.ds(col, self.cols)]


def stream(name, body, where, parts, outs, scratch=(), after=(), buffers=()):
    count, extra, made = len(parts), len(after), len(outs)
    single = [p for p in parts if p.into is None]
    chunks = 16

    def kernel(w, *refs):
        sources = refs[:count]
        targets = refs[count + extra:count + extra + made]
        at = count + extra + made
        shared = refs[at:at + len(buffers)]
        at += len(buffers)
        alone = iter(refs[at:at + len(single)])
        held = [next(alone) if p.into is None else shared[p.into[0]].at[
            pl.ds(p.into[1](w) if callable(p.into[1]) else p.into[1], p.rows), pl.ds(p.into[2], p.cols)] for p in parts]
        at += len(single)
        ready = refs[at:at + made]
        in_sems, out_sems = refs[at + made:at + made + 2]
        rest = shared + refs[at + made + 2:]
        loads = []
        for k, part in enumerate(parts):
            copy = pltpu.make_async_copy(part.view(sources[k], w), held[k], in_sems.at[k])
            copy.start()
            loads.append(copy)
        waited = set()
        sent = []

        def get(k):
            if k not in waited:
                loads[k].wait()
                waited.add(k)
            return held[k]

        def put(k, row=None, rows=None, col=None, cols=None):
            spot = (pl.ds(0, outs[k].shape[0]) if row is None else pl.ds(row, rows),
                    pl.ds(0, outs[k].shape[1]) if col is None else pl.ds(col, cols))
            copy = pltpu.make_async_copy(ready[k].at[spot], targets[k].at[spot], out_sems.at[k, len([1 for i, _ in sent if i == k])])
            copy.start()
            sent.append((k, copy))

        body(w, get, ready, put, rest)
        for _, copy in sent:
            copy.wait()

    return pl.pallas_call(
        kernel,
        grid_spec=pltpu.PrefetchScalarGridSpec(
            num_scalar_prefetch=1, grid=(),
            in_specs=[pl.BlockSpec(memory_space=pl.ANY)] * (count + extra),
            out_specs=[pl.BlockSpec(memory_space=pl.ANY)] * made,
            scratch_shapes=[pltpu.VMEM(b, bf16) for b in buffers]
            + [pltpu.VMEM((p.rows, p.cols), p.array.dtype) for p in single]
            + [pltpu.VMEM(o.shape, o.dtype) for o in outs]
            + [pltpu.SemaphoreType.DMA((count,)), pltpu.SemaphoreType.DMA((made, chunks))] + list(scratch),
        ),
        out_shape=list(outs),
        compiler_params=pltpu.CompilerParams(vmem_limit_bytes=58 << 20),
        cost_estimate=pl.CostEstimate(flops=STEP, bytes_accessed=1, transcendentals=0),
        name=name,
    )(where, *[p.array for p in parts], *after)


def fixed(array):
    return (array, array.shape, lambda i, w: (0,) * array.ndim)


def fixed_out(dims, dtype):
    return (shape(dims, dtype), dims, lambda i, w: (0,) * len(dims))


def halves(values, pieces, core):
    count = values.shape[0] // pieces
    even = jnp.concatenate([values[p * count:(p + 1) * count] for p in range(0, pieces, 2)], axis=0)
    odd = jnp.concatenate([values[p * count:(p + 1) * count] for p in range(1, pieces, 2)], axis=0)
    return jnp.where(core == 0, odd, even), jnp.where(core == 0, even, odd)


def three(values):
    top = low(values)
    rest = values - top.astype(f32)
    middle = low(rest)
    return top, middle, low(rest - middle.astype(f32))


def log_keep(values):
    return jnp.minimum(values, 0.0) - jnp.log1p(jnp.exp(-jnp.abs(values)))


def lower(flip=False):
    r = lax.broadcasted_iota(jnp.int32, (BLK, BLK), 0)
    c = lax.broadcasted_iota(jnp.int32, (BLK, BLK), 1)
    return jnp.where(r <= c if flip else r >= c, 1.0, 0.0).astype(bf16)


TOK = 512


def project_tail(i, mixed, width, bias, outs, carry):
    q_ref, k_ref, v_ref, g_ref, f_ref, ccol_ref, crow_ref = outs
    q_ref[...] = low(mixed[:, :width] * (HEAD ** -0.5 * LOG2E))
    for p, ref in ((1, k_ref), (2, v_ref), (3, g_ref)):
        ref[...] = low(mixed[:, p * width:(p + 1) * width])
    heads = f_ref.shape[1]
    forget = mixed[:, 4 * width:4 * width + heads] + bias
    f_ref[...] = forget

    @pl.when(i == 0)
    def _():
        carry[...] = jnp.zeros_like(carry)

    mask = lower()
    hp = crow_ref.shape[1]
    tokens = forget.shape[0]
    for t in range(tokens // BLK):
        rows = slice(t * BLK, (t + 1) * BLK)
        wide = jnp.concatenate([log_keep(forget[rows]) * LOG2E, jnp.zeros((BLK, 128 - heads), f32)], axis=1)
        sums = sum(mm(mask, part) for part in three(wide)) + carry[0:1, :]
        carry[0:1, :] = sums[BLK - 1:BLK, :]
        ccol_ref[rows, :] = sums[:, :heads]
        flat = sums.T
        for s in range(crow_ref.shape[0]):
            crow_ref[s, :, rows] = flat[s * hp:(s + 1) * hp, :]


def together(heads):
    return 2 if heads % 2 == 0 else heads


def project_outs(length, width, heads):
    tokens = lambda i, w: (i, 0)
    return [(shape((length, width), bf16), (TOK, width), tokens) for _ in range(4)] + [
        (shape((length, heads), f32), (TOK, heads), tokens),
        (shape((length, heads), f32), (TOK, heads), tokens),
        (shape((heads // together(heads), together(heads), length), f32),
         (heads // together(heads), together(heads), TOK), lambda i, w: (0, 0, i)),
    ]


def project_own(where, length, inputs, gain, weights, bias, after=()):
    model = inputs.shape[1]
    width, heads = weights[0].shape[1], weights[4].shape[1]

    def body(w, ins, outs, scratch):
        x_ref, gain_ref, wq, wk, wv, wg, wf, b_ref = ins
        a_ref, inv_ref = outs[:2]
        x = x_ref[...].astype(f32)
        inverse = lax.rsqrt(jnp.mean(x * x, axis=1, keepdims=True) + EPS)
        a = low(x * inverse * gain_ref[...])
        a_ref[...] = a
        inv_ref[...] = inverse
        mixed = mm(a, jnp.concatenate([r[...] for r in (wq, wk, wv, wg, wf)], axis=1))
        project_tail(pl.program_id(0), mixed, width, b_ref[...], outs[2:], scratch[0])

    blocks = length // TOK
    tokens = lambda i, w: (i, 0)
    return run(
        "project_own", body, where, (blocks,),
        [(inputs, (TOK, model), lambda i, w: (w[ROW] * blocks + i, 0)), fixed(gain)]
        + [fixed(a) for a in weights] + [fixed(bias)],
        [(shape((length, model), bf16), (TOK, model), tokens), (shape((length, 1), f32), (TOK, 1), tokens)]
        + project_outs(length, width, heads),
        [pltpu.VMEM((8, 128), f32)], after, 2 * length * model * (4 * width + heads),
    )


def core_halves(ref, w, half):
    return (ref[:, pl.ds(pl.multiple_of(w[CORE] * half, 128), half)],
            ref[:, pl.ds(pl.multiple_of((1 - w[CORE]) * half, 128), half)])


def project_other(where, normed, gathered, counts, width, heads, bias, after=()):
    length, model = normed.shape
    half = model // 2

    def body(w, ins, outs, scratch):
        a_ref, b_ref = ins[:2]
        am, at = core_halves(a_ref, w, half)
        mixed = [mm(am, ins[2 + 2 * k][:, :n]) + mm(at, ins[3 + 2 * k][:, :n]) for k, n in enumerate(counts)]
        project_tail(pl.program_id(0), jnp.concatenate(mixed, axis=1), width, b_ref[...], outs, scratch[0])

    return run(
        "project_other", body, where, (length // TOK,),
        [(normed, (TOK, model), lambda i, w: (i, 0)), fixed(bias)] + [fixed(a) for pair in gathered for a in pair],
        project_outs(length, width, heads),
        [pltpu.VMEM((8, 128), f32)], after, 2 * length * model * (4 * width + heads),
    )


def attend_forward(where, q, k, v, g, crow, scol, srow, after=()):
    length, n = q.shape
    heads = n // HEAD
    hp = together(heads)
    width = hp * HEAD

    def body(w, ins, outs, scratch):
        q_ref, k_ref, v_ref, g_ref, crow_ref, scol_ref, srow_ref = ins
        z_ref, lse_ref = outs
        lane = lax.broadcasted_iota(jnp.int32, (1, width), 1) // HEAD
        lane1 = lax.broadcasted_iota(jnp.int32, (BLK, 128), 1)
        tri = lax.broadcasted_iota(jnp.int32, (BLK, BLK), 0) >= lax.broadcasted_iota(jnp.int32, (BLK, BLK), 1)
        crows = crow_ref[0]
        for i in range(length // BLK):
            rows = pl.ds(i * BLK, BLK)
            reach = (i + 1) * BLK
            q = q_ref[rows, :]
            same = scol_ref[rows, :] == srow_ref[:, :reach]
            if i:
                allowed = jnp.concatenate([same[:, :reach - BLK], same[:, reach - BLK:] & tri], axis=1)
            else:
                allowed = same & tri
            out = jnp.zeros((BLK, width), f32)
            stats = jnp.zeros((BLK, 128), f32)
            for h in range(hp):
                s = last(jnp.where(lane == h, q, 0), k_ref[:reach, :])
                s = jnp.where(allowed, s - crows[h:h + 1, :reach], -1e30)
                top = jnp.max(s, axis=1, keepdims=True)
                e = jnp.exp2(s - top)
                total = jnp.sum(e, axis=1, keepdims=True)
                part = mm(low(e), v_ref[:reach, :])
                out = jnp.where(lane == h, part * (1.0 / total), out)
                stats = jnp.where(lane1 == h, top + jnp.log2(total), stats)
            z_ref[rows, :] = low(out * jax.nn.sigmoid(g_ref[rows, :].astype(f32)))
            lse_ref[0, :, i * BLK:(i + 1) * BLK] = stats.T[:hp, :]

    tokens = lambda i, w: (0, i)
    return run(
        "attend_forward", body, where, (heads // hp,),
        [(a, (length, width), tokens) for a in (q, k, v, g)]
        + [(crow, (1, hp, length), lambda i, w: (i, 0, 0)), fixed(scol), fixed(srow)],
        [(shape((length, n), bf16), (length, width), tokens),
         (shape((heads // hp, hp, length), f32), (1, hp, length), lambda i, w: (i, 0, 0))],
        (), after, heads * length * length * 1100,
    )


def attend_backward(where, q, k, v, g, z, dz_parts, lse, ccol, forget, scol, srow, after=()):
    length, n = q.shape
    heads = n // HEAD
    hp = together(heads)
    width = hp * HEAD
    steps = heads // hp
    group = len(dz_parts)
    share = length // group

    def body(w, ins, outs, scratch):
        q_ref, k_ref, v_ref, g_ref, z_ref = ins[:5]
        dz_refs = ins[5:5 + group]
        lse_ref, ccol_ref, f_ref, scol_ref, srow_ref = ins[5 + group:]
        dq_ref, dk_ref, dv_ref, dg_ref, df_ref, db_ref = outs
        dqacc, dkacc, rates, dzfull = scratch
        step = pl.program_id(0)
        lane = lax.broadcasted_iota(jnp.int32, (1, width), 1) // HEAD
        lane1 = lax.broadcasted_iota(jnp.int32, (1, 128), 1)
        tri = lax.broadcasted_iota(jnp.int32, (BLK, BLK), 1) >= lax.broadcasted_iota(jnp.int32, (BLK, BLK), 0)
        blocks = length // BLK

        @pl.when(step == 0)
        def _():
            rates[...] = jnp.zeros_like(rates)

        for s in range(group):
            at = lax.rem(w[MEMBER] + s, group) * share
            dzfull[pl.ds(pl.multiple_of(at, share), share), :] = dz_refs[s][...]
        sig = jax.nn.sigmoid(g_ref[...].astype(f32))
        dz = dzfull[...].astype(f32)
        prod = dz * z_ref[...].astype(f32)
        dout = low(dz * sig)
        dg_ref[...] = low(prod * (1.0 - sig))
        prod_hi = low(prod)
        prod_lo = low(prod - prod_hi.astype(f32))
        lses = lse_ref[0]
        for h in range(hp):
            head = lane == h
            index = step * hp + h
            decay = jnp.sum(jnp.where(lane1[:, :heads] == index, ccol_ref[...], 0.0), axis=1, keepdims=True)
            ones = jnp.broadcast_to(jnp.where(head, 1.0, 0.0).astype(bf16), (8, width))
            centre = (last(ones, prod_hi) + last(ones, prod_lo))[0:1, :]
            q_one = jnp.where(head, q_ref[...], 1.0)
            q_zero = jnp.where(head, q_ref[...], 0.0)
            k_one = jnp.where(head, k_ref[...], 1.0)
            d_zero = jnp.where(head, dout, 0.0)
            dqacc[...] = jnp.zeros_like(dqacc)
            for j in range(blocks):
                keys = pl.ds(j * BLK, BLK)
                lo = j * BLK
                s = last(k_ref[keys, :], q_zero[lo:, :])
                s = s - decay[lo:lo + BLK, :] - lses[h:h + 1, lo:]
                same = scol_ref[keys, :] == srow_ref[:, lo:]
                if j < blocks - 1:
                    allowed = jnp.concatenate([same[:, :BLK] & tri, same[:, BLK:]], axis=1)
                else:
                    allowed = same & tri
                p = jnp.exp2(jnp.where(allowed, s, -1e30))
                dp = last(v_ref[keys, :], d_zero[lo:, :])
                ds = low(p * (dp - centre[:, lo:]))
                dv = mm(low(p), dout[lo:, :])
                dk = mm(ds, q_one[lo:, :])
                dqacc[lo:, :] += first(ds, k_one[lo:lo + BLK, :])
                dkacc[keys, :] = dk
                if h == 0:
                    dk_ref[keys, :] = low(dk * LN2)
                    dv_ref[keys, :] = low(dv)
                else:
                    dk_ref[keys, :] = jnp.where(head, low(dk * LN2), dk_ref[keys, :])
                    dv_ref[keys, :] = jnp.where(head, low(dv), dv_ref[keys, :])
            dq = dqacc[...]
            if h == 0:
                dq_ref[...] = low(dq * HEAD ** -0.5)
            else:
                dq_ref[...] = jnp.where(head, low(dq * HEAD ** -0.5), dq_ref[...])
            spare = HEAD if h == 0 else 0
            rate = (dq - dkacc[...])[:, spare:spare + 1]
            rates[...] = jnp.where(lane1 == index, rate, rates[...])

        @pl.when(step == steps - 1)
        def _():
            mask = lower(True)
            carry = jnp.zeros((1, 128), f32)
            bias = jnp.zeros((1, heads), f32)
            for b in reversed(range(blocks)):
                rows = pl.ds(b * BLK, BLK)
                sums = sum(mm(mask, part) for part in three(rates[rows, :])) + carry
                carry = sums[0:1, :]
                df = low(sums[:, :heads] * jax.nn.sigmoid(-f_ref[rows, :]))
                df_ref[rows, :] = df
                bias = bias + jnp.sum(df.astype(f32), axis=0, keepdims=True)
            db_ref[...] = bias

    tokens = lambda i, w: (0, i)
    wide = (shape((length, n), bf16), (length, width), tokens)
    return run(
        "attend_backward", body, where, (steps,),
        [(a, (length, width), tokens) for a in (q, k, v, g, z)]
        + [(a, (share, width), lambda i, w, off=off: (0, off + i)) for a, off in dz_parts]
        + [(lse, (1, hp, length), lambda i, w: (i, 0, 0))] + [fixed(a) for a in (ccol, forget, scol, srow)],
        [wide] * 4 + [fixed_out((length, heads), bf16), fixed_out((1, heads), f32)],
        [pltpu.VMEM((length, width), f32), pltpu.VMEM((length, width), f32), pltpu.VMEM((length, 128), f32),
         pltpu.VMEM((length, width), bf16)],
        after, heads * length * length * 1500,
    )


def close_attention(where, length, inputs, gated, out_own, out_mine, out_theirs, gain, after=()):
    model = inputs.shape[1]
    half = model // 2
    width = out_own.shape[1]

    def body(w, ins, outs, scratch):
        x_ref, own_ref, m_ref, t_ref, gain_ref = ins[:5]
        z = jnp.concatenate([r[...] for r in ins[5:]], axis=1)
        h_ref, a_ref, inv_ref = outs
        for ref, core in ((m_ref, w[CORE]), (t_ref, 1 - w[CORE])):
            at = pl.ds(pl.multiple_of(core * half, 128), half)
            own = own_ref[pl.ds(pl.multiple_of(core * half, 128), half), :]
            rest = ref[:, :(len(gated) - 1) * width]
            h_ref[:, at] = x_ref[:, at].astype(f32) + last(z, jnp.concatenate([own, rest], axis=1))
        h = h_ref[...]
        inverse = lax.rsqrt(jnp.mean(h * h, axis=1, keepdims=True) + EPS)
        a = low(h * inverse * gain_ref[...])
        a_ref[...] = a
        inv_ref[...] = inverse

    blocks = length // TOK
    tokens = lambda i, w: (i, 0)
    return run(
        "close_attention", body, where, (blocks,),
        [(inputs, (TOK, model), lambda i, w: (w[ROW] * blocks + i, 0))]
        + [fixed(a) for a in (out_own, out_mine, out_theirs, gain)]
        + [(z, (TOK, width), tokens) for z in gated],
        [(shape((length, model), f32), (TOK, model), tokens), (shape((length, model), bf16), (TOK, model), tokens),
         (shape((length, 1), f32), (TOK, 1), tokens)],
        (), after, 2 * length * model * width * len(gated),
    )


def once(array_or_shape, block, at):
    return (array_or_shape, block, at, pl.Buffered(1))


def feed_forward(where, normed, cotangent, weights, hidden, gain, group, pieces, before, final, after=()):
    length, model = normed.shape
    half = model // 2
    share = length // group
    wide = BLK if hidden % BLK == 0 else hidden
    steps = hidden // wide
    own = len(weights) == 3
    tokens = length // TOK

    def body(w, ins, outs, scratch):
        a_ref, e_ref, gain_ref = ins[:3]
        blocks = ins[3:3 + (3 if own else 6)]
        rest = ins[3 + len(blocks):]
        back, out = scratch[:2]
        kept = scratch[2:5]
        step = pl.program_id(0)
        core = pl.ds(pl.multiple_of(w[CORE] * half, 128), half)
        other = pl.ds(pl.multiple_of((1 - w[CORE]) * half, 128), half)
        copies = [pltpu.make_async_copy(r, scratch[5 + k], scratch[5 + len(rest)].at[k]) for k, r in enumerate(rest)]

        @pl.when(step == 0)
        def _():
            for c in copies:
                c.start()
            back[...] = jnp.zeros_like(back)
            out[...] = jnp.zeros_like(out)

        for t in range(tokens):
            rows = pl.ds(t * TOK, TOK)
            if own:
                gate, up = mm(a_ref[rows, :], blocks[0][...]), mm(a_ref[rows, :], blocks[1][...])
                dm = mm(e_ref[rows, :], blocks[2][...])
            else:
                both = lambda ref, p: mm(ref[rows, core], blocks[p][...]) + mm(ref[rows, other], blocks[3 + p][...])
                gate, up, dm = both(a_ref, 0), both(a_ref, 1), both(e_ref, 2)
            sig = jax.nn.sigmoid(gate)
            act = gate * sig
            values = (low(dm * up * (sig * (1.0 + gate * (1.0 - sig)))), low(dm * act), low(act * up))
            for k, value in enumerate(values):
                kept[k][rows, :] = value
                if final:
                    outs[k][rows, :] = value
        du, dw, m = kept
        if own:
            back[...] += last(du[...], blocks[0][...]) + last(dw[...], blocks[1][...])
            out[...] += last(m[...], blocks[2][...])
        else:
            for where_to, p in ((core, 0), (other, 3)):
                back[:, where_to] += last(du[...], blocks[p][...]) + last(dw[...], blocks[p + 1][...])
                out[:, where_to] += last(m[...], blocks[p + 2][...])
        if not final:
            for k, left in enumerate((a_ref, a_ref, e_ref)):
                send, keep = halves(low(first(left[...], kept[k][...])), pieces, w[CORE])
                outs[0][:, k * wide:(k + 1) * wide] = send
                outs[1][:, k * wide:(k + 1) * wide] = keep

        @pl.when(step == steps - 1)
        def _():
            for c in copies:
                c.wait()
            if rest:
                back[...] += scratch[5][...].astype(f32)
                out[...] += scratch[6][...].astype(f32)
            if final:
                for k in range(group):
                    member = lax.rem(w[MEMBER] + (k + 1) % group, group)
                    rows = pl.ds(pl.multiple_of(member * share, share), share)
                    outs[3 + k][...] = low(back[rows, :])
                    outs[3 + group + k][...] = low(out[rows, :])
                outs[3 + 2 * group][...] = jnp.sum(back[...] * a_ref[...].astype(f32), axis=0, keepdims=True) / gain_ref[...]
            else:
                outs[2][...] = low(back[...])
                outs[3][...] = low(out[...])

    whole = lambda i, w: (0, 0)
    column = lambda i, w: (0, i)
    if own:
        parts = [(a, (model, wide), column) for a in weights]
    else:
        gm, gt, dm, dt = weights
        parts = [(a, (half, wide), lambda i, w, p=p: (0, p * steps + i))
                 for a, p in ((gm, 0), (gm, 1), (dm, 0), (gt, 0), (gt, 1), (dt, 0))]
    row_sum = once(shape((length, model), bf16), (length, model), whole)
    if final:
        outs = [(shape((length, hidden), bf16), (length, wide), column)] * 3
        outs += [once(shape((share, model), bf16), (share, model), whole)] * (2 * group)
        outs += [fixed_out((1, model), f32)]
    else:
        side = (shape((half, 3 * hidden), bf16), (half, 3 * wide), column)
        outs = [side, side, row_sum, row_sum]
    return run(
        "feed_forward", body, where, (steps,),
        [once(normed, (length, model), whole), once(cotangent, (length, model), lambda i, w: (w[ROW], 0)), fixed(gain)] + parts
        + [(a, None, None) for a in before],
        outs,
        [pltpu.VMEM((length, model), f32)] * 2 + [pltpu.VMEM((length, wide), bf16)] * 3
        + [pltpu.VMEM((length, model), bf16) for _ in before]
        + ([pltpu.SemaphoreType.DMA((len(before),))] if before else []),
        after,
    )


def weight_grads(name, where, lefts, groups, pieces, rows_of=False, row_of=(), mixed=0, after=()):
    length = groups[0][1][0].shape[0] if not rows_of else lefts[0].shape[0]
    half = lefts[0].shape[1] // 2
    widths = [sum(r.shape[1] for r in rights) for _, rights in groups]
    padded = [-(-n // 128) * 128 for n in widths]
    padded[-1] += -sum(padded) % 256
    parts, plan, loaded = [], [], {}
    row_at = (lambda w: w[MEMBER] * length) if rows_of else None
    for k, (s, rights) in enumerate(groups):
        if s not in loaded:
            loaded[s] = len(parts)
            parts.append(Part(lefts[s], length, (lambda w: w[ROW] * length) if s in row_of else None))
        at = []
        for r in rights:
            at.append(len(parts))
            parts.append(Part(r, length, row_at, r.shape[1]))
        plan.append((loaded[s], at, sum(padded[:k]), widths[k], padded[k]))

    def body(w, get, ready, put, rest):
        for k, (left, at, col, n, full) in enumerate(plan):
            left = get(left)[...]
            right = [get(k)[...] for k in at]
            value = low(first(left, right[0] if len(right) == 1 else jnp.concatenate(right, axis=1)))
            for which, part in enumerate(halves(value, pieces, w[CORE])):
                if mixed:
                    for b in range(n // mixed):
                        spot = (b * len(plan) + k) * mixed
                        ready[which][:, spot:spot + mixed] = part[:, b * mixed:(b + 1) * mixed]
                        put(which, col=spot, cols=mixed)
                    continue
                ready[which][:, col:col + n] = part
                if n < full:
                    ready[which][:, col + n:col + full] = jnp.zeros((half, full - n), bf16)
                put(which, col=col, cols=full)

    return stream(name, body, where, parts, [shape((half, sum(padded)), bf16)] * 2, (), after)


def fold(where, entries, after=()):
    keep, _, bits, _, _, width = entries[0]
    rows = keep.shape[0]
    count = len(bits)
    pieces = 1 << count
    piece = rows // pieces
    wide = next(n for n in (768, 512, 384, width) if width % n == 0)
    across = width // wide
    block = (piece, wide)
    ins, outs = [], []
    for keep, got, bits, bit_at, col, _ in entries:
        place = count - 1 - bits.index(bit_at)

        def index(mine, place=place, bit_at=bit_at, col=col):
            def at(i, c, w):
                own = lax.rem(w[CHIP] // (bit_at >> 1), 2)
                bit = own if mine else 1 - own
                low_part = lax.rem(i, 1 << place)
                high = i // (1 << place)
                return ((high * 2 + bit) * (1 << place) + low_part, col * across + c)
            return at

        for mine in (False, True):
            ins += [(keep, block, index(mine)), (got, block, index(mine))]
            outs.append((shape((rows // 2, width), bf16), block, lambda i, c, w: (i, c)))

    def body(w, ins_, outs_, scratch):
        for k, out in enumerate(outs_):
            out[...] = ins_[2 * k][...] + ins_[2 * k + 1][...]

    return run("fold", body, where, (pieces // 2, across), ins, outs, (), after, 10 ** 9)


def assemble(where, pieces, masks, after=()):
    count, extra = len(pieces), len(after)
    rows, width = pieces[0].shape

    def kernel(w, *refs):
        out, sems = refs[count + extra], refs[count + extra + 1]
        copies = []
        for k in range(count):
            at = pl.multiple_of(jnp.bitwise_xor(w[CHIP], masks[k]) * rows, rows)
            copies.append(pltpu.make_async_copy(refs[k], out.at[pl.ds(at, rows), :], sems.at[k]))
        for c in copies:
            c.start()
        for c in copies:
            c.wait()

    return pl.pallas_call(
        kernel,
        grid_spec=pltpu.PrefetchScalarGridSpec(
            num_scalar_prefetch=1, grid=(1,),
            in_specs=[pl.BlockSpec(memory_space=pl.ANY)] * (count + extra),
            out_specs=pl.BlockSpec((count * rows, width), lambda i, w: (0, 0)),
            scratch_shapes=[pltpu.SemaphoreType.DMA((count,))],
        ),
        out_shape=shape((count * rows, width), bf16),
        compiler_params=pltpu.CompilerParams(vmem_limit_bytes=56 << 20),
        cost_estimate=pl.CostEstimate(flops=STEP, bytes_accessed=1, transcendentals=0),
        name="assemble",
    )(where, *pieces, *after)


def back_rows(name, where, step, group, own_x, own_w, pair_terms, normed, gain, after=()):
    length, model = normed.shape
    half = model // 2
    share = length // group
    member = lambda w: lax.rem(w[MEMBER] + step, group)
    row_at = lambda w: member(w) * share
    parts, tails, cuts = [], [], []
    col = 0

    def lay(arrays, buffer, narrow):
        at = col
        for a in arrays:
            n = a.shape[1]
            rows, pick = (share, row_at) if buffer == 0 else (a.shape[0], None)
            if n % 128 == 0 and at % 128 == 0:
                parts.append(Part(a, rows, pick, n, None, (buffer, 0, at)))
            else:
                tails.append((len(parts), buffer, at, n))
                parts.append(Part(a, rows, pick, n))
            at += n
        return at

    if any(a.shape[1] % 128 for a in own_x[:-1]):
        own_x, own_w = [jnp.concatenate(own_x, axis=1)], [jnp.concatenate(own_w, axis=1)]
        pair_terms = [([jnp.concatenate(xs, axis=1)], mine, theirs) for xs, mine, theirs in pair_terms]
    lay(own_x, 0, True)
    end = lay(own_w, 1, True)
    full = -(-end // 128) * 128
    cuts.append((0, len(parts), 0, full))
    col = full
    for xs, mine, theirs in pair_terms:
        first_part = len(parts)
        lay(xs, 0, True)
        n = mine.shape[1]
        parts.append(Part(mine, into=(1, lambda w: pl.multiple_of(w[CORE] * half, half), col)))
        parts.append(Part(theirs, into=(1, lambda w: pl.multiple_of((1 - w[CORE]) * half, half), col)))
        cuts.append((first_part, len(parts), col, n))
        col += n
    unit_at = len(parts)
    parts.append(Part(normed, share, row_at))
    parts.append(Part(gain))

    def body(w, get, ready, put, rest):
        x_all, w_all = rest[:2]
        for low_part, high_part, at, n in cuts:
            for k in range(low_part, high_part):
                get(k)
            for k, buffer, spot, count in tails:
                if low_part <= k < high_part:
                    target = (x_all, w_all)[buffer]
                    last_col = at + n if spot + count <= at + n else spot + count
                    value = get(k)[...]
                    fill = jnp.zeros((value.shape[0], last_col - spot - count), bf16)
                    target[:, spot:last_col] = jnp.concatenate([value, fill], axis=1) if last_col > spot + count else value
            part = last(x_all[:, at:at + n], w_all[:, at:at + n])
            rest[2][...] = part if at == 0 else rest[2][...] + part
        total = rest[2][...]
        ready[0][...] = low(total)
        put(0)
        u = get(unit_at)[...].astype(f32)
        ready[1][...] = jnp.sum(total * u, axis=0, keepdims=True) / get(unit_at + 1)[...]
        put(1)

    return stream(
        name, body, where, parts, [shape((share, model), bf16), shape((1, model), f32)],
        [pltpu.VMEM((share, model), f32)], after, [(share, col), (model, col)],
    )


def close_feed_forward(where, share, group, part, got, hidden_row, inverse, gain, cotangent,
                       out_own, out_mine, out_theirs, after=()):
    model = part.shape[1]
    half = model // 2
    width = out_own.shape[1]
    filled = width + out_mine.shape[1]
    own_slots = filled // group

    def body(w, ins, outs, scratch):
        p_ref, h_ref, i_ref, gain_ref, e_ref, own_ref, m_ref, t_ref = ins[:8]
        dh_ref, low_ref, mine_out, peer_out = outs
        total = p_ref[...].astype(f32)
        for r in ins[8:]:
            total = total + r[...].astype(f32)
        unit = h_ref[...] * i_ref[...]
        scaled = total * gain_ref[...]
        dh = e_ref[...].astype(f32) + i_ref[...] * (scaled - unit * jnp.mean(scaled * unit, axis=1, keepdims=True))
        dh_ref[...] = dh
        d = low(dh)
        low_ref[...] = d
        dz = 0.0
        for d_half, ref, core in zip(core_halves(low_ref, w, half), (m_ref, t_ref), (w[CORE], 1 - w[CORE])):
            own = own_ref[pl.ds(pl.multiple_of(core * half, 128), half), :]
            dz = dz + mm(d_half, jnp.concatenate([own, ref[...]], axis=1))
        mine_out[...] = low(dz[:, :own_slots])
        peer_out[...] = low(dz[:, own_slots:])

    whole = lambda i, w: (0, 0)
    mine = lambda i, w: (w[MEMBER], 0)
    return run(
        "close_feed_forward", body, where, (1,),
        [fixed(part), (hidden_row, (share, model), mine), (inverse, (share, 1), mine), fixed(gain),
         (cotangent, (share, model), lambda i, w: (w[ROW] * group + w[MEMBER], 0)),
         fixed(out_own), fixed(out_mine), fixed(out_theirs)] + [fixed(a) for a in got],
        [(shape((share, model), f32), (share, model), whole), (shape((share, model), bf16), (share, model), whole),
         (shape((share, own_slots), bf16), (share, own_slots), whole),
         (shape((share, filled - own_slots), bf16), (share, filled - own_slots), whole)],
        (), after, 2 * share * model * filled,
    )


def close_block(where, share, group, part, got, inputs, inverse, gain, dh, after=()):
    model = part.shape[1]
    step_rows = min(BLK, share)
    blocks = share // step_rows
    row_blocks = group * blocks

    def body(w, ins, outs, scratch):
        p_ref, x_ref, i_ref, gain_ref, dh_ref = ins[:5]
        total = p_ref[...].astype(f32)
        for r in ins[5:]:
            total = total + r[...].astype(f32)
        unit = x_ref[...].astype(f32) * i_ref[...]
        scaled = total * gain_ref[...]
        outs[0][...] = dh_ref[...] + i_ref[...] * (scaled - unit * jnp.mean(scaled * unit, axis=1, keepdims=True))

    tokens = lambda i, w: (i, 0)
    return run(
        "close_block", body, where, (blocks,),
        [(part, (step_rows, model), tokens),
         (inputs, (step_rows, model), lambda i, w: (w[ROW] * row_blocks + w[MEMBER] * blocks + i, 0)),
         (inverse, (step_rows, 1), lambda i, w: (w[MEMBER] * blocks + i, 0)), fixed(gain),
         (dh, (step_rows, model), tokens)] + [(a, (step_rows, model), tokens) for a in got],
        [(shape((share, model), f32), (step_rows, model), tokens)], (), after,
    )[0]


def collect(where, arrays, pieces, unit=1, after=()):
    count = arrays[0].shape[0] // pieces
    filled = sum(a.shape[1] for a in arrays)
    total = -(-filled // unit) * unit

    def body(w, ins, outs, scratch):
        at = 0
        for r in ins:
            n = r.shape[1]
            outs[0][:, at:at + n] = r[...]
            at += n
        if at < total:
            outs[0][:, at:] = jnp.zeros((count, total - at), bf16)

    return run(
        "collect", body, where, (1,),
        [(a, (count, a.shape[1]), lambda i, w: (w[PIECE], 0)) for a in arrays],
        [(shape((count, total), bf16), (count, total), lambda i, w: (0, 0))], (), after,
    )[0]


class Place:
    def __init__(self, rows):
        self.tensor = lax.axis_size("tensor")
        self.dp = lax.axis_size("dp")
        self.rows = rows
        self.group = self.tensor // rows
        self.at = lax.axis_index("tensor")
        self.dp_at = lax.axis_index("dp")
        self.bits = [1 << b for b in reversed(range(1, self.dp.bit_length() - 1))]

    def owner(self, at, step, turn):
        row, member = at // self.group, at % self.group
        return ((row + turn) % self.rows) * self.group + (member + step) % self.group

    def fetch(self, value, step, turn):
        pairs = [(self.owner(i, step, turn), i) for i in range(self.tensor)]
        return lax.ppermute(value, "tensor", pairs)

    def deliver(self, value, step, turn):
        pairs = [(i, self.owner(i, step, turn)) for i in range(self.tensor)]
        return lax.ppermute(value, "tensor", pairs)

    def swap(self, value, bit):
        return lax.ppermute(value, "dp", [(i, i ^ bit) for i in range(self.dp)])


class Chain:
    def __init__(self, where):
        self.where = where
        self.behind = ()

    def __call__(self, make, *args, extra=(), **keys):
        made = make(self.where, *args, after=self.behind + tuple(extra), **keys)
        outs = made if isinstance(made, (list, tuple)) else [made]
        self.behind = (min(outs, key=lambda a: a.size),)
        return made

    def sync(self, *values):
        out = lax.optimization_barrier((*values, *self.behind))
        self.behind = tuple(out[len(values):])
        return out[:len(values)]


def on_device(
    inputs, gain_attn, w_query, w_key, w_value, w_outgate, w_forget, forget_bias, w_out,
    gain_mlp, w_gate, w_up, w_down, segment_ids, cotangent,
):
    rows, length = segment_ids.shape
    here = Place(rows)
    group, pieces = here.group, here.dp
    heads, width, hidden = w_forget.shape[1], w_query.shape[1], w_gate.shape[1]
    model = inputs.shape[1]
    share = length // group
    row, member = here.at // group, here.at % group
    core, chip = here.dp_at % 2, here.dp_at // 2
    where = jnp.stack([row, member, core, chip, core * (pieces // 2) + chip]).astype(jnp.int32)
    go = Chain(where)
    gain_attn, gain_mlp = gain_attn[None], gain_mlp[None]
    segment = lax.dynamic_index_in_dim(segment_ids, row, 0, keepdims=False)
    scol, srow = segment[:, None], segment[None, :]
    turns = range(1, rows)
    slots = [(s, j) for s in range(group) for j in range(rows)]

    def to_member(value, step):
        return lax.ppermute(value, "tensor", [
            (i, (i // group) * group + (i % group + step) % group) for i in range(here.tensor)])

    class Gather:
        def __init__(self, piece):
            others = range(1, here.dp // 2)
            self.masks = [0] + sorted(others, key=lambda k: bin(k).count("1"))
            self.held = [piece] + [here.swap(piece, 2 * k) for k in self.masks[1:]]

        def wait(self):
            self.held[1:] = go.sync(*self.held[1:])

        def close(self):
            self.mine = go(assemble, self.held, self.masks)
            self.theirs = here.swap(self.mine, 1)
            return self.mine, self.theirs

    class Reduce:
        def __init__(self, send, keep, orders):
            self.parts = None
            self.keep, self.got, self.orders = keep, here.swap(send, 1), orders

        def hop(self):
            if self.parts is None:
                n = self.keep.shape[1]
                split = len(self.orders) if n % (128 * len(self.orders)) == 0 else 1
                entries = [(self.keep, self.got, list(here.bits), self.orders[c][0], c, n // split) for c in range(split)]
                orders = [order[1:] for order in self.orders[:split]]
            else:
                entries = [(kept, got, left, order[0], 0, kept.shape[1]) for kept, got, left, order in self.parts]
                orders = [order[1:] for _, _, _, order in self.parts]
            outs = go(fold, entries)
            self.parts = [
                [outs[2 * c + 1], here.swap(outs[2 * c], e[3]), [b for b in e[2] if b != e[3]], orders[c]]
                for c, e in enumerate(entries)
            ]

        def close(self):
            while self.parts is None or self.parts[0][3]:
                self.hop()
            sums = [kept.astype(f32) + got.astype(f32) for kept, got, _, _ in self.parts]
            return sums[0] if len(sums) == 1 else jnp.concatenate(sums, axis=1)

        def wait(self):
            got = go.sync(*([self.got] if self.parts is None else [p[1] for p in self.parts]))
            if self.parts is None:
                self.got = got[0]
            else:
                for p, g in zip(self.parts, got):
                    p[1] = g

    both_ways = [here.bits, here.bits[::-1]]

    attn_cut = [[w_query, w_key], [w_value, w_outgate, w_forget]]
    attn_counts = [sum(a.shape[1] for a in cut) for cut in attn_cut]
    attn_pieces = [go(collect, cut, pieces, 128) for cut in attn_cut]
    attn_got = [here.fetch(attn_pieces[0], 0, j) for j in turns]
    bias_got = [here.fetch(forget_bias, 0, j) for j in turns]
    own = go(project_own, length, inputs, gain_attn,
             [w_query, w_key, w_value, w_outgate, w_forget], forget_bias[None])
    normed, inverse_attn = own[:2]
    mixed = {0: own[2:]}
    gated = {}
    logs = {}

    def attend(j):
        q, k, v, g, _, _, crow = mixed[j]
        z, logs[j] = go(attend_forward, q, k, v, g, crow, scol, srow)
        gated[0, j] = z
        for s in range(1, group):
            gated[s, j] = here.fetch(z, s, 0)

    def wait_gated(j):
        arrived = go.sync(*[gated[s, j] for s in range(1, group)])
        for s in range(1, group):
            gated[s, j] = arrived[s - 1]

    arrived = go.sync(*attn_got, *bias_got, attn_pieces[1])
    attn_got, bias_got = arrived[:rows - 1], arrived[rows - 1:-1]
    attn_later = [here.fetch(arrived[-1], 0, j) for j in turns]
    attn_gather = [[Gather(p)] for p in attn_got]
    attend(0)
    for gathers, p in zip(attn_gather, go.sync(*attn_later)):
        gathers[0].wait()
        gathers.append(Gather(p))
    out_piece = go(collect, [w_out], pieces)
    attn_w = [[gathers[0].close()] for gathers in attn_gather]
    out_got = [here.fetch(out_piece, 0, j) for j in turns]
    gate_piece = go(collect, [w_gate, w_up], pieces)
    wait_gated(0)
    for gathers in attn_gather:
        gathers[1].wait()
    for done, gathers in zip(attn_w, attn_gather):
        done.append(gathers[1].close())
    out_got = go.sync(*out_got)
    out_own = jnp.concatenate([out_piece, *out_got], axis=1)
    out_peers = [here.fetch(out_own, s, 0) for s in range(1, group)]
    gate_piece = go.sync(gate_piece)[0]
    gate_got = [here.fetch(gate_piece, 0, j) for j in turns]
    for j in turns:
        mixed[j] = go(project_other, normed, attn_w[j - 1], attn_counts, width, heads, bias_got[j - 1][None])
    out_peers = go.sync(*out_peers)
    out_gather = Gather(jnp.concatenate([*out_got, *out_peers], axis=1))
    for j in turns:
        attend(j)
    out_gather.wait()
    out_mine, out_theirs = out_gather.close()
    gate_got = go.sync(*gate_got)
    gate_gather = [Gather(p) for p in gate_got]
    down_piece = go(collect, [w_down], pieces)
    for j in turns:
        wait_gated(j)
    down_piece, out_theirs = go.sync(down_piece, out_theirs)
    down_got = [here.fetch(down_piece, 0, j) for j in turns]
    hidden_row, mlp_normed, inverse_mlp = go(
        close_attention, length, inputs, [gated[slot] for slot in slots], w_out, out_mine, out_theirs, gain_mlp
    )
    for gather in gate_gather:
        gather.wait()
    down_got = go.sync(*down_got)
    down_gather = [Gather(p) for p in down_got]

    def ffn(weights, before, final):
        return go(feed_forward, mlp_normed, cotangent, weights, hidden, gain_mlp, group, pieces, before, final)

    wide = BLK if hidden % BLK == 0 else hidden
    mlp_sums = {}
    send, keep, *carried = ffn([w_gate, w_up, w_down], [], False)
    gate_w = [gather.close() for gather in gate_gather]
    down_w = [gather.close() for gather in down_gather]
    mlp_sums[0] = Reduce(send, keep, both_ways)
    mlp_w = {}
    for j in turns:
        mlp_w[j] = gate_w[j - 1] + down_w[j - 1]
        if j < rows - 1:
            send, keep, *carried = ffn(mlp_w[j], carried, False)
            mlp_sums[j] = Reduce(send, keep, both_ways)
    mlp_sums[0].hop()
    du, dw, m, *made = ffn(mlp_w[rows - 1], carried, True)
    peers = list(range(1, group))
    part, out_part_own, gain_mlp_part = made[group - 1], made[2 * group - 1], made[2 * group]
    out_send = made[group:2 * group - 1]
    got = [to_member(v, s) for v, s in zip(made, peers)]
    mlp_sums[0].hop()
    mlp_sums[rows - 1] = Reduce(*go(lambda w, after: weight_grads(
        "mlp_grads", w, [mlp_normed, cotangent], [(0, [du]), (0, [dw]), (1, [m])], pieces, row_of=(1,), mixed=wide, after=after)), both_ways)
    dh, dh_low, dz_mine, dz_peers = go(
        close_feed_forward, share, group, part, got, hidden_row, inverse_mlp, gain_mlp, cotangent,
        w_out, out_mine, out_theirs,
    )
    dz_parts = [dz_mine]
    own_slots = rows * width
    for s in peers:
        lo = (group - s - 1) * own_slots
        dz_parts.append(here.fetch(dz_peers if group == 2 else dz_peers[:, lo:lo + own_slots], s, 0))
    mlp_sums[0].wait()
    mlp_own = mlp_sums[0].close()
    for j in turns:
        mlp_sums[j].hop()
    out_sum = Reduce(*go(lambda w, after: weight_grads(
        "out_grads", w, [dh_low], [(0, [gated[slot] for slot in slots])], pieces, True, after=after)), both_ways)

    back = {}
    attn_sums = {}
    per_step = together(heads) * HEAD

    def attend_back(j):
        q, k, v, g, forget, ccol, _ = mixed[j]
        parts = [(d, j * width // per_step) for d in dz_parts]
        if width % 128:
            parts = [(a[:, o * per_step:(o + 1) * per_step], 0) for a, o in parts]
        back[j] = go(attend_backward, q, k, v, g, gated[0, j], parts, logs[j], ccol, forget, scol, srow)

    def attn_grads(j, orders):
        attn_sums[j] = Reduce(*go(lambda w, after: weight_grads(
            "attn_grads", w, [normed], [(0, back[j][:2]), (0, back[j][2:5])], pieces, after=after)), orders)

    arrived = go.sync(*dz_parts[1:], *out_send)
    dz_parts[1:], out_send = arrived[:group - 1], arrived[group - 1:]
    out_got = [to_member(v, s) for v, s in zip(out_send, peers)]
    for j in turns:
        attend_back(j)
        attn_grads(j, both_ways)
    for j in turns:
        mlp_sums[j].hop()
    out_sum.hop()
    out_got = go.sync(*out_got)
    for j in turns:
        attn_sums[j].hop()
    for j in turns:
        mlp_sums[j].wait()
    mlp_other = [here.deliver(low(mlp_sums[j].close()), 0, j) for j in turns]
    attend_back(0)
    out_sum.hop()
    for j in turns:
        attn_sums[j].hop()
    attn_grads(0, both_ways)
    own_w = [w_query, w_key, w_value, w_outgate, w_forget]
    pair_terms = [
        (list(back[j][lo:hi]), *attn_w[j - 1][k]) for j in turns for k, (lo, hi) in enumerate(((0, 2), (2, 5)))
    ]

    def attn_back(name, steps):
        outs = []
        for s in steps:
            outs.append(go(lambda w, after: back_rows(
                name, w, s, group, list(back[0][:5]), own_w, pair_terms, normed, gain_attn, after)))
        return [o[0] for o in outs] + [sum(o[1] for o in outs)]

    made = attn_back("attn_back_send", peers)
    got = [to_member(v, s) for v, s in zip(made, peers)]
    mlp_other = go.sync(*mlp_other)
    for j in turns:
        attn_sums[j].wait()
    attn_other = [here.deliver(low(attn_sums[j].close()), 0, j) for j in turns]
    out_sum.wait()
    attn_sums[0].hop()
    out_part = out_sum.close().reshape(-1, group, rows, width)
    out_part = go.sync(out_part)[0]
    out_turned = [here.deliver(low(out_part[:, :, j]).reshape(-1, group * width), 0, j) for j in turns]
    part, gained = attn_back("attn_back_own", [0])
    bias_full = jnp.zeros((here.tensor, heads), f32)
    for j in range(rows):
        bias_full = lax.dynamic_update_slice(bias_full, back[j][5], (here.owner(here.at, 0, j), 0))
    small = jnp.concatenate([made[-1] + gained, gain_mlp_part, bias_full.reshape(1, -1)], axis=1)
    small_hops = [lambda v, b=b: here.swap(v, b) for b in [1] + here.bits] + [
        lambda v, b=b: lax.ppermute(v, "tensor", [(i, i ^ b) for i in range(here.tensor)])
        for b in [1 << k for k in range(here.tensor.bit_length() - 1)]]
    flying = small_hops.pop(0)(small)

    def small_step():
        arrived = go.sync(flying)[0]
        total = small + arrived
        return total, (small_hops.pop(0)(total) if small_hops else None)

    attn_other = go.sync(*attn_other)
    attn_sums[0].hop()
    small, flying = small_step()
    out_own, *arrived = go.sync(out_part_own, *out_got)
    output = lax.dynamic_slice_in_dim(hidden_row, member * share, share, 0) + out_own.astype(f32)
    for v in arrived:
        output = output + v.astype(f32)
    out_turned = go.sync(*out_turned, output)
    output = out_turned[-1]
    out_part = out_part[:, :, 0].reshape(-1, group * width) + sum(v.astype(f32) for v in out_turned[:-1])
    grad_out = out_part[:, :width]
    out_rest = [here.deliver(low(out_part[:, s * width:(s + 1) * width]), s, 0) for s in peers]
    small, flying = small_step()
    mlp_own, *mlp_other = go.sync(mlp_own, *mlp_other)
    attn_sums[0].wait()
    attn = attn_sums[0].close()
    while flying is not None:
        small, flying = small_step()
    out_rest = go.sync(*out_rest)
    grad_inputs = go(close_block, share, group, part, got, inputs, inverse_attn, gain_attn, dh)
    mlp = mlp_own
    for v in mlp_other:
        mlp = mlp + v.astype(f32)

    def columns(kind):
        return jnp.concatenate([mlp[:, b + kind * wide:b + (kind + 1) * wide] for b in range(0, 3 * hidden, 3 * wide)], axis=1)

    for v in out_rest:
        grad_out = grad_out + v.astype(f32)
    for v in attn_other:
        attn = attn + v.astype(f32)
    bias_own = lax.dynamic_slice_in_dim(small[0, 2 * model:], here.at * heads, heads, 0)
    return (
        output,
        grad_inputs,
        small[0, :model],
        attn[:, :width],
        attn[:, width:2 * width],
        attn[:, 2 * width:3 * width],
        attn[:, 3 * width:4 * width],
        attn[:, 4 * width:4 * width + heads],
        bias_own,
        grad_out,
        small[0, model:2 * model],
        columns(0),
        columns(1),
        columns(2),
    )


def solution(mesh):
    placed = (
        P("dp", None), P(), P(None, "tensor"), P(None, "tensor"), P(None, "tensor"),
        P(None, "tensor"), P(None, "tensor"), P("tensor"), P(None, "tensor"), P(),
        P(None, "tensor"), P(None, "tensor"), P(None, "tensor"), P("dp", None), P("dp", None),
    )
    weight = P("dp", "tensor")
    tokens = P(("dp", "tensor"), None)
    return jax.shard_map(
        on_device,
        mesh=mesh,
        in_specs=placed,
        out_specs=(
            tokens, tokens, P(), weight, weight, weight, weight, weight, P("tensor"),
            weight, P(), weight, weight, weight,
        ),
        check_vma=False,
    )
```

```python
import jax
import jax.numpy as jnp
from jax import lax
from jax.sharding import PartitionSpec as P
from jax.experimental import pallas as pl
from jax.experimental.pallas import tpu as pltpu

LOG2E = 1.4426950408889634
LN2 = 0.6931471805599453
HEAD = 64
BLK = 256
EPS = 1e-06
STEP = 115 * 10 ** 9
ROW, MEMBER, CORE, CHIP, PIECE = 0, 1, 2, 3, 4
f32 = jnp.float32
bf16 = jnp.bfloat16


def last(a, b):
    return lax.dot_general(a, b, (((1,), (1,)), ((), ())), preferred_element_type=f32)


def first(a, b):
    return lax.dot_general(a, b, (((0,), (0,)), ((), ())), preferred_element_type=f32)


def mm(a, b):
    return jnp.dot(a, b, preferred_element_type=f32)


def low(values):
    return values.astype(bf16)


def shape(dims, dtype):
    return jax.ShapeDtypeStruct(dims, dtype)


def spec(block, at, mode=None):
    if block is None:
        return pl.BlockSpec(memory_space=pl.ANY)
    return pl.BlockSpec(block, at) if mode is None else pl.BlockSpec(block, at, pipeline_mode=mode)


def run(name, body, where, grid, ins, outs, scratch=(), after=(), flops=0, vmem=56):
    count, extra, made = len(ins), len(after), len(outs)

    def kernel(where_ref, *refs):
        body(where_ref, refs[:count], refs[count + extra:count + extra + made], refs[count + extra + made:])

    return pl.pallas_call(
        kernel,
        grid_spec=pltpu.PrefetchScalarGridSpec(
            num_scalar_prefetch=1,
            grid=grid,
            in_specs=[spec(*entry[1:]) for entry in ins] + [pl.BlockSpec(memory_space=pl.ANY)] * extra,
            out_specs=[spec(*entry[1:]) for entry in outs],
            scratch_shapes=list(scratch),
        ),
        out_shape=[entry[0] for entry in outs],
        compiler_params=pltpu.CompilerParams(vmem_limit_bytes=vmem << 20),
        cost_estimate=pl.CostEstimate(flops=STEP, bytes_accessed=1, transcendentals=0),
        name=name,
    )(where, *[entry[0] for entry in ins], *after)


class Part:
    def __init__(self, array, rows=None, row_at=None, cols=None, col_at=None, into=None):
        self.array = array
        self.rows = array.shape[0] if rows is None else rows
        self.cols = array.shape[1] if cols is None else cols
        self.row_at, self.col_at = row_at, col_at
        self.into = into

    def view(self, ref, w):
        if self.row_at is None and self.col_at is None:
            return ref
        row = 0 if self.row_at is None else pl.multiple_of(self.row_at(w), self.rows)
        col = 0 if self.col_at is None else pl.multiple_of(self.col_at(w), self.cols)
        return ref.at[pl.ds(row, self.rows), pl.ds(col, self.cols)]


def stream(name, body, where, parts, outs, scratch=(), after=(), buffers=()):
    count, extra, made = len(parts), len(after), len(outs)
    single = [p for p in parts if p.into is None]
    chunks = 16

    def kernel(w, *refs):
        sources = refs[:count]
        targets = refs[count + extra:count + extra + made]
        at = count + extra + made
        shared = refs[at:at + len(buffers)]
        at += len(buffers)
        alone = iter(refs[at:at + len(single)])
        held = [next(alone) if p.into is None else shared[p.into[0]].at[
            pl.ds(p.into[1](w) if callable(p.into[1]) else p.into[1], p.rows), pl.ds(p.into[2], p.cols)] for p in parts]
        at += len(single)
        ready = refs[at:at + made]
        in_sems, out_sems = refs[at + made:at + made + 2]
        rest = shared + refs[at + made + 2:]
        loads = []
        for k, part in enumerate(parts):
            copy = pltpu.make_async_copy(part.view(sources[k], w), held[k], in_sems.at[k])
            copy.start()
            loads.append(copy)
        waited = set()
        sent = []

        def get(k):
            if k not in waited:
                loads[k].wait()
                waited.add(k)
            return held[k]

        def put(k, row=None, rows=None, col=None, cols=None):
            spot = (pl.ds(0, outs[k].shape[0]) if row is None else pl.ds(row, rows),
                    pl.ds(0, outs[k].shape[1]) if col is None else pl.ds(col, cols))
            copy = pltpu.make_async_copy(ready[k].at[spot], targets[k].at[spot], out_sems.at[k, len([1 for i, _ in sent if i == k])])
            copy.start()
            sent.append((k, copy))

        body(w, get, ready, put, rest)
        for _, copy in sent:
            copy.wait()

    return pl.pallas_call(
        kernel,
        grid_spec=pltpu.PrefetchScalarGridSpec(
            num_scalar_prefetch=1, grid=(),
            in_specs=[pl.BlockSpec(memory_space=pl.ANY)] * (count + extra),
            out_specs=[pl.BlockSpec(memory_space=pl.ANY)] * made,
            scratch_shapes=[pltpu.VMEM(b, bf16) for b in buffers]
            + [pltpu.VMEM((p.rows, p.cols), p.array.dtype) for p in single]
            + [pltpu.VMEM(o.shape, o.dtype) for o in outs]
            + [pltpu.SemaphoreType.DMA((count,)), pltpu.SemaphoreType.DMA((made, chunks))] + list(scratch),
        ),
        out_shape=list(outs),
        compiler_params=pltpu.CompilerParams(vmem_limit_bytes=58 << 20),
        cost_estimate=pl.CostEstimate(flops=STEP, bytes_accessed=1, transcendentals=0),
        name=name,
    )(where, *[p.array for p in parts], *after)


def fixed(array):
    return (array, array.shape, lambda i, w: (0,) * array.ndim)


def fixed_out(dims, dtype):
    return (shape(dims, dtype), dims, lambda i, w: (0,) * len(dims))


def halves(values, pieces, core):
    count = values.shape[0] // pieces
    even = jnp.concatenate([values[p * count:(p + 1) * count] for p in range(0, pieces, 2)], axis=0)
    odd = jnp.concatenate([values[p * count:(p + 1) * count] for p in range(1, pieces, 2)], axis=0)
    return jnp.where(core == 0, odd, even), jnp.where(core == 0, even, odd)


def three(values):
    top = low(values)
    rest = values - top.astype(f32)
    middle = low(rest)
    return top, middle, low(rest - middle.astype(f32))


def log_keep(values):
    return jnp.minimum(values, 0.0) - jnp.log1p(jnp.exp(-jnp.abs(values)))


def lower(flip=False):
    r = lax.broadcasted_iota(jnp.int32, (BLK, BLK), 0)
    c = lax.broadcasted_iota(jnp.int32, (BLK, BLK), 1)
    return jnp.where(r <= c if flip else r >= c, 1.0, 0.0).astype(bf16)


TOK = 512


def project_tail(i, mixed, width, bias, outs, carry):
    q_ref, k_ref, v_ref, g_ref, f_ref, ccol_ref, crow_ref = outs
    q_ref[...] = low(mixed[:, :width] * (HEAD ** -0.5 * LOG2E))
    for p, ref in ((1, k_ref), (2, v_ref), (3, g_ref)):
        ref[...] = low(mixed[:, p * width:(p + 1) * width])
    heads = f_ref.shape[1]
    forget = mixed[:, 4 * width:4 * width + heads] + bias
    f_ref[...] = forget

    @pl.when(i == 0)
    def _():
        carry[...] = jnp.zeros_like(carry)

    mask = lower()
    hp = crow_ref.shape[1]
    tokens = forget.shape[0]
    for t in range(tokens // BLK):
        rows = slice(t * BLK, (t + 1) * BLK)
        wide = jnp.concatenate([log_keep(forget[rows]) * LOG2E, jnp.zeros((BLK, 128 - heads), f32)], axis=1)
        sums = sum(mm(mask, part) for part in three(wide)) + carry[0:1, :]
        carry[0:1, :] = sums[BLK - 1:BLK, :]
        ccol_ref[rows, :] = sums[:, :heads]
        flat = sums.T
        for s in range(crow_ref.shape[0]):
            crow_ref[s, :, rows] = flat[s * hp:(s + 1) * hp, :]


def together(heads):
    return 2 if heads % 2 == 0 else heads


def project_outs(length, width, heads):
    tokens = lambda i, w: (i, 0)
    return [(shape((length, width), bf16), (TOK, width), tokens) for _ in range(4)] + [
        (shape((length, heads), f32), (TOK, heads), tokens),
        (shape((length, heads), f32), (TOK, heads), tokens),
        (shape((heads // together(heads), together(heads), length), f32),
         (heads // together(heads), together(heads), TOK), lambda i, w: (0, 0, i)),
    ]


def project_own(where, length, inputs, gain, weights, bias, after=()):
    model = inputs.shape[1]
    width, heads = weights[0].shape[1], weights[4].shape[1]

    def body(w, ins, outs, scratch):
        x_ref, gain_ref, wq, wk, wv, wg, wf, b_ref = ins
        a_ref, inv_ref = outs[:2]
        x = x_ref[...].astype(f32)
        inverse = lax.rsqrt(jnp.mean(x * x, axis=1, keepdims=True) + EPS)
        a = low(x * inverse * gain_ref[...])
        a_ref[...] = a
        inv_ref[...] = inverse
        mixed = mm(a, jnp.concatenate([r[...] for r in (wq, wk, wv, wg, wf)], axis=1))
        project_tail(pl.program_id(0), mixed, width, b_ref[...], outs[2:], scratch[0])

    blocks = length // TOK
    tokens = lambda i, w: (i, 0)
    return run(
        "project_own", body, where, (blocks,),
        [(inputs, (TOK, model), lambda i, w: (w[ROW] * blocks + i, 0)), fixed(gain)]
        + [fixed(a) for a in weights] + [fixed(bias)],
        [(shape((length, model), bf16), (TOK, model), tokens), (shape((length, 1), f32), (TOK, 1), tokens)]
        + project_outs(length, width, heads),
        [pltpu.VMEM((8, 128), f32)], after, 2 * length * model * (4 * width + heads),
    )


def core_halves(ref, w, half):
    return (ref[:, pl.ds(pl.multiple_of(w[CORE] * half, 128), half)],
            ref[:, pl.ds(pl.multiple_of((1 - w[CORE]) * half, 128), half)])


def project_other(where, normed, gathered, counts, width, heads, bias, after=()):
    length, model = normed.shape
    half = model // 2

    def body(w, ins, outs, scratch):
        a_ref, b_ref = ins[:2]
        am, at = core_halves(a_ref, w, half)
        mixed = [mm(am, ins[2 + 2 * k][:, :n]) + mm(at, ins[3 + 2 * k][:, :n]) for k, n in enumerate(counts)]
        project_tail(pl.program_id(0), jnp.concatenate(mixed, axis=1), width, b_ref[...], outs, scratch[0])

    return run(
        "project_other", body, where, (length // TOK,),
        [(normed, (TOK, model), lambda i, w: (i, 0)), fixed(bias)] + [fixed(a) for pair in gathered for a in pair],
        project_outs(length, width, heads),
        [pltpu.VMEM((8, 128), f32)], after, 2 * length * model * (4 * width + heads),
    )


def attend_forward(where, q, k, v, g, crow, scol, srow, after=()):
    length, n = q.shape
    heads = n // HEAD
    hp = together(heads)
    width = hp * HEAD

    def body(w, ins, outs, scratch):
        q_ref, k_ref, v_ref, g_ref, crow_ref, scol_ref, srow_ref = ins
        z_ref, lse_ref = outs
        lane = lax.broadcasted_iota(jnp.int32, (1, width), 1) // HEAD
        lane1 = lax.broadcasted_iota(jnp.int32, (BLK, 128), 1)
        tri = lax.broadcasted_iota(jnp.int32, (BLK, BLK), 0) >= lax.broadcasted_iota(jnp.int32, (BLK, BLK), 1)
        crows = crow_ref[0]
        v_wide = jnp.concatenate([v_ref[...], jnp.ones((length, 128), bf16)], axis=1)
        for i in range(length // BLK):
            rows = pl.ds(i * BLK, BLK)
            reach = (i + 1) * BLK
            q = q_ref[rows, :]
            same = scol_ref[rows, :] == srow_ref[:, :reach]
            if i:
                allowed = jnp.concatenate([same[:, :reach - BLK], same[:, reach - BLK:] & tri], axis=1)
            else:
                allowed = same & tri
            scores = last(jnp.concatenate([jnp.where(lane == h, q, 0) for h in range(hp)], axis=0), k_ref[:reach, :])
            tops, grown = [], []
            for h in range(hp):
                s = jnp.where(allowed, scores[h * BLK:(h + 1) * BLK] - crows[h:h + 1, :reach], -1e30)
                top = jnp.max(s, axis=1, keepdims=True)
                tops.append(top)
                grown.append(low(jnp.exp2(s - top)))
            parts = mm(jnp.concatenate(grown, axis=0), v_wide[:reach, :])
            out = jnp.zeros((BLK, width), f32)
            stats = jnp.zeros((BLK, 128), f32)
            for h in range(hp):
                part = parts[h * BLK:(h + 1) * BLK]
                total = part[:, width:width + 1]
                out = jnp.where(lane == h, part[:, :width] * (1.0 / total), out)
                stats = jnp.where(lane1 == h, tops[h] + jnp.log2(total), stats)
            z_ref[rows, :] = low(out * jax.nn.sigmoid(g_ref[rows, :].astype(f32)))
            lse_ref[0, :, i * BLK:(i + 1) * BLK] = stats.T[:hp, :]

    tokens = lambda i, w: (0, i)
    return run(
        "attend_forward", body, where, (heads // hp,),
        [(a, (length, width), tokens) for a in (q, k, v, g)]
        + [(crow, (1, hp, length), lambda i, w: (i, 0, 0)), fixed(scol), fixed(srow)],
        [(shape((length, n), bf16), (length, width), tokens),
         (shape((heads // hp, hp, length), f32), (1, hp, length), lambda i, w: (i, 0, 0))],
        (), after, heads * length * length * 1100,
    )


def attend_backward(where, q, k, v, g, z, dz_parts, lse, ccol, forget, scol, srow, after=()):
    length, n = q.shape
    heads = n // HEAD
    hp = together(heads)
    width = hp * HEAD
    steps = heads // hp
    group = len(dz_parts)
    share = length // group

    def body(w, ins, outs, scratch):
        q_ref, k_ref, v_ref, g_ref, z_ref = ins[:5]
        dz_refs = ins[5:5 + group]
        lse_ref, ccol_ref, f_ref, scol_ref, srow_ref = ins[5 + group:]
        dq_ref, dk_ref, dv_ref, dg_ref, df_ref, db_ref = outs
        dqacc, rates, dzfull = scratch
        step = pl.program_id(0)
        lane = lax.broadcasted_iota(jnp.int32, (1, width), 1) // HEAD
        lane1 = lax.broadcasted_iota(jnp.int32, (1, 128), 1)
        tri = lax.broadcasted_iota(jnp.int32, (BLK, BLK), 1) >= lax.broadcasted_iota(jnp.int32, (BLK, BLK), 0)
        blocks = length // BLK

        @pl.when(step == 0)
        def _():
            rates[...] = jnp.zeros_like(rates)

        for s in range(group):
            at = lax.rem(w[MEMBER] + s, group) * share
            dzfull[pl.ds(pl.multiple_of(at, share), share), :] = dz_refs[s][...]
        sig = jax.nn.sigmoid(g_ref[...].astype(f32))
        dz = dzfull[...].astype(f32)
        prod = dz * z_ref[...].astype(f32)
        dout = low(dz * sig)
        dg_ref[...] = low(prod * (1.0 - sig))
        prod_hi = low(prod)
        prod_lo = low(prod - prod_hi.astype(f32))
        lses = lse_ref[0]
        chosen = lax.broadcasted_iota(jnp.int32, (8, width), 0) == lax.broadcasted_iota(jnp.int32, (8, width), 1) // HEAD
        chosen = jnp.where(chosen, 1.0, 0.0).astype(bf16)
        centres = last(chosen, prod_hi) + last(chosen, prod_lo)
        ones = jnp.ones((length, 128), bf16)
        q_wide = jnp.concatenate([q_ref[...], ones], axis=1)
        k_wide = jnp.concatenate([k_ref[...], ones], axis=1)
        decays = [
            jnp.sum(jnp.where(lane1[:, :heads] == step * hp + h, ccol_ref[...], 0.0), axis=1, keepdims=True)
            for h in range(hp)
        ]
        dqacc[...] = jnp.zeros_like(dqacc)
        for j in range(blocks):
            keys = pl.ds(j * BLK, BLK)
            lo = j * BLK
            count = length - lo
            keyed = lambda ref: jnp.concatenate([jnp.where(lane == h, ref[keys, :], 0) for h in range(hp)], axis=0)
            scores = last(keyed(k_ref), q_ref[lo:, :])
            dps = last(keyed(v_ref), dout[lo:, :])
            same = scol_ref[keys, :] == srow_ref[:, lo:]
            if j < blocks - 1:
                allowed = jnp.concatenate([same[:, :BLK] & tri, same[:, BLK:]], axis=1)
            else:
                allowed = same & tri
            ps, dss = [], []
            for h in range(hp):
                rows = slice(h * BLK, (h + 1) * BLK)
                s = scores[rows] - decays[h][lo:lo + BLK, :] - lses[h:h + 1, lo:]
                p = jnp.exp2(jnp.where(allowed, s, -1e30))
                ps.append(low(p))
                dss.append(low(p * (dps[rows] - centres[h:h + 1, lo:])))
            dvs = mm(jnp.concatenate(ps, axis=0), dout[lo:, :])
            dks = mm(jnp.concatenate(dss, axis=0), q_wide[lo:, :])
            dqs = first(jnp.concatenate(dss, axis=1), k_wide[lo:lo + BLK, :])
            dk = jnp.zeros((BLK, width), f32)
            dv = jnp.zeros((BLK, width), f32)
            for h in range(hp):
                rows = slice(h * BLK, (h + 1) * BLK)
                dk = jnp.where(lane == h, dks[rows, :width], dk)
                dv = jnp.where(lane == h, dvs[rows], dv)
                rates[keys, :] = jnp.where(lane1 == step * hp + h, -dks[rows, width:width + 1], rates[keys, :])
                dqacc[h * length + lo:(h + 1) * length, :] += dqs[h * count:(h + 1) * count]
            dk_ref[keys, :] = low(dk * LN2)
            dv_ref[keys, :] = low(dv)
        dq = jnp.zeros((length, width), f32)
        for h in range(hp):
            part = dqacc[h * length:(h + 1) * length, :]
            dq = jnp.where(lane == h, part[:, :width], dq)
            rates[...] = jnp.where(lane1 == step * hp + h, rates[...] + part[:, width:width + 1], rates[...])
        dq_ref[...] = low(dq * HEAD ** -0.5)

        @pl.when(step == steps - 1)
        def _():
            mask = lower(True)
            carry = jnp.zeros((1, 128), f32)
            bias = jnp.zeros((1, heads), f32)
            for b in reversed(range(blocks)):
                rows = pl.ds(b * BLK, BLK)
                sums = sum(mm(mask, part) for part in three(rates[rows, :])) + carry
                carry = sums[0:1, :]
                df = low(sums[:, :heads] * jax.nn.sigmoid(-f_ref[rows, :]))
                df_ref[rows, :] = df
                bias = bias + jnp.sum(df.astype(f32), axis=0, keepdims=True)
            db_ref[...] = bias

    tokens = lambda i, w: (0, i)
    wide = (shape((length, n), bf16), (length, width), tokens)
    return run(
        "attend_backward", body, where, (steps,),
        [(a, (length, width), tokens) for a in (q, k, v, g, z)]
        + [(a, (share, width), lambda i, w, off=off: (0, off + i)) for a, off in dz_parts]
        + [(lse, (1, hp, length), lambda i, w: (i, 0, 0))] + [fixed(a) for a in (ccol, forget, scol, srow)],
        [wide] * 4 + [fixed_out((length, heads), bf16), fixed_out((1, heads), f32)],
        [pltpu.VMEM((hp * length, width + 128), f32), pltpu.VMEM((length, 128), f32), pltpu.VMEM((length, width), bf16)],
        after, heads * length * length * 1500,
    )


def close_attention(where, length, inputs, gated, out_own, out_mine, out_theirs, gain, after=()):
    model = inputs.shape[1]
    half = model // 2
    width = out_own.shape[1]

    def body(w, ins, outs, scratch):
        x_ref, own_ref, m_ref, t_ref, gain_ref = ins[:5]
        z = jnp.concatenate([r[...] for r in ins[5:]], axis=1)
        h_ref, a_ref, inv_ref = outs
        for ref, core in ((m_ref, w[CORE]), (t_ref, 1 - w[CORE])):
            at = pl.ds(pl.multiple_of(core * half, 128), half)
            own = own_ref[pl.ds(pl.multiple_of(core * half, 128), half), :]
            rest = ref[:, :(len(gated) - 1) * width]
            h_ref[:, at] = x_ref[:, at].astype(f32) + last(z, jnp.concatenate([own, rest], axis=1))
        h = h_ref[...]
        inverse = lax.rsqrt(jnp.mean(h * h, axis=1, keepdims=True) + EPS)
        a = low(h * inverse * gain_ref[...])
        a_ref[...] = a
        inv_ref[...] = inverse

    blocks = length // TOK
    tokens = lambda i, w: (i, 0)
    return run(
        "close_attention", body, where, (blocks,),
        [(inputs, (TOK, model), lambda i, w: (w[ROW] * blocks + i, 0))]
        + [fixed(a) for a in (out_own, out_mine, out_theirs, gain)]
        + [(z, (TOK, width), tokens) for z in gated],
        [(shape((length, model), f32), (TOK, model), tokens), (shape((length, model), bf16), (TOK, model), tokens),
         (shape((length, 1), f32), (TOK, 1), tokens)],
        (), after, 2 * length * model * width * len(gated),
    )


def once(array_or_shape, block, at):
    return (array_or_shape, block, at, pl.Buffered(1))


def feed_forward(where, normed, cotangent, weights, hidden, gain, group, pieces, before, final, after=()):
    length, model = normed.shape
    half = model // 2
    share = length // group
    wide = BLK if hidden % BLK == 0 else hidden
    steps = hidden // wide
    own = len(weights) == 3
    tokens = length // TOK

    def body(w, ins, outs, scratch):
        a_ref, e_ref, gain_ref = ins[:3]
        blocks = ins[3:3 + (3 if own else 6)]
        rest = ins[3 + len(blocks):]
        back, out = scratch[:2]
        kept = scratch[2:5]
        step = pl.program_id(0)
        core = pl.ds(pl.multiple_of(w[CORE] * half, 128), half)
        other = pl.ds(pl.multiple_of((1 - w[CORE]) * half, 128), half)
        copies = [pltpu.make_async_copy(r, scratch[5 + k], scratch[5 + len(rest)].at[k]) for k, r in enumerate(rest)]

        @pl.when(step == 0)
        def _():
            for c in copies:
                c.start()
            back[...] = jnp.zeros_like(back)
            out[...] = jnp.zeros_like(out)

        for t in range(tokens):
            rows = pl.ds(t * TOK, TOK)
            if own:
                gate, up = mm(a_ref[rows, :], blocks[0][...]), mm(a_ref[rows, :], blocks[1][...])
                dm = mm(e_ref[rows, :], blocks[2][...])
            else:
                both = lambda ref, p: mm(ref[rows, core], blocks[p][...]) + mm(ref[rows, other], blocks[3 + p][...])
                gate, up, dm = both(a_ref, 0), both(a_ref, 1), both(e_ref, 2)
            sig = jax.nn.sigmoid(gate)
            act = gate * sig
            values = (low(dm * up * (sig * (1.0 + gate * (1.0 - sig)))), low(dm * act), low(act * up))
            for k, value in enumerate(values):
                kept[k][rows, :] = value
                if final:
                    outs[k][rows, :] = value
        du, dw, m = kept
        if own:
            back[...] += last(du[...], blocks[0][...]) + last(dw[...], blocks[1][...])
            out[...] += last(m[...], blocks[2][...])
        else:
            for where_to, p in ((core, 0), (other, 3)):
                back[:, where_to] += last(du[...], blocks[p][...]) + last(dw[...], blocks[p + 1][...])
                out[:, where_to] += last(m[...], blocks[p + 2][...])
        if not final:
            for k, left in enumerate((a_ref, a_ref, e_ref)):
                send, keep = halves(low(first(left[...], kept[k][...])), pieces, w[CORE])
                outs[0][:, k * wide:(k + 1) * wide] = send
                outs[1][:, k * wide:(k + 1) * wide] = keep

        @pl.when(step == steps - 1)
        def _():
            for c in copies:
                c.wait()
            if rest:
                back[...] += scratch[5][...].astype(f32)
                out[...] += scratch[6][...].astype(f32)
            if final:
                for k in range(group):
                    member = lax.rem(w[MEMBER] + (k + 1) % group, group)
                    rows = pl.ds(pl.multiple_of(member * share, share), share)
                    outs[3 + k][...] = low(back[rows, :])
                    outs[3 + group + k][...] = low(out[rows, :])
                outs[3 + 2 * group][...] = jnp.sum(back[...] * a_ref[...].astype(f32), axis=0, keepdims=True) / gain_ref[...]
            else:
                outs[2][...] = low(back[...])
                outs[3][...] = low(out[...])

    whole = lambda i, w: (0, 0)
    column = lambda i, w: (0, i)
    if own:
        parts = [(a, (model, wide), column) for a in weights]
    else:
        gm, gt, dm, dt = weights
        parts = [(a, (half, wide), lambda i, w, p=p: (0, p * steps + i))
                 for a, p in ((gm, 0), (gm, 1), (dm, 0), (gt, 0), (gt, 1), (dt, 0))]
    row_sum = once(shape((length, model), bf16), (length, model), whole)
    if final:
        outs = [(shape((length, hidden), bf16), (length, wide), column)] * 3
        outs += [once(shape((share, model), bf16), (share, model), whole)] * (2 * group)
        outs += [fixed_out((1, model), f32)]
    else:
        side = (shape((half, 3 * hidden), bf16), (half, 3 * wide), column)
        outs = [side, side, row_sum, row_sum]
    return run(
        "feed_forward", body, where, (steps,),
        [once(normed, (length, model), whole), once(cotangent, (length, model), lambda i, w: (w[ROW], 0)), fixed(gain)] + parts
        + [(a, None, None) for a in before],
        outs,
        [pltpu.VMEM((length, model), f32)] * 2 + [pltpu.VMEM((length, wide), bf16)] * 3
        + [pltpu.VMEM((length, model), bf16) for _ in before]
        + ([pltpu.SemaphoreType.DMA((len(before),))] if before else []),
        after,
    )


def weight_grads(name, where, lefts, groups, pieces, rows_of=False, row_of=(), mixed=0, after=()):
    length = groups[0][1][0].shape[0] if not rows_of else lefts[0].shape[0]
    half = lefts[0].shape[1] // 2
    widths = [sum(r.shape[1] for r in rights) for _, rights in groups]
    padded = [-(-n // 128) * 128 for n in widths]
    padded[-1] += -sum(padded) % 256
    parts, plan, loaded = [], [], {}
    row_at = (lambda w: w[MEMBER] * length) if rows_of else None
    for k, (s, rights) in enumerate(groups):
        if s not in loaded:
            loaded[s] = len(parts)
            parts.append(Part(lefts[s], length, (lambda w: w[ROW] * length) if s in row_of else None))
        at = []
        for r in rights:
            at.append(len(parts))
            parts.append(Part(r, length, row_at, r.shape[1]))
        plan.append((loaded[s], at, sum(padded[:k]), widths[k], padded[k]))

    def body(w, get, ready, put, rest):
        for k, (left, at, col, n, full) in enumerate(plan):
            left = get(left)[...]
            right = [get(k)[...] for k in at]
            value = low(first(left, right[0] if len(right) == 1 else jnp.concatenate(right, axis=1)))
            for which, part in enumerate(halves(value, pieces, w[CORE])):
                if mixed:
                    for b in range(n // mixed):
                        spot = (b * len(plan) + k) * mixed
                        ready[which][:, spot:spot + mixed] = part[:, b * mixed:(b + 1) * mixed]
                        put(which, col=spot, cols=mixed)
                    continue
                ready[which][:, col:col + n] = part
                if n < full:
                    ready[which][:, col + n:col + full] = jnp.zeros((half, full - n), bf16)
                put(which, col=col, cols=full)

    return stream(name, body, where, parts, [shape((half, sum(padded)), bf16)] * 2, (), after)


def fold(where, entries, after=()):
    keep, _, bits, _, _, width = entries[0]
    rows = keep.shape[0]
    count = len(bits)
    pieces = 1 << count
    piece = rows // pieces
    wide = next(n for n in (768, 512, 384, width) if width % n == 0)
    across = width // wide
    block = (piece, wide)
    ins, outs = [], []
    for keep, got, bits, bit_at, col, _ in entries:
        place = count - 1 - bits.index(bit_at)

        def index(mine, place=place, bit_at=bit_at, col=col):
            def at(i, c, w):
                own = lax.rem(w[CHIP] // (bit_at >> 1), 2)
                bit = own if mine else 1 - own
                low_part = lax.rem(i, 1 << place)
                high = i // (1 << place)
                return ((high * 2 + bit) * (1 << place) + low_part, col * across + c)
            return at

        for mine in (False, True):
            ins += [(keep, block, index(mine)), (got, block, index(mine))]
            outs.append((shape((rows // 2, width), bf16), block, lambda i, c, w: (i, c)))

    def body(w, ins_, outs_, scratch):
        for k, out in enumerate(outs_):
            out[...] = ins_[2 * k][...] + ins_[2 * k + 1][...]

    return run("fold", body, where, (pieces // 2, across), ins, outs, (), after, 10 ** 9)


def assemble(where, pieces, masks, after=()):
    count, extra = len(pieces), len(after)
    rows, width = pieces[0].shape

    def kernel(w, *refs):
        out, sems = refs[count + extra], refs[count + extra + 1]
        copies = []
        for k in range(count):
            at = pl.multiple_of(jnp.bitwise_xor(w[CHIP], masks[k]) * rows, rows)
            copies.append(pltpu.make_async_copy(refs[k], out.at[pl.ds(at, rows), :], sems.at[k]))
        for c in copies:
            c.start()
        for c in copies:
            c.wait()

    return pl.pallas_call(
        kernel,
        grid_spec=pltpu.PrefetchScalarGridSpec(
            num_scalar_prefetch=1, grid=(1,),
            in_specs=[pl.BlockSpec(memory_space=pl.ANY)] * (count + extra),
            out_specs=pl.BlockSpec((count * rows, width), lambda i, w: (0, 0)),
            scratch_shapes=[pltpu.SemaphoreType.DMA((count,))],
        ),
        out_shape=shape((count * rows, width), bf16),
        compiler_params=pltpu.CompilerParams(vmem_limit_bytes=56 << 20),
        cost_estimate=pl.CostEstimate(flops=STEP, bytes_accessed=1, transcendentals=0),
        name="assemble",
    )(where, *pieces, *after)


def back_rows(name, where, step, group, own_x, own_w, pair_terms, normed, gain, after=()):
    length, model = normed.shape
    half = model // 2
    share = length // group
    member = lambda w: lax.rem(w[MEMBER] + step, group)
    row_at = lambda w: member(w) * share
    parts, tails, cuts = [], [], []
    col = 0

    def lay(arrays, buffer, narrow):
        at = col
        for a in arrays:
            n = a.shape[1]
            rows, pick = (share, row_at) if buffer == 0 else (a.shape[0], None)
            if n % 128 == 0 and at % 128 == 0:
                parts.append(Part(a, rows, pick, n, None, (buffer, 0, at)))
            else:
                tails.append((len(parts), buffer, at, n))
                parts.append(Part(a, rows, pick, n))
            at += n
        return at

    if any(a.shape[1] % 128 for a in own_x[:-1]):
        own_x, own_w = [jnp.concatenate(own_x, axis=1)], [jnp.concatenate(own_w, axis=1)]
        pair_terms = [([jnp.concatenate(xs, axis=1)], mine, theirs) for xs, mine, theirs in pair_terms]
    lay(own_x, 0, True)
    end = lay(own_w, 1, True)
    full = -(-end // 128) * 128
    cuts.append((0, len(parts), 0, full))
    col = full
    for xs, mine, theirs in pair_terms:
        first_part = len(parts)
        lay(xs, 0, True)
        n = mine.shape[1]
        parts.append(Part(mine, into=(1, lambda w: pl.multiple_of(w[CORE] * half, half), col)))
        parts.append(Part(theirs, into=(1, lambda w: pl.multiple_of((1 - w[CORE]) * half, half), col)))
        cuts.append((first_part, len(parts), col, n))
        col += n
    unit_at = len(parts)
    parts.append(Part(normed, share, row_at))
    parts.append(Part(gain))

    def body(w, get, ready, put, rest):
        x_all, w_all = rest[:2]
        for low_part, high_part, at, n in cuts:
            for k in range(low_part, high_part):
                get(k)
            for k, buffer, spot, count in tails:
                if low_part <= k < high_part:
                    target = (x_all, w_all)[buffer]
                    last_col = at + n if spot + count <= at + n else spot + count
                    value = get(k)[...]
                    fill = jnp.zeros((value.shape[0], last_col - spot - count), bf16)
                    target[:, spot:last_col] = jnp.concatenate([value, fill], axis=1) if last_col > spot + count else value
            part = last(x_all[:, at:at + n], w_all[:, at:at + n])
            rest[2][...] = part if at == 0 else rest[2][...] + part
        total = rest[2][...]
        ready[0][...] = low(total)
        put(0)
        u = get(unit_at)[...].astype(f32)
        ready[1][...] = jnp.sum(total * u, axis=0, keepdims=True) / get(unit_at + 1)[...]
        put(1)

    return stream(
        name, body, where, parts, [shape((share, model), bf16), shape((1, model), f32)],
        [pltpu.VMEM((share, model), f32)], after, [(share, col), (model, col)],
    )


def close_feed_forward(where, share, group, part, got, hidden_row, inverse, gain, cotangent,
                       out_own, out_mine, out_theirs, after=()):
    model = part.shape[1]
    half = model // 2
    width = out_own.shape[1]
    filled = width + out_mine.shape[1]
    own_slots = filled // group

    def body(w, ins, outs, scratch):
        p_ref, h_ref, i_ref, gain_ref, e_ref, own_ref, m_ref, t_ref = ins[:8]
        dh_ref, low_ref, mine_out, peer_out = outs
        total = p_ref[...].astype(f32)
        for r in ins[8:]:
            total = total + r[...].astype(f32)
        unit = h_ref[...] * i_ref[...]
        scaled = total * gain_ref[...]
        dh = e_ref[...].astype(f32) + i_ref[...] * (scaled - unit * jnp.mean(scaled * unit, axis=1, keepdims=True))
        dh_ref[...] = dh
        d = low(dh)
        low_ref[...] = d
        dz = 0.0
        for d_half, ref, core in zip(core_halves(low_ref, w, half), (m_ref, t_ref), (w[CORE], 1 - w[CORE])):
            own = own_ref[pl.ds(pl.multiple_of(core * half, 128), half), :]
            dz = dz + mm(d_half, jnp.concatenate([own, ref[...]], axis=1))
        mine_out[...] = low(dz[:, :own_slots])
        peer_out[...] = low(dz[:, own_slots:])

    whole = lambda i, w: (0, 0)
    mine = lambda i, w: (w[MEMBER], 0)
    return run(
        "close_feed_forward", body, where, (1,),
        [fixed(part), (hidden_row, (share, model), mine), (inverse, (share, 1), mine), fixed(gain),
         (cotangent, (share, model), lambda i, w: (w[ROW] * group + w[MEMBER], 0)),
         fixed(out_own), fixed(out_mine), fixed(out_theirs)] + [fixed(a) for a in got],
        [(shape((share, model), f32), (share, model), whole), (shape((share, model), bf16), (share, model), whole),
         (shape((share, own_slots), bf16), (share, own_slots), whole),
         (shape((share, filled - own_slots), bf16), (share, filled - own_slots), whole)],
        (), after, 2 * share * model * filled,
    )


def close_block(where, share, group, part, got, inputs, inverse, gain, dh, after=()):
    model = part.shape[1]
    step_rows = min(BLK, share)
    blocks = share // step_rows
    row_blocks = group * blocks

    def body(w, ins, outs, scratch):
        p_ref, x_ref, i_ref, gain_ref, dh_ref = ins[:5]
        total = p_ref[...].astype(f32)
        for r in ins[5:]:
            total = total + r[...].astype(f32)
        unit = x_ref[...].astype(f32) * i_ref[...]
        scaled = total * gain_ref[...]
        outs[0][...] = dh_ref[...] + i_ref[...] * (scaled - unit * jnp.mean(scaled * unit, axis=1, keepdims=True))

    tokens = lambda i, w: (i, 0)
    return run(
        "close_block", body, where, (blocks,),
        [(part, (step_rows, model), tokens),
         (inputs, (step_rows, model), lambda i, w: (w[ROW] * row_blocks + w[MEMBER] * blocks + i, 0)),
         (inverse, (step_rows, 1), lambda i, w: (w[MEMBER] * blocks + i, 0)), fixed(gain),
         (dh, (step_rows, model), tokens)] + [(a, (step_rows, model), tokens) for a in got],
        [(shape((share, model), f32), (step_rows, model), tokens)], (), after,
    )[0]


def collect(where, arrays, pieces, unit=1, after=()):
    count = arrays[0].shape[0] // pieces
    filled = sum(a.shape[1] for a in arrays)
    total = -(-filled // unit) * unit

    def body(w, ins, outs, scratch):
        at = 0
        for r in ins:
            n = r.shape[1]
            outs[0][:, at:at + n] = r[...]
            at += n
        if at < total:
            outs[0][:, at:] = jnp.zeros((count, total - at), bf16)

    return run(
        "collect", body, where, (1,),
        [(a, (count, a.shape[1]), lambda i, w: (w[PIECE], 0)) for a in arrays],
        [(shape((count, total), bf16), (count, total), lambda i, w: (0, 0))], (), after,
    )[0]


class Place:
    def __init__(self, rows):
        self.tensor = lax.axis_size("tensor")
        self.dp = lax.axis_size("dp")
        self.rows = rows
        self.group = self.tensor // rows
        self.at = lax.axis_index("tensor")
        self.dp_at = lax.axis_index("dp")
        self.bits = [1 << b for b in reversed(range(1, self.dp.bit_length() - 1))]

    def owner(self, at, step, turn):
        row, member = at // self.group, at % self.group
        return ((row + turn) % self.rows) * self.group + (member + step) % self.group

    def fetch(self, value, step, turn):
        pairs = [(self.owner(i, step, turn), i) for i in range(self.tensor)]
        return lax.ppermute(value, "tensor", pairs)

    def deliver(self, value, step, turn):
        pairs = [(i, self.owner(i, step, turn)) for i in range(self.tensor)]
        return lax.ppermute(value, "tensor", pairs)

    def swap(self, value, bit):
        return lax.ppermute(value, "dp", [(i, i ^ bit) for i in range(self.dp)])


class Chain:
    def __init__(self, where):
        self.where = where
        self.behind = ()

    def __call__(self, make, *args, extra=(), **keys):
        made = make(self.where, *args, after=self.behind + tuple(extra), **keys)
        outs = made if isinstance(made, (list, tuple)) else [made]
        self.behind = (min(outs, key=lambda a: a.size),)
        return made

    def sync(self, *values):
        out = lax.optimization_barrier((*values, *self.behind))
        self.behind = tuple(out[len(values):])
        return out[:len(values)]


def on_device(
    inputs, gain_attn, w_query, w_key, w_value, w_outgate, w_forget, forget_bias, w_out,
    gain_mlp, w_gate, w_up, w_down, segment_ids, cotangent,
):
    rows, length = segment_ids.shape
    here = Place(rows)
    group, pieces = here.group, here.dp
    heads, width, hidden = w_forget.shape[1], w_query.shape[1], w_gate.shape[1]
    model = inputs.shape[1]
    share = length // group
    row, member = here.at // group, here.at % group
    core, chip = here.dp_at % 2, here.dp_at // 2
    where = jnp.stack([row, member, core, chip, core * (pieces // 2) + chip]).astype(jnp.int32)
    go = Chain(where)
    gain_attn, gain_mlp = gain_attn[None], gain_mlp[None]
    segment = lax.dynamic_index_in_dim(segment_ids, row, 0, keepdims=False)
    scol, srow = segment[:, None], segment[None, :]
    turns = range(1, rows)
    slots = [(s, j) for s in range(group) for j in range(rows)]

    def to_member(value, step):
        return lax.ppermute(value, "tensor", [
            (i, (i // group) * group + (i % group + step) % group) for i in range(here.tensor)])

    class Gather:
        def __init__(self, piece):
            others = range(1, here.dp // 2)
            self.masks = [0] + sorted(others, key=lambda k: bin(k).count("1"))
            self.held = [piece] + [here.swap(piece, 2 * k) for k in self.masks[1:]]

        def wait(self):
            self.held[1:] = go.sync(*self.held[1:])

        def close(self):
            self.mine = go(assemble, self.held, self.masks)
            self.theirs = here.swap(self.mine, 1)
            return self.mine, self.theirs

    class Reduce:
        def __init__(self, send, keep, orders):
            self.parts = None
            self.keep, self.got, self.orders = keep, here.swap(send, 1), orders

        def hop(self):
            if self.parts is None:
                n = self.keep.shape[1]
                split = len(self.orders) if n % (128 * len(self.orders)) == 0 else 1
                entries = [(self.keep, self.got, list(here.bits), self.orders[c][0], c, n // split) for c in range(split)]
                orders = [order[1:] for order in self.orders[:split]]
            else:
                entries = [(kept, got, left, order[0], 0, kept.shape[1]) for kept, got, left, order in self.parts]
                orders = [order[1:] for _, _, _, order in self.parts]
            outs = go(fold, entries)
            self.parts = [
                [outs[2 * c + 1], here.swap(outs[2 * c], e[3]), [b for b in e[2] if b != e[3]], orders[c]]
                for c, e in enumerate(entries)
            ]

        def close(self):
            while self.parts is None or self.parts[0][3]:
                self.hop()
            sums = [kept.astype(f32) + got.astype(f32) for kept, got, _, _ in self.parts]
            return sums[0] if len(sums) == 1 else jnp.concatenate(sums, axis=1)

        def wait(self):
            got = go.sync(*([self.got] if self.parts is None else [p[1] for p in self.parts]))
            if self.parts is None:
                self.got = got[0]
            else:
                for p, g in zip(self.parts, got):
                    p[1] = g

    both_ways = [here.bits, here.bits[::-1]]

    attn_cut = [[w_query, w_key], [w_value, w_outgate, w_forget]]
    attn_counts = [sum(a.shape[1] for a in cut) for cut in attn_cut]
    attn_pieces = [go(collect, cut, pieces, 128) for cut in attn_cut]
    attn_got = [here.fetch(attn_pieces[0], 0, j) for j in turns]
    bias_got = [here.fetch(forget_bias, 0, j) for j in turns]
    own = go(project_own, length, inputs, gain_attn,
             [w_query, w_key, w_value, w_outgate, w_forget], forget_bias[None])
    normed, inverse_attn = own[:2]
    mixed = {0: own[2:]}
    gated = {}
    logs = {}

    def attend(j):
        q, k, v, g, _, _, crow = mixed[j]
        z, logs[j] = go(attend_forward, q, k, v, g, crow, scol, srow)
        gated[0, j] = z
        for s in range(1, group):
            gated[s, j] = here.fetch(z, s, 0)

    def wait_gated(j):
        arrived = go.sync(*[gated[s, j] for s in range(1, group)])
        for s in range(1, group):
            gated[s, j] = arrived[s - 1]

    out_piece = go(collect, [w_out], pieces)
    arrived = go.sync(*attn_got, *bias_got, attn_pieces[1], out_piece)
    attn_got, bias_got = arrived[:rows - 1], arrived[rows - 1:-2]
    attn_later = [here.fetch(arrived[-2], 0, j) for j in turns]
    attn_gather = [[Gather(p)] for p in attn_got]
    attend(0)
    out_got = [here.fetch(arrived[-1], 0, j) for j in turns]
    for gathers, p in zip(attn_gather, go.sync(*attn_later)):
        gathers[0].wait()
        gathers.append(Gather(p))
    attn_w = [[gathers[0].close()] for gathers in attn_gather]
    gate_piece = go(collect, [w_gate, w_up], pieces)
    wait_gated(0)
    out_got = go.sync(*out_got)
    out_own = jnp.concatenate([out_piece, *out_got], axis=1)
    out_peers = [here.fetch(out_own, s, 0) for s in range(1, group)]
    for gathers in attn_gather:
        gathers[1].wait()
    for done, gathers in zip(attn_w, attn_gather):
        done.append(gathers[1].close())
    gate_piece = go.sync(gate_piece)[0]
    gate_got = [here.fetch(gate_piece, 0, j) for j in turns]
    for j in turns:
        mixed[j] = go(project_other, normed, attn_w[j - 1], attn_counts, width, heads, bias_got[j - 1][None])
    out_peers = go.sync(*out_peers)
    out_gather = Gather(jnp.concatenate([*out_got, *out_peers], axis=1))
    for j in turns:
        attend(j)
    out_gather.wait()
    out_mine, out_theirs = out_gather.close()
    gate_got = go.sync(*gate_got)
    gate_gather = [Gather(p) for p in gate_got]
    down_piece = go(collect, [w_down], pieces)
    for j in turns:
        wait_gated(j)
    down_piece, out_theirs = go.sync(down_piece, out_theirs)
    down_got = [here.fetch(down_piece, 0, j) for j in turns]
    hidden_row, mlp_normed, inverse_mlp = go(
        close_attention, length, inputs, [gated[slot] for slot in slots], w_out, out_mine, out_theirs, gain_mlp
    )
    for gather in gate_gather:
        gather.wait()
    down_got = go.sync(*down_got)
    down_gather = [Gather(p) for p in down_got]

    def ffn(weights, before, final):
        return go(feed_forward, mlp_normed, cotangent, weights, hidden, gain_mlp, group, pieces, before, final)

    wide = BLK if hidden % BLK == 0 else hidden
    mlp_sums = {}
    send, keep, *carried = ffn([w_gate, w_up, w_down], [], False)
    gate_w = [gather.close() for gather in gate_gather]
    down_w = [gather.close() for gather in down_gather]
    mlp_sums[0] = Reduce(send, keep, both_ways)
    mlp_w = {}
    for j in turns:
        mlp_w[j] = gate_w[j - 1] + down_w[j - 1]
        if j < rows - 1:
            send, keep, *carried = ffn(mlp_w[j], carried, False)
            mlp_sums[j] = Reduce(send, keep, both_ways)
    mlp_sums[0].hop()
    du, dw, m, *made = ffn(mlp_w[rows - 1], carried, True)
    peers = list(range(1, group))
    part, out_part_own, gain_mlp_part = made[group - 1], made[2 * group - 1], made[2 * group]
    out_send = made[group:2 * group - 1]
    got = [to_member(v, s) for v, s in zip(made, peers)]
    mlp_sums[0].hop()
    mlp_sums[rows - 1] = Reduce(*go(lambda w, after: weight_grads(
        "mlp_grads", w, [mlp_normed, cotangent], [(0, [du]), (0, [dw]), (1, [m])], pieces, row_of=(1,), mixed=wide, after=after)), both_ways)
    dh, dh_low, dz_mine, dz_peers = go(
        close_feed_forward, share, group, part, got, hidden_row, inverse_mlp, gain_mlp, cotangent,
        w_out, out_mine, out_theirs,
    )
    dz_parts = [dz_mine]
    own_slots = rows * width
    for s in peers:
        lo = (group - s - 1) * own_slots
        dz_parts.append(here.fetch(dz_peers if group == 2 else dz_peers[:, lo:lo + own_slots], s, 0))
    mlp_sums[0].wait()
    mlp_own = mlp_sums[0].close()
    for j in turns:
        mlp_sums[j].hop()
    out_sum = Reduce(*go(lambda w, after: weight_grads(
        "out_grads", w, [dh_low], [(0, [gated[slot] for slot in slots])], pieces, True, after=after)), both_ways)

    back = {}
    attn_sums = {}
    per_step = together(heads) * HEAD

    def attend_back(j):
        q, k, v, g, forget, ccol, _ = mixed[j]
        parts = [(d, j * width // per_step) for d in dz_parts]
        if width % 128:
            parts = [(a[:, o * per_step:(o + 1) * per_step], 0) for a, o in parts]
        back[j] = go(attend_backward, q, k, v, g, gated[0, j], parts, logs[j], ccol, forget, scol, srow)

    def attn_grads(j, orders):
        attn_sums[j] = Reduce(*go(lambda w, after: weight_grads(
            "attn_grads", w, [normed], [(0, back[j][:2]), (0, back[j][2:5])], pieces, after=after)), orders)

    arrived = go.sync(*dz_parts[1:], *out_send)
    dz_parts[1:], out_send = arrived[:group - 1], arrived[group - 1:]
    out_got = [to_member(v, s) for v, s in zip(out_send, peers)]
    for j in turns:
        attend_back(j)
        attn_grads(j, both_ways)
    for j in turns:
        mlp_sums[j].hop()
    out_sum.hop()
    out_got = go.sync(*out_got)
    for j in turns:
        attn_sums[j].hop()
    for j in turns:
        mlp_sums[j].wait()
    mlp_other = [here.deliver(low(mlp_sums[j].close()), 0, j) for j in turns]
    attend_back(0)
    out_sum.hop()
    for j in turns:
        attn_sums[j].hop()
    attn_grads(0, both_ways)
    own_w = [w_query, w_key, w_value, w_outgate, w_forget]
    pair_terms = [
        (list(back[j][lo:hi]), *attn_w[j - 1][k]) for j in turns for k, (lo, hi) in enumerate(((0, 2), (2, 5)))
    ]

    def attn_back(name, steps):
        outs = []
        for s in steps:
            outs.append(go(lambda w, after: back_rows(
                name, w, s, group, list(back[0][:5]), own_w, pair_terms, normed, gain_attn, after)))
        return [o[0] for o in outs] + [sum(o[1] for o in outs)]

    mlp_other = go.sync(*mlp_other)
    for j in turns:
        attn_sums[j].wait()
    attn_other = [here.deliver(low(attn_sums[j].close()), 0, j) for j in turns]
    out_sum.wait()
    made = attn_back("attn_back_send", peers)
    got = [to_member(v, s) for v, s in zip(made, peers)]
    attn_sums[0].hop()
    out_part = out_sum.close().reshape(-1, group, rows, width)
    out_part = go.sync(out_part)[0]
    out_turned = [here.deliver(low(out_part[:, :, j]).reshape(-1, group * width), 0, j) for j in turns]
    part, gained = attn_back("attn_back_own", [0])
    bias_full = jnp.zeros((here.tensor, heads), f32)
    for j in range(rows):
        bias_full = lax.dynamic_update_slice(bias_full, back[j][5], (here.owner(here.at, 0, j), 0))
    small = jnp.concatenate([made[-1] + gained, gain_mlp_part, bias_full.reshape(1, -1)], axis=1)
    small_hops = [lambda v, b=b: here.swap(v, b) for b in [1] + here.bits] + [
        lambda v, b=b: lax.ppermute(v, "tensor", [(i, i ^ b) for i in range(here.tensor)])
        for b in [1 << k for k in range(here.tensor.bit_length() - 1)]]
    flying = small_hops.pop(0)(small)

    def small_step():
        arrived = go.sync(flying)[0]
        total = small + arrived
        return total, (small_hops.pop(0)(total) if small_hops else None)

    attn_other = go.sync(*attn_other)
    attn_sums[0].hop()
    small, flying = small_step()
    out_own, *arrived = go.sync(out_part_own, *out_got)
    output = lax.dynamic_slice_in_dim(hidden_row, member * share, share, 0) + out_own.astype(f32)
    for v in arrived:
        output = output + v.astype(f32)
    out_turned = go.sync(*out_turned, output)
    output = out_turned[-1]
    out_part = out_part[:, :, 0].reshape(-1, group * width) + sum(v.astype(f32) for v in out_turned[:-1])
    grad_out = out_part[:, :width]
    out_rest = [here.deliver(low(out_part[:, s * width:(s + 1) * width]), s, 0) for s in peers]
    small, flying = small_step()
    mlp_own, *mlp_other = go.sync(mlp_own, *mlp_other)
    attn_sums[0].wait()
    attn = attn_sums[0].close()
    while flying is not None:
        small, flying = small_step()
    out_rest = go.sync(*out_rest)
    grad_inputs = go(close_block, share, group, part, got, inputs, inverse_attn, gain_attn, dh)
    mlp = mlp_own
    for v in mlp_other:
        mlp = mlp + v.astype(f32)

    def columns(kind):
        return jnp.concatenate([mlp[:, b + kind * wide:b + (kind + 1) * wide] for b in range(0, 3 * hidden, 3 * wide)], axis=1)

    for v in out_rest:
        grad_out = grad_out + v.astype(f32)
    for v in attn_other:
        attn = attn + v.astype(f32)
    bias_own = lax.dynamic_slice_in_dim(small[0, 2 * model:], here.at * heads, heads, 0)
    return (
        output,
        grad_inputs,
        small[0, :model],
        attn[:, :width],
        attn[:, width:2 * width],
        attn[:, 2 * width:3 * width],
        attn[:, 3 * width:4 * width],
        attn[:, 4 * width:4 * width + heads],
        bias_own,
        grad_out,
        small[0, model:2 * model],
        columns(0),
        columns(1),
        columns(2),
    )


def solution(mesh):
    placed = (
        P("dp", None), P(), P(None, "tensor"), P(None, "tensor"), P(None, "tensor"),
        P(None, "tensor"), P(None, "tensor"), P("tensor"), P(None, "tensor"), P(),
        P(None, "tensor"), P(None, "tensor"), P(None, "tensor"), P("dp", None), P("dp", None),
    )
    weight = P("dp", "tensor")
    tokens = P(("dp", "tensor"), None)
    return jax.shard_map(
        on_device,
        mesh=mesh,
        in_specs=placed,
        out_specs=(
            tokens, tokens, P(), weight, weight, weight, weight, weight, P("tensor"),
            weight, P(), weight, weight, weight,
        ),
        check_vma=False,
    )
```

```python
import jax
import jax.numpy as jnp
from jax import lax
from jax.sharding import PartitionSpec as P
from jax.experimental import pallas as pl
from jax.experimental.pallas import tpu as pltpu

LOG2E = 1.4426950408889634
LN2 = 0.6931471805599453
HEAD = 64
BLK = 256
EPS = 1e-06
STEP = 115 * 10 ** 9
ROW, MEMBER, CORE, CHIP, PIECE = 0, 1, 2, 3, 4
f32 = jnp.float32
bf16 = jnp.bfloat16


def last(a, b):
    return lax.dot_general(a, b, (((1,), (1,)), ((), ())), preferred_element_type=f32)


def first(a, b):
    return lax.dot_general(a, b, (((0,), (0,)), ((), ())), preferred_element_type=f32)


def mm(a, b):
    return jnp.dot(a, b, preferred_element_type=f32)


def low(values):
    return values.astype(bf16)


def shape(dims, dtype):
    return jax.ShapeDtypeStruct(dims, dtype)


def spec(block, at, mode=None):
    if block is None:
        return pl.BlockSpec(memory_space=pl.ANY)
    return pl.BlockSpec(block, at) if mode is None else pl.BlockSpec(block, at, pipeline_mode=mode)


def run(name, body, where, grid, ins, outs, scratch=(), after=(), flops=0, vmem=56):
    count, extra, made = len(ins), len(after), len(outs)

    def kernel(where_ref, *refs):
        body(where_ref, refs[:count], refs[count + extra:count + extra + made], refs[count + extra + made:])

    return pl.pallas_call(
        kernel,
        grid_spec=pltpu.PrefetchScalarGridSpec(
            num_scalar_prefetch=1,
            grid=grid,
            in_specs=[spec(*entry[1:]) for entry in ins] + [pl.BlockSpec(memory_space=pl.ANY)] * extra,
            out_specs=[spec(*entry[1:]) for entry in outs],
            scratch_shapes=list(scratch),
        ),
        out_shape=[entry[0] for entry in outs],
        compiler_params=pltpu.CompilerParams(vmem_limit_bytes=vmem << 20),
        cost_estimate=pl.CostEstimate(flops=STEP, bytes_accessed=1, transcendentals=0),
        name=name,
    )(where, *[entry[0] for entry in ins], *after)


class Part:
    def __init__(self, array, rows=None, row_at=None, cols=None, col_at=None, into=None):
        self.array = array
        self.rows = array.shape[0] if rows is None else rows
        self.cols = array.shape[1] if cols is None else cols
        self.row_at, self.col_at = row_at, col_at
        self.into = into

    def view(self, ref, w):
        if self.row_at is None and self.col_at is None:
            return ref
        row = 0 if self.row_at is None else pl.multiple_of(self.row_at(w), self.rows)
        col = 0 if self.col_at is None else pl.multiple_of(self.col_at(w), self.cols)
        return ref.at[pl.ds(row, self.rows), pl.ds(col, self.cols)]


def stream(name, body, where, parts, outs, scratch=(), after=(), buffers=()):
    count, extra, made = len(parts), len(after), len(outs)
    single = [p for p in parts if p.into is None]
    chunks = 16

    def kernel(w, *refs):
        sources = refs[:count]
        targets = refs[count + extra:count + extra + made]
        at = count + extra + made
        shared = refs[at:at + len(buffers)]
        at += len(buffers)
        alone = iter(refs[at:at + len(single)])
        held = [next(alone) if p.into is None else shared[p.into[0]].at[
            pl.ds(p.into[1](w) if callable(p.into[1]) else p.into[1], p.rows), pl.ds(p.into[2], p.cols)] for p in parts]
        at += len(single)
        ready = refs[at:at + made]
        in_sems, out_sems = refs[at + made:at + made + 2]
        rest = shared + refs[at + made + 2:]
        loads = []
        for k, part in enumerate(parts):
            copy = pltpu.make_async_copy(part.view(sources[k], w), held[k], in_sems.at[k])
            copy.start()
            loads.append(copy)
        waited = set()
        sent = []

        def get(k):
            if k not in waited:
                loads[k].wait()
                waited.add(k)
            return held[k]

        def put(k, row=None, rows=None, col=None, cols=None):
            spot = (pl.ds(0, outs[k].shape[0]) if row is None else pl.ds(row, rows),
                    pl.ds(0, outs[k].shape[1]) if col is None else pl.ds(col, cols))
            copy = pltpu.make_async_copy(ready[k].at[spot], targets[k].at[spot], out_sems.at[k, len([1 for i, _ in sent if i == k])])
            copy.start()
            sent.append((k, copy))

        body(w, get, ready, put, rest)
        for _, copy in sent:
            copy.wait()

    return pl.pallas_call(
        kernel,
        grid_spec=pltpu.PrefetchScalarGridSpec(
            num_scalar_prefetch=1, grid=(),
            in_specs=[pl.BlockSpec(memory_space=pl.ANY)] * (count + extra),
            out_specs=[pl.BlockSpec(memory_space=pl.ANY)] * made,
            scratch_shapes=[pltpu.VMEM(b, bf16) for b in buffers]
            + [pltpu.VMEM((p.rows, p.cols), p.array.dtype) for p in single]
            + [pltpu.VMEM(o.shape, o.dtype) for o in outs]
            + [pltpu.SemaphoreType.DMA((count,)), pltpu.SemaphoreType.DMA((made, chunks))] + list(scratch),
        ),
        out_shape=list(outs),
        compiler_params=pltpu.CompilerParams(vmem_limit_bytes=58 << 20),
        cost_estimate=pl.CostEstimate(flops=STEP, bytes_accessed=1, transcendentals=0),
        name=name,
    )(where, *[p.array for p in parts], *after)


def fixed(array):
    return (array, array.shape, lambda i, w: (0,) * array.ndim)


def fixed_out(dims, dtype):
    return (shape(dims, dtype), dims, lambda i, w: (0,) * len(dims))


def halves(values, pieces, core):
    count = values.shape[0] // pieces
    even = jnp.concatenate([values[p * count:(p + 1) * count] for p in range(0, pieces, 2)], axis=0)
    odd = jnp.concatenate([values[p * count:(p + 1) * count] for p in range(1, pieces, 2)], axis=0)
    return jnp.where(core == 0, odd, even), jnp.where(core == 0, even, odd)


def three(values):
    top = low(values)
    rest = values - top.astype(f32)
    middle = low(rest)
    return top, middle, low(rest - middle.astype(f32))


def log_keep(values):
    return jnp.minimum(values, 0.0) - jnp.log1p(jnp.exp(-jnp.abs(values)))


def lower(flip=False):
    r = lax.broadcasted_iota(jnp.int32, (BLK, BLK), 0)
    c = lax.broadcasted_iota(jnp.int32, (BLK, BLK), 1)
    return jnp.where(r <= c if flip else r >= c, 1.0, 0.0).astype(bf16)


TOK = 512


def project_tail(i, mixed, width, bias, outs, carry):
    q_ref, k_ref, v_ref, g_ref, f_ref, ccol_ref, crow_ref = outs
    q_ref[...] = low(mixed[:, :width] * (HEAD ** -0.5 * LOG2E))
    for p, ref in ((1, k_ref), (2, v_ref), (3, g_ref)):
        ref[...] = low(mixed[:, p * width:(p + 1) * width])
    heads = f_ref.shape[1]
    forget = mixed[:, 4 * width:4 * width + heads] + bias
    f_ref[...] = forget

    @pl.when(i == 0)
    def _():
        carry[...] = jnp.zeros_like(carry)

    mask = lower()
    hp = crow_ref.shape[1]
    tokens = forget.shape[0]
    for t in range(tokens // BLK):
        rows = slice(t * BLK, (t + 1) * BLK)
        wide = jnp.concatenate([log_keep(forget[rows]) * LOG2E, jnp.zeros((BLK, 128 - heads), f32)], axis=1)
        sums = sum(mm(mask, part) for part in three(wide)) + carry[0:1, :]
        carry[0:1, :] = sums[BLK - 1:BLK, :]
        ccol_ref[rows, :] = sums[:, :heads]
        flat = sums.T
        for s in range(crow_ref.shape[0]):
            crow_ref[s, :, rows] = flat[s * hp:(s + 1) * hp, :]


def together(heads):
    return 2 if heads % 2 == 0 else heads


def project_outs(length, width, heads):
    tokens = lambda i, w: (i, 0)
    return [(shape((length, width), bf16), (TOK, width), tokens) for _ in range(4)] + [
        (shape((length, heads), f32), (TOK, heads), tokens),
        (shape((length, heads), f32), (TOK, heads), tokens),
        (shape((heads // together(heads), together(heads), length), f32),
         (heads // together(heads), together(heads), TOK), lambda i, w: (0, 0, i)),
    ]


def project_own(where, length, inputs, gain, weights, bias, after=()):
    model = inputs.shape[1]
    width, heads = weights[0].shape[1], weights[4].shape[1]

    def body(w, ins, outs, scratch):
        x_ref, gain_ref, wq, wk, wv, wg, wf, b_ref = ins
        a_ref, inv_ref = outs[:2]
        x = x_ref[...].astype(f32)
        inverse = lax.rsqrt(jnp.mean(x * x, axis=1, keepdims=True) + EPS)
        a = low(x * inverse * gain_ref[...])
        a_ref[...] = a
        inv_ref[...] = inverse
        mixed = mm(a, jnp.concatenate([r[...] for r in (wq, wk, wv, wg, wf)], axis=1))
        project_tail(pl.program_id(0), mixed, width, b_ref[...], outs[2:], scratch[0])

    blocks = length // TOK
    tokens = lambda i, w: (i, 0)
    return run(
        "project_own", body, where, (blocks,),
        [(inputs, (TOK, model), lambda i, w: (w[ROW] * blocks + i, 0)), fixed(gain)]
        + [fixed(a) for a in weights] + [fixed(bias)],
        [(shape((length, model), bf16), (TOK, model), tokens), (shape((length, 1), f32), (TOK, 1), tokens)]
        + project_outs(length, width, heads),
        [pltpu.VMEM((8, 128), f32)], after, 2 * length * model * (4 * width + heads),
    )


def core_halves(ref, w, half):
    return (ref[:, pl.ds(pl.multiple_of(w[CORE] * half, 128), half)],
            ref[:, pl.ds(pl.multiple_of((1 - w[CORE]) * half, 128), half)])


def project_other(where, normed, gathered, counts, width, heads, bias, after=()):
    length, model = normed.shape
    half = model // 2

    def body(w, ins, outs, scratch):
        a_ref, b_ref = ins[:2]
        am, at = core_halves(a_ref, w, half)
        mixed = [mm(am, ins[2 + 2 * k][:, :n]) + mm(at, ins[3 + 2 * k][:, :n]) for k, n in enumerate(counts)]
        project_tail(pl.program_id(0), jnp.concatenate(mixed, axis=1), width, b_ref[...], outs, scratch[0])

    return run(
        "project_other", body, where, (length // TOK,),
        [(normed, (TOK, model), lambda i, w: (i, 0)), fixed(bias)] + [fixed(a) for pair in gathered for a in pair],
        project_outs(length, width, heads),
        [pltpu.VMEM((8, 128), f32)], after, 2 * length * model * (4 * width + heads),
    )


def attend_forward(where, q, k, v, g, crow, scol, srow, after=()):
    length, n = q.shape
    heads = n // HEAD
    hp = together(heads)
    width = hp * HEAD

    def body(w, ins, outs, scratch):
        q_ref, k_ref, v_ref, g_ref, crow_ref, scol_ref, srow_ref = ins
        z_ref, lse_ref = outs
        lane = lax.broadcasted_iota(jnp.int32, (1, width), 1) // HEAD
        lane1 = lax.broadcasted_iota(jnp.int32, (BLK, 128), 1)
        tri = lax.broadcasted_iota(jnp.int32, (BLK, BLK), 0) >= lax.broadcasted_iota(jnp.int32, (BLK, BLK), 1)
        crows = crow_ref[0]
        v_wide = jnp.concatenate([v_ref[...], jnp.ones((length, 128), bf16)], axis=1)
        for i in range(length // BLK):
            rows = pl.ds(i * BLK, BLK)
            reach = (i + 1) * BLK
            q = q_ref[rows, :]
            same = scol_ref[rows, :] == srow_ref[:, :reach]
            if i:
                allowed = jnp.concatenate([same[:, :reach - BLK], same[:, reach - BLK:] & tri], axis=1)
            else:
                allowed = same & tri
            scores = last(jnp.concatenate([jnp.where(lane == h, q, 0) for h in range(hp)], axis=0), k_ref[:reach, :])
            tops, grown = [], []
            for h in range(hp):
                s = jnp.where(allowed, scores[h * BLK:(h + 1) * BLK] - crows[h:h + 1, :reach], -1e30)
                top = jnp.max(s, axis=1, keepdims=True)
                tops.append(top)
                grown.append(low(jnp.exp2(s - top)))
            parts = mm(jnp.concatenate(grown, axis=0), v_wide[:reach, :])
            out = jnp.zeros((BLK, width), f32)
            stats = jnp.zeros((BLK, 128), f32)
            for h in range(hp):
                part = parts[h * BLK:(h + 1) * BLK]
                total = part[:, width:width + 1]
                out = jnp.where(lane == h, part[:, :width] * (1.0 / total), out)
                stats = jnp.where(lane1 == h, tops[h] + jnp.log2(total), stats)
            z_ref[rows, :] = low(out * jax.nn.sigmoid(g_ref[rows, :].astype(f32)))
            lse_ref[0, :, i * BLK:(i + 1) * BLK] = stats.T[:hp, :]

    tokens = lambda i, w: (0, i)
    return run(
        "attend_forward", body, where, (heads // hp,),
        [(a, (length, width), tokens) for a in (q, k, v, g)]
        + [(crow, (1, hp, length), lambda i, w: (i, 0, 0)), fixed(scol), fixed(srow)],
        [(shape((length, n), bf16), (length, width), tokens),
         (shape((heads // hp, hp, length), f32), (1, hp, length), lambda i, w: (i, 0, 0))],
        (), after, heads * length * length * 1100,
    )


def attend_backward(where, q, k, v, g, z, dz_parts, lse, ccol, forget, scol, srow, after=()):
    length, n = q.shape
    heads = n // HEAD
    hp = together(heads)
    width = hp * HEAD
    steps = heads // hp
    group = len(dz_parts)
    share = length // group

    def body(w, ins, outs, scratch):
        q_ref, k_ref, v_ref, g_ref, z_ref = ins[:5]
        dz_refs = ins[5:5 + group]
        lse_ref, ccol_ref, f_ref, scol_ref, srow_ref = ins[5 + group:]
        dq_ref, dk_ref, dv_ref, dg_ref, df_ref, db_ref = outs
        dqacc, rates, dzfull = scratch
        step = pl.program_id(0)
        lane = lax.broadcasted_iota(jnp.int32, (1, width), 1) // HEAD
        lane1 = lax.broadcasted_iota(jnp.int32, (1, 128), 1)
        tri = lax.broadcasted_iota(jnp.int32, (BLK, BLK), 1) >= lax.broadcasted_iota(jnp.int32, (BLK, BLK), 0)
        blocks = length // BLK

        @pl.when(step == 0)
        def _():
            rates[...] = jnp.zeros_like(rates)

        for s in range(group):
            at = lax.rem(w[MEMBER] + s, group) * share
            dzfull[pl.ds(pl.multiple_of(at, share), share), :] = dz_refs[s][...]
        sig = jax.nn.sigmoid(g_ref[...].astype(f32))
        dz = dzfull[...].astype(f32)
        prod = dz * z_ref[...].astype(f32)
        dout = low(dz * sig)
        dg_ref[...] = low(prod * (1.0 - sig))
        prod_hi = low(prod)
        prod_lo = low(prod - prod_hi.astype(f32))
        lses = lse_ref[0]
        chosen = lax.broadcasted_iota(jnp.int32, (8, width), 0) == lax.broadcasted_iota(jnp.int32, (8, width), 1) // HEAD
        chosen = jnp.where(chosen, 1.0, 0.0).astype(bf16)
        centres = last(chosen, prod_hi) + last(chosen, prod_lo)
        ones = jnp.ones((length, 128), bf16)
        q_wide = jnp.concatenate([q_ref[...], ones], axis=1)
        k_wide = jnp.concatenate([k_ref[...], ones], axis=1)
        decays = [
            jnp.sum(jnp.where(lane1[:, :heads] == step * hp + h, ccol_ref[...], 0.0), axis=1, keepdims=True)
            for h in range(hp)
        ]
        dqacc[...] = jnp.zeros_like(dqacc)
        for j in range(blocks):
            keys = pl.ds(j * BLK, BLK)
            lo = j * BLK
            count = length - lo
            keyed = lambda ref: jnp.concatenate([jnp.where(lane == h, ref[keys, :], 0) for h in range(hp)], axis=0)
            scores = last(keyed(k_ref), q_ref[lo:, :])
            dps = last(keyed(v_ref), dout[lo:, :])
            same = scol_ref[keys, :] == srow_ref[:, lo:]
            if j < blocks - 1:
                allowed = jnp.concatenate([same[:, :BLK] & tri, same[:, BLK:]], axis=1)
            else:
                allowed = same & tri
            ps, dss = [], []
            for h in range(hp):
                rows = slice(h * BLK, (h + 1) * BLK)
                s = scores[rows] - decays[h][lo:lo + BLK, :] - lses[h:h + 1, lo:]
                p = jnp.exp2(jnp.where(allowed, s, -1e30))
                ps.append(low(p))
                dss.append(low(p * (dps[rows] - centres[h:h + 1, lo:])))
            dvs = mm(jnp.concatenate(ps, axis=0), dout[lo:, :])
            dks = mm(jnp.concatenate(dss, axis=0), q_wide[lo:, :])
            dqs = first(jnp.concatenate(dss, axis=1), k_wide[lo:lo + BLK, :])
            dk = jnp.zeros((BLK, width), f32)
            dv = jnp.zeros((BLK, width), f32)
            for h in range(hp):
                rows = slice(h * BLK, (h + 1) * BLK)
                dk = jnp.where(lane == h, dks[rows, :width], dk)
                dv = jnp.where(lane == h, dvs[rows], dv)
                rates[keys, :] = jnp.where(lane1 == step * hp + h, -dks[rows, width:width + 1], rates[keys, :])
                dqacc[h * length + lo:(h + 1) * length, :] += dqs[h * count:(h + 1) * count]
            dk_ref[keys, :] = low(dk * LN2)
            dv_ref[keys, :] = low(dv)
        dq = jnp.zeros((length, width), f32)
        for h in range(hp):
            part = dqacc[h * length:(h + 1) * length, :]
            dq = jnp.where(lane == h, part[:, :width], dq)
            rates[...] = jnp.where(lane1 == step * hp + h, rates[...] + part[:, width:width + 1], rates[...])
        dq_ref[...] = low(dq * HEAD ** -0.5)

        @pl.when(step == steps - 1)
        def _():
            mask = lower(True)
            carry = jnp.zeros((1, 128), f32)
            bias = jnp.zeros((1, heads), f32)
            for b in reversed(range(blocks)):
                rows = pl.ds(b * BLK, BLK)
                sums = sum(mm(mask, part) for part in three(rates[rows, :])) + carry
                carry = sums[0:1, :]
                df = low(sums[:, :heads] * jax.nn.sigmoid(-f_ref[rows, :]))
                df_ref[rows, :] = df
                bias = bias + jnp.sum(df.astype(f32), axis=0, keepdims=True)
            db_ref[...] = bias

    tokens = lambda i, w: (0, i)
    wide = (shape((length, n), bf16), (length, width), tokens)
    return run(
        "attend_backward", body, where, (steps,),
        [(a, (length, width), tokens) for a in (q, k, v, g, z)]
        + [(a, (share, width), lambda i, w, off=off: (0, off + i)) for a, off in dz_parts]
        + [(lse, (1, hp, length), lambda i, w: (i, 0, 0))] + [fixed(a) for a in (ccol, forget, scol, srow)],
        [wide] * 4 + [fixed_out((length, heads), bf16), fixed_out((1, heads), f32)],
        [pltpu.VMEM((hp * length, width + 128), f32), pltpu.VMEM((length, 128), f32), pltpu.VMEM((length, width), bf16)],
        after, heads * length * length * 1500,
    )


def close_attention(where, length, inputs, gated, out_own, out_mine, out_theirs, gain, after=()):
    model = inputs.shape[1]
    half = model // 2
    width = out_own.shape[1]

    def body(w, ins, outs, scratch):
        x_ref, own_ref, m_ref, t_ref, gain_ref = ins[:5]
        z = jnp.concatenate([r[...] for r in ins[5:]], axis=1)
        h_ref, a_ref, inv_ref = outs
        for ref, core in ((m_ref, w[CORE]), (t_ref, 1 - w[CORE])):
            at = pl.ds(pl.multiple_of(core * half, 128), half)
            own = own_ref[pl.ds(pl.multiple_of(core * half, 128), half), :]
            rest = ref[:, :(len(gated) - 1) * width]
            h_ref[:, at] = x_ref[:, at].astype(f32) + last(z, jnp.concatenate([own, rest], axis=1))
        h = h_ref[...]
        inverse = lax.rsqrt(jnp.mean(h * h, axis=1, keepdims=True) + EPS)
        a = low(h * inverse * gain_ref[...])
        a_ref[...] = a
        inv_ref[...] = inverse

    blocks = length // TOK
    tokens = lambda i, w: (i, 0)
    return run(
        "close_attention", body, where, (blocks,),
        [(inputs, (TOK, model), lambda i, w: (w[ROW] * blocks + i, 0))]
        + [fixed(a) for a in (out_own, out_mine, out_theirs, gain)]
        + [(z, (TOK, width), tokens) for z in gated],
        [(shape((length, model), f32), (TOK, model), tokens), (shape((length, model), bf16), (TOK, model), tokens),
         (shape((length, 1), f32), (TOK, 1), tokens)],
        (), after, 2 * length * model * width * len(gated),
    )


def once(array_or_shape, block, at):
    return (array_or_shape, block, at, pl.Buffered(1))


def feed_forward(where, normed, cotangent, weights, hidden, gain, group, pieces, before, final, after=()):
    length, model = normed.shape
    half = model // 2
    share = length // group
    wide = BLK if hidden % BLK == 0 else hidden
    steps = hidden // wide
    own = len(weights) == 3
    tokens = length // TOK

    def body(w, ins, outs, scratch):
        a_ref, e_ref, gain_ref = ins[:3]
        blocks = ins[3:3 + (3 if own else 6)]
        rest = ins[3 + len(blocks):]
        back, out = scratch[:2]
        kept = scratch[2:5]
        step = pl.program_id(0)
        core = pl.ds(pl.multiple_of(w[CORE] * half, 128), half)
        other = pl.ds(pl.multiple_of((1 - w[CORE]) * half, 128), half)
        copies = [pltpu.make_async_copy(r, scratch[5 + k], scratch[5 + len(rest)].at[k]) for k, r in enumerate(rest)]

        @pl.when(step == 0)
        def _():
            for c in copies:
                c.start()
            back[...] = jnp.zeros_like(back)
            out[...] = jnp.zeros_like(out)

        for t in range(tokens):
            rows = pl.ds(t * TOK, TOK)
            if own:
                gate, up = mm(a_ref[rows, :], blocks[0][...]), mm(a_ref[rows, :], blocks[1][...])
                dm = mm(e_ref[rows, :], blocks[2][...])
            else:
                both = lambda ref, p: mm(ref[rows, core], blocks[p][...]) + mm(ref[rows, other], blocks[3 + p][...])
                gate, up, dm = both(a_ref, 0), both(a_ref, 1), both(e_ref, 2)
            sig = jax.nn.sigmoid(gate)
            act = gate * sig
            values = (low(dm * up * (sig * (1.0 + gate * (1.0 - sig)))), low(dm * act), low(act * up))
            for k, value in enumerate(values):
                kept[k][rows, :] = value
                if final:
                    outs[k][rows, :] = value
        du, dw, m = kept
        if own:
            back[...] += last(du[...], blocks[0][...]) + last(dw[...], blocks[1][...])
            out[...] += last(m[...], blocks[2][...])
        else:
            for where_to, p in ((core, 0), (other, 3)):
                back[:, where_to] += last(du[...], blocks[p][...]) + last(dw[...], blocks[p + 1][...])
                out[:, where_to] += last(m[...], blocks[p + 2][...])
        if not final:
            for k, left in enumerate((a_ref, a_ref, e_ref)):
                send, keep = halves(low(first(left[...], kept[k][...])), pieces, w[CORE])
                outs[0][:, k * wide:(k + 1) * wide] = send
                outs[1][:, k * wide:(k + 1) * wide] = keep

        @pl.when(step == steps - 1)
        def _():
            for c in copies:
                c.wait()
            if rest:
                back[...] += scratch[5][...].astype(f32)
                out[...] += scratch[6][...].astype(f32)
            if final:
                for k in range(group):
                    member = lax.rem(w[MEMBER] + (k + 1) % group, group)
                    rows = pl.ds(pl.multiple_of(member * share, share), share)
                    outs[3 + k][...] = low(back[rows, :])
                    outs[3 + group + k][...] = low(out[rows, :])
                outs[3 + 2 * group][...] = jnp.sum(back[...] * a_ref[...].astype(f32), axis=0, keepdims=True) / gain_ref[...]
            else:
                outs[2][...] = low(back[...])
                outs[3][...] = low(out[...])

    whole = lambda i, w: (0, 0)
    column = lambda i, w: (0, i)
    if own:
        parts = [(a, (model, wide), column) for a in weights]
    else:
        gm, gt, dm, dt = weights
        parts = [(a, (half, wide), lambda i, w, p=p: (0, p * steps + i))
                 for a, p in ((gm, 0), (gm, 1), (dm, 0), (gt, 0), (gt, 1), (dt, 0))]
    row_sum = once(shape((length, model), bf16), (length, model), whole)
    if final:
        outs = [(shape((length, hidden), bf16), (length, wide), column)] * 3
        outs += [once(shape((share, model), bf16), (share, model), whole)] * (2 * group)
        outs += [fixed_out((1, model), f32)]
    else:
        side = (shape((half, 3 * hidden), bf16), (half, 3 * wide), column)
        outs = [side, side, row_sum, row_sum]
    return run(
        "feed_forward", body, where, (steps,),
        [once(normed, (length, model), whole), once(cotangent, (length, model), lambda i, w: (w[ROW], 0)), fixed(gain)] + parts
        + [(a, None, None) for a in before],
        outs,
        [pltpu.VMEM((length, model), f32)] * 2 + [pltpu.VMEM((length, wide), bf16)] * 3
        + [pltpu.VMEM((length, model), bf16) for _ in before]
        + ([pltpu.SemaphoreType.DMA((len(before),))] if before else []),
        after,
    )


def weight_grads(name, where, lefts, groups, pieces, rows_of=False, row_of=(), mixed=0, after=()):
    length = groups[0][1][0].shape[0] if not rows_of else lefts[0].shape[0]
    half = lefts[0].shape[1] // 2
    widths = [sum(r.shape[1] for r in rights) for _, rights in groups]
    padded = [-(-n // 128) * 128 for n in widths]
    padded[-1] += -sum(padded) % 256
    parts, plan, loaded = [], [], {}
    row_at = (lambda w: w[MEMBER] * length) if rows_of else None
    for k, (s, rights) in enumerate(groups):
        if s not in loaded:
            loaded[s] = len(parts)
            parts.append(Part(lefts[s], length, (lambda w: w[ROW] * length) if s in row_of else None))
        at = []
        for r in rights:
            at.append(len(parts))
            parts.append(Part(r, length, row_at, r.shape[1]))
        plan.append((loaded[s], at, sum(padded[:k]), widths[k], padded[k]))

    def body(w, get, ready, put, rest):
        for k, (left, at, col, n, full) in enumerate(plan):
            left = get(left)[...]
            right = [get(k)[...] for k in at]
            value = low(first(left, right[0] if len(right) == 1 else jnp.concatenate(right, axis=1)))
            for which, part in enumerate(halves(value, pieces, w[CORE])):
                if mixed:
                    for b in range(n // mixed):
                        spot = (b * len(plan) + k) * mixed
                        ready[which][:, spot:spot + mixed] = part[:, b * mixed:(b + 1) * mixed]
                        put(which, col=spot, cols=mixed)
                    continue
                ready[which][:, col:col + n] = part
                if n < full:
                    ready[which][:, col + n:col + full] = jnp.zeros((half, full - n), bf16)
                put(which, col=col, cols=full)

    return stream(name, body, where, parts, [shape((half, sum(padded)), bf16)] * 2, (), after)


def fold(where, entries, after=()):
    keep, _, bits, _, _, width = entries[0]
    rows = keep.shape[0]
    count = len(bits)
    pieces = 1 << count
    piece = rows // pieces
    wide = next(n for n in (768, 512, 384, width) if width % n == 0)
    across = width // wide
    block = (piece, wide)
    ins, outs = [], []
    for keep, got, bits, bit_at, col, _ in entries:
        place = count - 1 - bits.index(bit_at)

        def index(mine, place=place, bit_at=bit_at, col=col):
            def at(i, c, w):
                own = lax.rem(w[CHIP] // (bit_at >> 1), 2)
                bit = own if mine else 1 - own
                low_part = lax.rem(i, 1 << place)
                high = i // (1 << place)
                return ((high * 2 + bit) * (1 << place) + low_part, col * across + c)
            return at

        for mine in (False, True):
            ins += [(keep, block, index(mine)), (got, block, index(mine))]
            outs.append((shape((rows // 2, width), bf16), block, lambda i, c, w: (i, c)))

    def body(w, ins_, outs_, scratch):
        for k, out in enumerate(outs_):
            out[...] = ins_[2 * k][...] + ins_[2 * k + 1][...]

    return run("fold", body, where, (pieces // 2, across), ins, outs, (), after, 10 ** 9)


def assemble(where, pieces, masks, after=()):
    count, extra = len(pieces), len(after)
    rows, width = pieces[0].shape

    def kernel(w, *refs):
        out, held, sems = refs[count + extra:]
        loads = [pltpu.make_async_copy(refs[k], held.at[k], sems.at[0, k]) for k in range(count)]
        for c in loads:
            c.start()
        stores = []
        for k in range(count):
            loads[k].wait()
            at = pl.multiple_of(jnp.bitwise_xor(w[CHIP], masks[k]) * rows, rows)
            stores.append(pltpu.make_async_copy(held.at[k], out.at[pl.ds(at, rows), :], sems.at[1, k]))
            stores[k].start()
        for c in stores:
            c.wait()

    return pl.pallas_call(
        kernel,
        grid_spec=pltpu.PrefetchScalarGridSpec(
            num_scalar_prefetch=1, grid=(),
            in_specs=[pl.BlockSpec(memory_space=pl.ANY)] * (count + extra),
            out_specs=pl.BlockSpec(memory_space=pl.ANY),
            scratch_shapes=[pltpu.VMEM((count, rows, width), bf16), pltpu.SemaphoreType.DMA((2, count))],
        ),
        out_shape=shape((count * rows, width), bf16),
        compiler_params=pltpu.CompilerParams(vmem_limit_bytes=56 << 20),
        cost_estimate=pl.CostEstimate(flops=STEP, bytes_accessed=1, transcendentals=0),
        name="assemble",
    )(where, *pieces, *after)


def back_rows(name, where, step, group, own_x, own_w, pair_terms, normed, gain, after=()):
    length, model = normed.shape
    half = model // 2
    share = length // group
    member = lambda w: lax.rem(w[MEMBER] + step, group)
    row_at = lambda w: member(w) * share
    parts, tails, cuts = [], [], []
    col = 0

    def lay(arrays, buffer, narrow):
        at = col
        for a in arrays:
            n = a.shape[1]
            rows, pick = (share, row_at) if buffer == 0 else (a.shape[0], None)
            if n % 128 == 0 and at % 128 == 0:
                parts.append(Part(a, rows, pick, n, None, (buffer, 0, at)))
            else:
                tails.append((len(parts), buffer, at, n))
                parts.append(Part(a, rows, pick, n))
            at += n
        return at

    if any(a.shape[1] % 128 for a in own_x[:-1]):
        own_x, own_w = [jnp.concatenate(own_x, axis=1)], [jnp.concatenate(own_w, axis=1)]
        pair_terms = [([jnp.concatenate(xs, axis=1)], mine, theirs) for xs, mine, theirs in pair_terms]
    lay(own_x, 0, True)
    end = lay(own_w, 1, True)
    full = -(-end // 128) * 128
    cuts.append((0, len(parts), 0, full))
    col = full
    for xs, mine, theirs in pair_terms:
        first_part = len(parts)
        lay(xs, 0, True)
        n = mine.shape[1]
        parts.append(Part(mine, into=(1, lambda w: pl.multiple_of(w[CORE] * half, half), col)))
        parts.append(Part(theirs, into=(1, lambda w: pl.multiple_of((1 - w[CORE]) * half, half), col)))
        cuts.append((first_part, len(parts), col, n))
        col += n
    unit_at = len(parts)
    parts.append(Part(normed, share, row_at))
    parts.append(Part(gain))

    def body(w, get, ready, put, rest):
        x_all, w_all = rest[:2]
        for low_part, high_part, at, n in cuts:
            for k in range(low_part, high_part):
                get(k)
            for k, buffer, spot, count in tails:
                if low_part <= k < high_part:
                    target = (x_all, w_all)[buffer]
                    last_col = at + n if spot + count <= at + n else spot + count
                    value = get(k)[...]
                    fill = jnp.zeros((value.shape[0], last_col - spot - count), bf16)
                    target[:, spot:last_col] = jnp.concatenate([value, fill], axis=1) if last_col > spot + count else value
            part = last(x_all[:, at:at + n], w_all[:, at:at + n])
            rest[2][...] = part if at == 0 else rest[2][...] + part
        total = rest[2][...]
        ready[0][...] = low(total)
        put(0)
        u = get(unit_at)[...].astype(f32)
        ready[1][...] = jnp.sum(total * u, axis=0, keepdims=True) / get(unit_at + 1)[...]
        put(1)

    return stream(
        name, body, where, parts, [shape((share, model), bf16), shape((1, model), f32)],
        [pltpu.VMEM((share, model), f32)], after, [(share, col), (model, col)],
    )


def close_feed_forward(where, share, group, part, got, hidden_row, inverse, gain, cotangent,
                       out_own, out_mine, out_theirs, after=()):
    model = part.shape[1]
    half = model // 2
    width = out_own.shape[1]
    filled = width + out_mine.shape[1]
    own_slots = filled // group

    def body(w, ins, outs, scratch):
        p_ref, h_ref, i_ref, gain_ref, e_ref, own_ref, m_ref, t_ref = ins[:8]
        dh_ref, low_ref, mine_out, peer_out = outs
        total = p_ref[...].astype(f32)
        for r in ins[8:]:
            total = total + r[...].astype(f32)
        unit = h_ref[...] * i_ref[...]
        scaled = total * gain_ref[...]
        dh = e_ref[...].astype(f32) + i_ref[...] * (scaled - unit * jnp.mean(scaled * unit, axis=1, keepdims=True))
        dh_ref[...] = dh
        d = low(dh)
        low_ref[...] = d
        dz = 0.0
        for d_half, ref, core in zip(core_halves(low_ref, w, half), (m_ref, t_ref), (w[CORE], 1 - w[CORE])):
            own = own_ref[pl.ds(pl.multiple_of(core * half, 128), half), :]
            dz = dz + mm(d_half, jnp.concatenate([own, ref[...]], axis=1))
        mine_out[...] = low(dz[:, :own_slots])
        peer_out[...] = low(dz[:, own_slots:])

    whole = lambda i, w: (0, 0)
    mine = lambda i, w: (w[MEMBER], 0)
    return run(
        "close_feed_forward", body, where, (1,),
        [fixed(part), (hidden_row, (share, model), mine), (inverse, (share, 1), mine), fixed(gain),
         (cotangent, (share, model), lambda i, w: (w[ROW] * group + w[MEMBER], 0)),
         fixed(out_own), fixed(out_mine), fixed(out_theirs)] + [fixed(a) for a in got],
        [(shape((share, model), f32), (share, model), whole), (shape((share, model), bf16), (share, model), whole),
         (shape((share, own_slots), bf16), (share, own_slots), whole),
         (shape((share, filled - own_slots), bf16), (share, filled - own_slots), whole)],
        (), after, 2 * share * model * filled,
    )


def close_block(where, share, group, part, got, inputs, inverse, gain, dh, after=()):
    model = part.shape[1]
    step_rows = min(BLK, share)
    blocks = share // step_rows
    row_blocks = group * blocks

    def body(w, ins, outs, scratch):
        p_ref, x_ref, i_ref, gain_ref, dh_ref = ins[:5]
        total = p_ref[...].astype(f32)
        for r in ins[5:]:
            total = total + r[...].astype(f32)
        unit = x_ref[...].astype(f32) * i_ref[...]
        scaled = total * gain_ref[...]
        outs[0][...] = dh_ref[...] + i_ref[...] * (scaled - unit * jnp.mean(scaled * unit, axis=1, keepdims=True))

    tokens = lambda i, w: (i, 0)
    return run(
        "close_block", body, where, (blocks,),
        [(part, (step_rows, model), tokens),
         (inputs, (step_rows, model), lambda i, w: (w[ROW] * row_blocks + w[MEMBER] * blocks + i, 0)),
         (inverse, (step_rows, 1), lambda i, w: (w[MEMBER] * blocks + i, 0)), fixed(gain),
         (dh, (step_rows, model), tokens)] + [(a, (step_rows, model), tokens) for a in got],
        [(shape((share, model), f32), (step_rows, model), tokens)], (), after,
    )[0]


def collect(where, arrays, pieces, unit=1, after=()):
    count = arrays[0].shape[0] // pieces
    filled = sum(a.shape[1] for a in arrays)
    total = -(-filled // unit) * unit

    def body(w, ins, outs, scratch):
        at = 0
        for r in ins:
            n = r.shape[1]
            outs[0][:, at:at + n] = r[...]
            at += n
        if at < total:
            outs[0][:, at:] = jnp.zeros((count, total - at), bf16)

    return run(
        "collect", body, where, (1,),
        [(a, (count, a.shape[1]), lambda i, w: (w[PIECE], 0)) for a in arrays],
        [(shape((count, total), bf16), (count, total), lambda i, w: (0, 0))], (), after,
    )[0]


class Place:
    def __init__(self, rows):
        self.tensor = lax.axis_size("tensor")
        self.dp = lax.axis_size("dp")
        self.rows = rows
        self.group = self.tensor // rows
        self.at = lax.axis_index("tensor")
        self.dp_at = lax.axis_index("dp")
        self.bits = [1 << b for b in reversed(range(1, self.dp.bit_length() - 1))]

    def owner(self, at, step, turn):
        row, member = at // self.group, at % self.group
        return ((row + turn) % self.rows) * self.group + (member + step) % self.group

    def fetch(self, value, step, turn):
        pairs = [(self.owner(i, step, turn), i) for i in range(self.tensor)]
        return lax.ppermute(value, "tensor", pairs)

    def deliver(self, value, step, turn):
        pairs = [(i, self.owner(i, step, turn)) for i in range(self.tensor)]
        return lax.ppermute(value, "tensor", pairs)

    def swap(self, value, bit):
        return lax.ppermute(value, "dp", [(i, i ^ bit) for i in range(self.dp)])


class Chain:
    def __init__(self, where):
        self.where = where
        self.behind = ()

    def __call__(self, make, *args, extra=(), **keys):
        made = make(self.where, *args, after=self.behind + tuple(extra), **keys)
        outs = made if isinstance(made, (list, tuple)) else [made]
        self.behind = (min(outs, key=lambda a: a.size),)
        return made

    def sync(self, *values):
        out = lax.optimization_barrier((*values, *self.behind))
        self.behind = tuple(out[len(values):])
        return out[:len(values)]


def on_device(
    inputs, gain_attn, w_query, w_key, w_value, w_outgate, w_forget, forget_bias, w_out,
    gain_mlp, w_gate, w_up, w_down, segment_ids, cotangent,
):
    rows, length = segment_ids.shape
    here = Place(rows)
    group, pieces = here.group, here.dp
    heads, width, hidden = w_forget.shape[1], w_query.shape[1], w_gate.shape[1]
    model = inputs.shape[1]
    share = length // group
    row, member = here.at // group, here.at % group
    core, chip = here.dp_at % 2, here.dp_at // 2
    where = jnp.stack([row, member, core, chip, core * (pieces // 2) + chip]).astype(jnp.int32)
    go = Chain(where)
    gain_attn, gain_mlp = gain_attn[None], gain_mlp[None]
    segment = lax.dynamic_index_in_dim(segment_ids, row, 0, keepdims=False)
    scol, srow = segment[:, None], segment[None, :]
    turns = range(1, rows)
    slots = [(s, j) for s in range(group) for j in range(rows)]

    def to_member(value, step):
        return lax.ppermute(value, "tensor", [
            (i, (i // group) * group + (i % group + step) % group) for i in range(here.tensor)])

    class Gather:
        def __init__(self, piece):
            others = range(1, here.dp // 2)
            self.masks = [0] + sorted(others, key=lambda k: bin(k).count("1"))
            self.held = [piece] + [here.swap(piece, 2 * k) for k in self.masks[1:]]

        def wait(self):
            self.held[1:] = go.sync(*self.held[1:])

        def close(self):
            self.mine = go(assemble, self.held, self.masks)
            self.theirs = here.swap(self.mine, 1)
            return self.mine, self.theirs

    class Reduce:
        def __init__(self, send, keep, orders):
            self.parts = None
            self.keep, self.got, self.orders = keep, here.swap(send, 1), orders

        def hop(self):
            if self.parts is None:
                n = self.keep.shape[1]
                split = len(self.orders) if n % (128 * len(self.orders)) == 0 else 1
                entries = [(self.keep, self.got, list(here.bits), self.orders[c][0], c, n // split) for c in range(split)]
                orders = [order[1:] for order in self.orders[:split]]
            else:
                entries = [(kept, got, left, order[0], 0, kept.shape[1]) for kept, got, left, order in self.parts]
                orders = [order[1:] for _, _, _, order in self.parts]
            outs = go(fold, entries)
            self.parts = [
                [outs[2 * c + 1], here.swap(outs[2 * c], e[3]), [b for b in e[2] if b != e[3]], orders[c]]
                for c, e in enumerate(entries)
            ]

        def close(self):
            while self.parts is None or self.parts[0][3]:
                self.hop()
            sums = [kept.astype(f32) + got.astype(f32) for kept, got, _, _ in self.parts]
            return sums[0] if len(sums) == 1 else jnp.concatenate(sums, axis=1)

        def wait(self):
            got = go.sync(*([self.got] if self.parts is None else [p[1] for p in self.parts]))
            if self.parts is None:
                self.got = got[0]
            else:
                for p, g in zip(self.parts, got):
                    p[1] = g

    both_ways = [here.bits, here.bits[::-1]]

    attn_cut = [[w_query, w_key], [w_value, w_outgate, w_forget]]
    attn_counts = [sum(a.shape[1] for a in cut) for cut in attn_cut]
    attn_pieces = [go(collect, cut, pieces, 128) for cut in attn_cut]
    attn_got = [here.fetch(attn_pieces[0], 0, j) for j in turns]
    bias_got = [here.fetch(forget_bias, 0, j) for j in turns]
    own = go(project_own, length, inputs, gain_attn,
             [w_query, w_key, w_value, w_outgate, w_forget], forget_bias[None])
    normed, inverse_attn = own[:2]
    mixed = {0: own[2:]}
    gated = {}
    logs = {}

    def attend(j):
        q, k, v, g, _, _, crow = mixed[j]
        z, logs[j] = go(attend_forward, q, k, v, g, crow, scol, srow)
        gated[0, j] = z
        for s in range(1, group):
            gated[s, j] = here.fetch(z, s, 0)

    def wait_gated(j):
        arrived = go.sync(*[gated[s, j] for s in range(1, group)])
        for s in range(1, group):
            gated[s, j] = arrived[s - 1]

    out_piece = go(collect, [w_out], pieces)
    arrived = go.sync(*attn_got, *bias_got, attn_pieces[1], out_piece)
    attn_got, bias_got = arrived[:rows - 1], arrived[rows - 1:-2]
    attn_later = [here.fetch(arrived[-2], 0, j) for j in turns]
    attn_gather = [[Gather(p)] for p in attn_got]
    attend(0)
    out_got = [here.fetch(arrived[-1], 0, j) for j in turns]
    for gathers, p in zip(attn_gather, go.sync(*attn_later)):
        gathers[0].wait()
        gathers.append(Gather(p))
    attn_w = [[gathers[0].close()] for gathers in attn_gather]
    gate_piece = go(collect, [w_gate, w_up], pieces)
    wait_gated(0)
    out_got = go.sync(*out_got)
    out_own = jnp.concatenate([out_piece, *out_got], axis=1)
    out_peers = [here.fetch(out_own, s, 0) for s in range(1, group)]
    for gathers in attn_gather:
        gathers[1].wait()
    for done, gathers in zip(attn_w, attn_gather):
        done.append(gathers[1].close())
    gate_piece = go.sync(gate_piece)[0]
    gate_got = [here.fetch(gate_piece, 0, j) for j in turns]
    for j in turns:
        mixed[j] = go(project_other, normed, attn_w[j - 1], attn_counts, width, heads, bias_got[j - 1][None])
    out_peers = go.sync(*out_peers)
    out_gather = Gather(jnp.concatenate([*out_got, *out_peers], axis=1))
    for j in turns:
        attend(j)
    out_gather.wait()
    out_mine, out_theirs = out_gather.close()
    gate_got = go.sync(*gate_got)
    gate_gather = [Gather(p) for p in gate_got]
    down_piece = go(collect, [w_down], pieces)
    for j in turns:
        wait_gated(j)
    down_piece, out_theirs = go.sync(down_piece, out_theirs)
    down_got = [here.fetch(down_piece, 0, j) for j in turns]
    hidden_row, mlp_normed, inverse_mlp = go(
        close_attention, length, inputs, [gated[slot] for slot in slots], w_out, out_mine, out_theirs, gain_mlp
    )
    for gather in gate_gather:
        gather.wait()
    down_got = go.sync(*down_got)
    down_gather = [Gather(p) for p in down_got]

    def ffn(weights, before, final):
        return go(feed_forward, mlp_normed, cotangent, weights, hidden, gain_mlp, group, pieces, before, final)

    wide = BLK if hidden % BLK == 0 else hidden
    mlp_sums = {}
    send, keep, *carried = ffn([w_gate, w_up, w_down], [], False)
    gate_w = [gather.close() for gather in gate_gather]
    down_w = [gather.close() for gather in down_gather]
    mlp_sums[0] = Reduce(send, keep, both_ways)
    mlp_w = {}
    for j in turns:
        mlp_w[j] = gate_w[j - 1] + down_w[j - 1]
        if j < rows - 1:
            send, keep, *carried = ffn(mlp_w[j], carried, False)
            mlp_sums[j] = Reduce(send, keep, both_ways)
    mlp_sums[0].hop()
    du, dw, m, *made = ffn(mlp_w[rows - 1], carried, True)
    peers = list(range(1, group))
    part, out_part_own, gain_mlp_part = made[group - 1], made[2 * group - 1], made[2 * group]
    out_send = made[group:2 * group - 1]
    got = [to_member(v, s) for v, s in zip(made, peers)]
    mlp_sums[0].hop()
    mlp_sums[rows - 1] = Reduce(*go(lambda w, after: weight_grads(
        "mlp_grads", w, [mlp_normed, cotangent], [(0, [du]), (0, [dw]), (1, [m])], pieces, row_of=(1,), mixed=wide, after=after)), both_ways)
    dh, dh_low, dz_mine, dz_peers = go(
        close_feed_forward, share, group, part, got, hidden_row, inverse_mlp, gain_mlp, cotangent,
        w_out, out_mine, out_theirs,
    )
    dz_parts = [dz_mine]
    own_slots = rows * width
    for s in peers:
        lo = (group - s - 1) * own_slots
        dz_parts.append(here.fetch(dz_peers if group == 2 else dz_peers[:, lo:lo + own_slots], s, 0))
    mlp_sums[0].wait()
    mlp_own = mlp_sums[0].close()
    for j in turns:
        mlp_sums[j].hop()
    out_sum = Reduce(*go(lambda w, after: weight_grads(
        "out_grads", w, [dh_low], [(0, [gated[slot] for slot in slots])], pieces, True, after=after)), both_ways)

    back = {}
    attn_sums = {}
    per_step = together(heads) * HEAD

    def attend_back(j):
        q, k, v, g, forget, ccol, _ = mixed[j]
        parts = [(d, j * width // per_step) for d in dz_parts]
        if width % 128:
            parts = [(a[:, o * per_step:(o + 1) * per_step], 0) for a, o in parts]
        back[j] = go(attend_backward, q, k, v, g, gated[0, j], parts, logs[j], ccol, forget, scol, srow)

    def attn_grads(j, orders):
        attn_sums[j] = Reduce(*go(lambda w, after: weight_grads(
            "attn_grads", w, [normed], [(0, back[j][:2]), (0, back[j][2:5])], pieces, after=after)), orders)

    arrived = go.sync(*dz_parts[1:], *out_send)
    dz_parts[1:], out_send = arrived[:group - 1], arrived[group - 1:]
    out_got = [to_member(v, s) for v, s in zip(out_send, peers)]
    for j in turns:
        attend_back(j)
        attn_grads(j, both_ways)
    for j in turns:
        mlp_sums[j].hop()
    out_sum.hop()
    out_got = go.sync(*out_got)
    for j in turns:
        attn_sums[j].hop()
    for j in turns:
        mlp_sums[j].wait()
    mlp_other = [here.deliver(low(mlp_sums[j].close()), 0, j) for j in turns]
    attend_back(0)
    out_sum.hop()
    for j in turns:
        attn_sums[j].hop()
    attn_grads(0, both_ways)
    own_w = [w_query, w_key, w_value, w_outgate, w_forget]
    pair_terms = [
        (list(back[j][lo:hi]), *attn_w[j - 1][k]) for j in turns for k, (lo, hi) in enumerate(((0, 2), (2, 5)))
    ]

    def attn_back(name, steps):
        outs = []
        for s in steps:
            outs.append(go(lambda w, after: back_rows(
                name, w, s, group, list(back[0][:5]), own_w, pair_terms, normed, gain_attn, after)))
        return [o[0] for o in outs] + [sum(o[1] for o in outs)]

    mlp_other = go.sync(*mlp_other)
    for j in turns:
        attn_sums[j].wait()
    attn_other = [here.deliver(low(attn_sums[j].close()), 0, j) for j in turns]
    out_sum.wait()
    made = attn_back("attn_back_send", peers)
    got = [to_member(v, s) for v, s in zip(made, peers)]
    attn_sums[0].hop()
    out_part = out_sum.close().reshape(-1, group, rows, width)
    out_part = go.sync(out_part)[0]
    out_turned = [here.deliver(low(out_part[:, :, j]).reshape(-1, group * width), 0, j) for j in turns]
    part, gained = attn_back("attn_back_own", [0])
    bias_full = jnp.zeros((here.tensor, heads), f32)
    for j in range(rows):
        bias_full = lax.dynamic_update_slice(bias_full, back[j][5], (here.owner(here.at, 0, j), 0))
    small = jnp.concatenate([made[-1] + gained, gain_mlp_part, bias_full.reshape(1, -1)], axis=1)
    small_hops = [lambda v, b=b: here.swap(v, b) for b in [1] + here.bits] + [
        lambda v, b=b: lax.ppermute(v, "tensor", [(i, i ^ b) for i in range(here.tensor)])
        for b in [1 << k for k in range(here.tensor.bit_length() - 1)]]
    flying = small_hops.pop(0)(small)

    def small_step():
        arrived = go.sync(flying)[0]
        total = small + arrived
        return total, (small_hops.pop(0)(total) if small_hops else None)

    attn_other = go.sync(*attn_other)
    attn_sums[0].hop()
    small, flying = small_step()
    out_own, *arrived = go.sync(out_part_own, *out_got)
    output = lax.dynamic_slice_in_dim(hidden_row, member * share, share, 0) + out_own.astype(f32)
    for v in arrived:
        output = output + v.astype(f32)
    out_turned = go.sync(*out_turned, output)
    output = out_turned[-1]
    out_part = out_part[:, :, 0].reshape(-1, group * width) + sum(v.astype(f32) for v in out_turned[:-1])
    grad_out = out_part[:, :width]
    out_rest = [here.deliver(low(out_part[:, s * width:(s + 1) * width]), s, 0) for s in peers]
    small, flying = small_step()
    mlp_own, *mlp_other = go.sync(mlp_own, *mlp_other)
    attn_sums[0].wait()
    attn = attn_sums[0].close()
    while small_hops:
        small, flying = small_step()
    out_rest = go.sync(*out_rest)
    grad_inputs = go(close_block, share, group, part, got, inputs, inverse_attn, gain_attn, dh)
    small, flying = small_step()
    mlp = mlp_own
    for v in mlp_other:
        mlp = mlp + v.astype(f32)

    def columns(kind):
        return jnp.concatenate([mlp[:, b + kind * wide:b + (kind + 1) * wide] for b in range(0, 3 * hidden, 3 * wide)], axis=1)

    for v in out_rest:
        grad_out = grad_out + v.astype(f32)
    for v in attn_other:
        attn = attn + v.astype(f32)
    bias_own = lax.dynamic_slice_in_dim(small[0, 2 * model:], here.at * heads, heads, 0)
    return (
        output,
        grad_inputs,
        small[0, :model],
        attn[:, :width],
        attn[:, width:2 * width],
        attn[:, 2 * width:3 * width],
        attn[:, 3 * width:4 * width],
        attn[:, 4 * width:4 * width + heads],
        bias_own,
        grad_out,
        small[0, model:2 * model],
        columns(0),
        columns(1),
        columns(2),
    )


def solution(mesh):
    placed = (
        P("dp", None), P(), P(None, "tensor"), P(None, "tensor"), P(None, "tensor"),
        P(None, "tensor"), P(None, "tensor"), P("tensor"), P(None, "tensor"), P(),
        P(None, "tensor"), P(None, "tensor"), P(None, "tensor"), P("dp", None), P("dp", None),
    )
    weight = P("dp", "tensor")
    tokens = P(("dp", "tensor"), None)
    return jax.shard_map(
        on_device,
        mesh=mesh,
        in_specs=placed,
        out_specs=(
            tokens, tokens, P(), weight, weight, weight, weight, weight, P("tensor"),
            weight, P(), weight, weight, weight,
        ),
        check_vma=False,
    )
```

```python
import jax
import jax.numpy as jnp
from jax import lax
from jax.sharding import PartitionSpec as P
from jax.experimental import pallas as pl
from jax.experimental.pallas import tpu as pltpu

LOG2E = 1.4426950408889634
LN2 = 0.6931471805599453
HEAD = 64
BLK = 256
EPS = 1e-06
STEP = 115 * 10 ** 9
ROW, MEMBER, CORE, CHIP, PIECE = 0, 1, 2, 3, 4
f32 = jnp.float32
bf16 = jnp.bfloat16


def last(a, b):
    return lax.dot_general(a, b, (((1,), (1,)), ((), ())), preferred_element_type=f32)


def first(a, b):
    return lax.dot_general(a, b, (((0,), (0,)), ((), ())), preferred_element_type=f32)


def mm(a, b):
    return jnp.dot(a, b, preferred_element_type=f32)


def low(values):
    return values.astype(bf16)


def shape(dims, dtype):
    return jax.ShapeDtypeStruct(dims, dtype)


def spec(block, at, mode=None):
    if block is None:
        return pl.BlockSpec(memory_space=pl.ANY)
    return pl.BlockSpec(block, at) if mode is None else pl.BlockSpec(block, at, pipeline_mode=mode)


def run(name, body, where, grid, ins, outs, scratch=(), after=(), flops=0, vmem=56):
    count, extra, made = len(ins), len(after), len(outs)

    def kernel(where_ref, *refs):
        body(where_ref, refs[:count], refs[count + extra:count + extra + made], refs[count + extra + made:])

    return pl.pallas_call(
        kernel,
        grid_spec=pltpu.PrefetchScalarGridSpec(
            num_scalar_prefetch=1,
            grid=grid,
            in_specs=[spec(*entry[1:]) for entry in ins] + [pl.BlockSpec(memory_space=pl.ANY)] * extra,
            out_specs=[spec(*entry[1:]) for entry in outs],
            scratch_shapes=list(scratch),
        ),
        out_shape=[entry[0] for entry in outs],
        compiler_params=pltpu.CompilerParams(vmem_limit_bytes=vmem << 20),
        cost_estimate=pl.CostEstimate(flops=STEP, bytes_accessed=1, transcendentals=0),
        name=name,
    )(where, *[entry[0] for entry in ins], *after)


class Part:
    def __init__(self, array, rows=None, row_at=None, cols=None, col_at=None, into=None):
        self.array = array
        self.rows = array.shape[0] if rows is None else rows
        self.cols = array.shape[1] if cols is None else cols
        self.row_at, self.col_at = row_at, col_at
        self.into = into

    def view(self, ref, w):
        if self.row_at is None and self.col_at is None:
            return ref
        row = 0 if self.row_at is None else pl.multiple_of(self.row_at(w), self.rows)
        col = 0 if self.col_at is None else pl.multiple_of(self.col_at(w), self.cols)
        return ref.at[pl.ds(row, self.rows), pl.ds(col, self.cols)]


def stream(name, body, where, parts, outs, scratch=(), after=(), buffers=()):
    count, extra, made = len(parts), len(after), len(outs)
    single = [p for p in parts if p.into is None]
    chunks = 16

    def kernel(w, *refs):
        sources = refs[:count]
        targets = refs[count + extra:count + extra + made]
        at = count + extra + made
        shared = refs[at:at + len(buffers)]
        at += len(buffers)
        alone = iter(refs[at:at + len(single)])
        held = [next(alone) if p.into is None else shared[p.into[0]].at[
            pl.ds(p.into[1](w) if callable(p.into[1]) else p.into[1], p.rows), pl.ds(p.into[2], p.cols)] for p in parts]
        at += len(single)
        ready = refs[at:at + made]
        in_sems, out_sems = refs[at + made:at + made + 2]
        rest = shared + refs[at + made + 2:]
        loads = []
        for k, part in enumerate(parts):
            copy = pltpu.make_async_copy(part.view(sources[k], w), held[k], in_sems.at[k])
            copy.start()
            loads.append(copy)
        waited = set()
        sent = []

        def get(k):
            if k not in waited:
                loads[k].wait()
                waited.add(k)
            return held[k]

        def put(k, row=None, rows=None, col=None, cols=None):
            spot = (pl.ds(0, outs[k].shape[0]) if row is None else pl.ds(row, rows),
                    pl.ds(0, outs[k].shape[1]) if col is None else pl.ds(col, cols))
            copy = pltpu.make_async_copy(ready[k].at[spot], targets[k].at[spot], out_sems.at[k, len([1 for i, _ in sent if i == k])])
            copy.start()
            sent.append((k, copy))

        body(w, get, ready, put, rest)
        for _, copy in sent:
            copy.wait()

    return pl.pallas_call(
        kernel,
        grid_spec=pltpu.PrefetchScalarGridSpec(
            num_scalar_prefetch=1, grid=(),
            in_specs=[pl.BlockSpec(memory_space=pl.ANY)] * (count + extra),
            out_specs=[pl.BlockSpec(memory_space=pl.ANY)] * made,
            scratch_shapes=[pltpu.VMEM(b, bf16) for b in buffers]
            + [pltpu.VMEM((p.rows, p.cols), p.array.dtype) for p in single]
            + [pltpu.VMEM(o.shape, o.dtype) for o in outs]
            + [pltpu.SemaphoreType.DMA((count,)), pltpu.SemaphoreType.DMA((made, chunks))] + list(scratch),
        ),
        out_shape=list(outs),
        compiler_params=pltpu.CompilerParams(vmem_limit_bytes=58 << 20),
        cost_estimate=pl.CostEstimate(flops=STEP, bytes_accessed=1, transcendentals=0),
        name=name,
    )(where, *[p.array for p in parts], *after)


def fixed(array):
    return (array, array.shape, lambda i, w: (0,) * array.ndim)


def fixed_out(dims, dtype):
    return (shape(dims, dtype), dims, lambda i, w: (0,) * len(dims))


def halves(values, pieces, core):
    count = values.shape[0] // pieces
    even = jnp.concatenate([values[p * count:(p + 1) * count] for p in range(0, pieces, 2)], axis=0)
    odd = jnp.concatenate([values[p * count:(p + 1) * count] for p in range(1, pieces, 2)], axis=0)
    return jnp.where(core == 0, odd, even), jnp.where(core == 0, even, odd)


def three(values):
    top = low(values)
    rest = values - top.astype(f32)
    middle = low(rest)
    return top, middle, low(rest - middle.astype(f32))


def log_keep(values):
    return jnp.minimum(values, 0.0) - jnp.log1p(jnp.exp(-jnp.abs(values)))


def lower(flip=False):
    r = lax.broadcasted_iota(jnp.int32, (BLK, BLK), 0)
    c = lax.broadcasted_iota(jnp.int32, (BLK, BLK), 1)
    return jnp.where(r <= c if flip else r >= c, 1.0, 0.0).astype(bf16)


TOK = 512


def project_tail(i, mixed, width, bias, outs, carry):
    q_ref, k_ref, v_ref, g_ref, f_ref, ccol_ref, crow_ref = outs
    q_ref[...] = low(mixed[:, :width] * (HEAD ** -0.5 * LOG2E))
    for p, ref in ((1, k_ref), (2, v_ref), (3, g_ref)):
        ref[...] = low(mixed[:, p * width:(p + 1) * width])
    heads = f_ref.shape[1]
    forget = mixed[:, 4 * width:4 * width + heads] + bias
    f_ref[...] = forget

    @pl.when(i == 0)
    def _():
        carry[...] = jnp.zeros_like(carry)

    mask = lower()
    hp = crow_ref.shape[1]
    tokens = forget.shape[0]
    for t in range(tokens // BLK):
        rows = slice(t * BLK, (t + 1) * BLK)
        wide = jnp.concatenate([log_keep(forget[rows]) * LOG2E, jnp.zeros((BLK, 128 - heads), f32)], axis=1)
        sums = sum(mm(mask, part) for part in three(wide)) + carry[0:1, :]
        carry[0:1, :] = sums[BLK - 1:BLK, :]
        ccol_ref[rows, :] = sums[:, :heads]
        flat = sums.T
        for s in range(crow_ref.shape[0]):
            crow_ref[s, :, rows] = flat[s * hp:(s + 1) * hp, :]


def together(heads):
    return 2 if heads % 2 == 0 else heads


def project_outs(length, width, heads):
    tokens = lambda i, w: (i, 0)
    return [(shape((length, width), bf16), (TOK, width), tokens) for _ in range(4)] + [
        (shape((length, heads), f32), (TOK, heads), tokens),
        (shape((length, heads), f32), (TOK, heads), tokens),
        (shape((heads // together(heads), together(heads), length), f32),
         (heads // together(heads), together(heads), TOK), lambda i, w: (0, 0, i)),
    ]


def project_own(where, length, inputs, gain, weights, bias, after=()):
    model = inputs.shape[1]
    width, heads = weights[0].shape[1], weights[4].shape[1]

    def body(w, ins, outs, scratch):
        x_ref, gain_ref, wq, wk, wv, wg, wf, b_ref = ins
        a_ref, inv_ref = outs[:2]
        x = x_ref[...].astype(f32)
        inverse = lax.rsqrt(jnp.mean(x * x, axis=1, keepdims=True) + EPS)
        a = low(x * inverse * gain_ref[...])
        a_ref[...] = a
        inv_ref[...] = inverse
        mixed = mm(a, jnp.concatenate([r[...] for r in (wq, wk, wv, wg, wf)], axis=1))
        project_tail(pl.program_id(0), mixed, width, b_ref[...], outs[2:], scratch[0])

    blocks = length // TOK
    tokens = lambda i, w: (i, 0)
    return run(
        "project_own", body, where, (blocks,),
        [(inputs, (TOK, model), lambda i, w: (w[ROW] * blocks + i, 0)), fixed(gain)]
        + [fixed(a) for a in weights] + [fixed(bias)],
        [(shape((length, model), bf16), (TOK, model), tokens), (shape((length, 1), f32), (TOK, 1), tokens)]
        + project_outs(length, width, heads),
        [pltpu.VMEM((8, 128), f32)], after, 2 * length * model * (4 * width + heads),
    )


def core_halves(ref, w, half):
    return (ref[:, pl.ds(pl.multiple_of(w[CORE] * half, 128), half)],
            ref[:, pl.ds(pl.multiple_of((1 - w[CORE]) * half, 128), half)])


def project_other(where, normed, gathered, counts, width, heads, bias, after=()):
    length, model = normed.shape
    half = model // 2

    def body(w, ins, outs, scratch):
        a_ref, b_ref = ins[:2]
        am, at = core_halves(a_ref, w, half)
        mixed = [mm(am, ins[2 + 2 * k][:, :n]) + mm(at, ins[3 + 2 * k][:, :n]) for k, n in enumerate(counts)]
        project_tail(pl.program_id(0), jnp.concatenate(mixed, axis=1), width, b_ref[...], outs, scratch[0])

    return run(
        "project_other", body, where, (length // TOK,),
        [(normed, (TOK, model), lambda i, w: (i, 0)), fixed(bias)] + [fixed(a) for pair in gathered for a in pair],
        project_outs(length, width, heads),
        [pltpu.VMEM((8, 128), f32)], after, 2 * length * model * (4 * width + heads),
    )


def attend_forward(where, q, k, v, g, crow, scol, srow, after=()):
    length, n = q.shape
    heads = n // HEAD
    hp = together(heads)
    width = hp * HEAD

    def body(w, ins, outs, scratch):
        q_ref, k_ref, v_ref, g_ref, crow_ref, scol_ref, srow_ref = ins
        z_ref, lse_ref = outs
        lane = lax.broadcasted_iota(jnp.int32, (1, width), 1) // HEAD
        lane1 = lax.broadcasted_iota(jnp.int32, (BLK, 128), 1)
        tri = lax.broadcasted_iota(jnp.int32, (BLK, BLK), 0) >= lax.broadcasted_iota(jnp.int32, (BLK, BLK), 1)
        crows = crow_ref[0]
        v_wide = jnp.concatenate([v_ref[...], jnp.ones((length, 128), bf16)], axis=1)
        for i in range(length // BLK):
            rows = pl.ds(i * BLK, BLK)
            reach = (i + 1) * BLK
            q = q_ref[rows, :]
            same = scol_ref[rows, :] == srow_ref[:, :reach]
            if i:
                allowed = jnp.concatenate([same[:, :reach - BLK], same[:, reach - BLK:] & tri], axis=1)
            else:
                allowed = same & tri
            scores = last(jnp.concatenate([jnp.where(lane == h, q, 0) for h in range(hp)], axis=0), k_ref[:reach, :])
            tops, grown = [], []
            for h in range(hp):
                s = jnp.where(allowed, scores[h * BLK:(h + 1) * BLK] - crows[h:h + 1, :reach], -1e30)
                top = jnp.max(s, axis=1, keepdims=True)
                tops.append(top)
                grown.append(low(jnp.exp2(s - top)))
            parts = mm(jnp.concatenate(grown, axis=0), v_wide[:reach, :])
            out = jnp.zeros((BLK, width), f32)
            stats = jnp.zeros((BLK, 128), f32)
            for h in range(hp):
                part = parts[h * BLK:(h + 1) * BLK]
                total = part[:, width:width + 1]
                out = jnp.where(lane == h, part[:, :width] * (1.0 / total), out)
                stats = jnp.where(lane1 == h, tops[h] + jnp.log2(total), stats)
            z_ref[rows, :] = low(out * jax.nn.sigmoid(g_ref[rows, :].astype(f32)))
            lse_ref[0, :, i * BLK:(i + 1) * BLK] = stats.T[:hp, :]

    tokens = lambda i, w: (0, i)
    return run(
        "attend_forward", body, where, (heads // hp,),
        [(a, (length, width), tokens) for a in (q, k, v, g)]
        + [(crow, (1, hp, length), lambda i, w: (i, 0, 0)), fixed(scol), fixed(srow)],
        [(shape((length, n), bf16), (length, width), tokens),
         (shape((heads // hp, hp, length), f32), (1, hp, length), lambda i, w: (i, 0, 0))],
        (), after, heads * length * length * 1100,
    )


def attend_backward(where, q, k, v, g, z, dz_parts, lse, ccol, forget, scol, srow, after=()):
    length, n = q.shape
    heads = n // HEAD
    hp = together(heads)
    width = hp * HEAD
    steps = heads // hp
    group = len(dz_parts)
    share = length // group

    def body(w, ins, outs, scratch):
        q_ref, k_ref, v_ref, g_ref, z_ref = ins[:5]
        dz_refs = ins[5:5 + group]
        lse_ref, ccol_ref, f_ref, scol_ref, srow_ref = ins[5 + group:]
        dq_ref, dk_ref, dv_ref, dg_ref, df_ref, db_ref = outs
        dqacc, rates, dzfull = scratch
        step = pl.program_id(0)
        lane = lax.broadcasted_iota(jnp.int32, (1, width), 1) // HEAD
        lane1 = lax.broadcasted_iota(jnp.int32, (1, 128), 1)
        tri = lax.broadcasted_iota(jnp.int32, (BLK, BLK), 1) >= lax.broadcasted_iota(jnp.int32, (BLK, BLK), 0)
        blocks = length // BLK

        @pl.when(step == 0)
        def _():
            rates[...] = jnp.zeros_like(rates)

        for s in range(group):
            at = lax.rem(w[MEMBER] + s, group) * share
            dzfull[pl.ds(pl.multiple_of(at, share), share), :] = dz_refs[s][...]
        sig = jax.nn.sigmoid(g_ref[...].astype(f32))
        dz = dzfull[...].astype(f32)
        prod = dz * z_ref[...].astype(f32)
        dout = low(dz * sig)
        dg_ref[...] = low(prod * (1.0 - sig))
        prod_hi = low(prod)
        prod_lo = low(prod - prod_hi.astype(f32))
        lses = lse_ref[0]
        chosen = lax.broadcasted_iota(jnp.int32, (8, width), 0) == lax.broadcasted_iota(jnp.int32, (8, width), 1) // HEAD
        chosen = jnp.where(chosen, 1.0, 0.0).astype(bf16)
        centres = last(chosen, prod_hi) + last(chosen, prod_lo)
        ones = jnp.ones((length, 128), bf16)
        q_wide = jnp.concatenate([q_ref[...], ones], axis=1)
        k_wide = jnp.concatenate([k_ref[...], ones], axis=1)
        decays = [
            jnp.sum(jnp.where(lane1[:, :heads] == step * hp + h, ccol_ref[...], 0.0), axis=1, keepdims=True)
            for h in range(hp)
        ]
        dqacc[...] = jnp.zeros_like(dqacc)
        for j in range(blocks):
            keys = pl.ds(j * BLK, BLK)
            lo = j * BLK
            count = length - lo
            keyed = lambda ref: jnp.concatenate([jnp.where(lane == h, ref[keys, :], 0) for h in range(hp)], axis=0)
            scores = last(keyed(k_ref), q_ref[lo:, :])
            dps = last(keyed(v_ref), dout[lo:, :])
            same = scol_ref[keys, :] == srow_ref[:, lo:]
            if j < blocks - 1:
                allowed = jnp.concatenate([same[:, :BLK] & tri, same[:, BLK:]], axis=1)
            else:
                allowed = same & tri
            ps, dss = [], []
            for h in range(hp):
                rows = slice(h * BLK, (h + 1) * BLK)
                s = scores[rows] - decays[h][lo:lo + BLK, :] - lses[h:h + 1, lo:]
                p = jnp.exp2(jnp.where(allowed, s, -1e30))
                ps.append(low(p))
                dss.append(low(p * (dps[rows] - centres[h:h + 1, lo:])))
            dvs = mm(jnp.concatenate(ps, axis=0), dout[lo:, :])
            dks = mm(jnp.concatenate(dss, axis=0), q_wide[lo:, :])
            dqs = first(jnp.concatenate(dss, axis=1), k_wide[lo:lo + BLK, :])
            dk = jnp.zeros((BLK, width), f32)
            dv = jnp.zeros((BLK, width), f32)
            for h in range(hp):
                rows = slice(h * BLK, (h + 1) * BLK)
                dk = jnp.where(lane == h, dks[rows, :width], dk)
                dv = jnp.where(lane == h, dvs[rows], dv)
                rates[keys, :] = jnp.where(lane1 == step * hp + h, -dks[rows, width:width + 1], rates[keys, :])
                dqacc[h * length + lo:(h + 1) * length, :] += dqs[h * count:(h + 1) * count]
            dk_ref[keys, :] = low(dk * LN2)
            dv_ref[keys, :] = low(dv)
        dq = jnp.zeros((length, width), f32)
        for h in range(hp):
            part = dqacc[h * length:(h + 1) * length, :]
            dq = jnp.where(lane == h, part[:, :width], dq)
            rates[...] = jnp.where(lane1 == step * hp + h, rates[...] + part[:, width:width + 1], rates[...])
        dq_ref[...] = low(dq * HEAD ** -0.5)

        @pl.when(step == steps - 1)
        def _():
            mask = lower(True)
            carry = jnp.zeros((1, 128), f32)
            bias = jnp.zeros((1, heads), f32)
            for b in reversed(range(blocks)):
                rows = pl.ds(b * BLK, BLK)
                sums = sum(mm(mask, part) for part in three(rates[rows, :])) + carry
                carry = sums[0:1, :]
                df = low(sums[:, :heads] * jax.nn.sigmoid(-f_ref[rows, :]))
                df_ref[rows, :] = df
                bias = bias + jnp.sum(df.astype(f32), axis=0, keepdims=True)
            db_ref[...] = bias

    tokens = lambda i, w: (0, i)
    wide = (shape((length, n), bf16), (length, width), tokens)
    return run(
        "attend_backward", body, where, (steps,),
        [(a, (length, width), tokens) for a in (q, k, v, g, z)]
        + [(a, (share, width), lambda i, w, off=off: (0, off + i)) for a, off in dz_parts]
        + [(lse, (1, hp, length), lambda i, w: (i, 0, 0))] + [fixed(a) for a in (ccol, forget, scol, srow)],
        [wide] * 4 + [fixed_out((length, heads), bf16), fixed_out((1, heads), f32)],
        [pltpu.VMEM((hp * length, width + 128), f32), pltpu.VMEM((length, 128), f32), pltpu.VMEM((length, width), bf16)],
        after, heads * length * length * 1500,
    )


def close_attention(where, length, inputs, gated, out_own, out_mine, out_theirs, gain, after=()):
    model = inputs.shape[1]
    half = model // 2
    width = out_own.shape[1]

    def body(w, ins, outs, scratch):
        x_ref, own_ref, m_ref, t_ref, gain_ref = ins[:5]
        z = jnp.concatenate([r[...] for r in ins[5:]], axis=1)
        h_ref, a_ref, inv_ref = outs
        for ref, core in ((m_ref, w[CORE]), (t_ref, 1 - w[CORE])):
            at = pl.ds(pl.multiple_of(core * half, 128), half)
            own = own_ref[pl.ds(pl.multiple_of(core * half, 128), half), :]
            rest = ref[:, :(len(gated) - 1) * width]
            h_ref[:, at] = x_ref[:, at].astype(f32) + last(z, jnp.concatenate([own, rest], axis=1))
        h = h_ref[...]
        inverse = lax.rsqrt(jnp.mean(h * h, axis=1, keepdims=True) + EPS)
        a = low(h * inverse * gain_ref[...])
        a_ref[...] = a
        inv_ref[...] = inverse

    blocks = length // TOK
    tokens = lambda i, w: (i, 0)
    return run(
        "close_attention", body, where, (blocks,),
        [(inputs, (TOK, model), lambda i, w: (w[ROW] * blocks + i, 0))]
        + [fixed(a) for a in (out_own, out_mine, out_theirs, gain)]
        + [(z, (TOK, width), tokens) for z in gated],
        [(shape((length, model), f32), (TOK, model), tokens), (shape((length, model), bf16), (TOK, model), tokens),
         (shape((length, 1), f32), (TOK, 1), tokens)],
        (), after, 2 * length * model * width * len(gated),
    )


def once(array_or_shape, block, at):
    return (array_or_shape, block, at, pl.Buffered(1))


def feed_forward(where, normed, cotangent, weights, hidden, gain, group, pieces, before, final, after=()):
    length, model = normed.shape
    half = model // 2
    share = length // group
    wide = BLK if hidden % BLK == 0 else hidden
    steps = hidden // wide
    own = len(weights) == 3
    tokens = length // TOK

    def body(w, ins, outs, scratch):
        a_ref, e_ref, gain_ref = ins[:3]
        blocks = ins[3:3 + (3 if own else 6)]
        rest = ins[3 + len(blocks):]
        back, out = scratch[:2]
        kept = scratch[2:5]
        step = pl.program_id(0)
        core = pl.ds(pl.multiple_of(w[CORE] * half, 128), half)
        other = pl.ds(pl.multiple_of((1 - w[CORE]) * half, 128), half)
        copies = [pltpu.make_async_copy(r, scratch[5 + k], scratch[5 + len(rest)].at[k]) for k, r in enumerate(rest)]

        @pl.when(step == 0)
        def _():
            for c in copies:
                c.start()
            back[...] = jnp.zeros_like(back)
            out[...] = jnp.zeros_like(out)

        for t in range(tokens):
            rows = pl.ds(t * TOK, TOK)
            if own:
                gate, up = mm(a_ref[rows, :], blocks[0][...]), mm(a_ref[rows, :], blocks[1][...])
                dm = mm(e_ref[rows, :], blocks[2][...])
            else:
                both = lambda ref, p: mm(ref[rows, core], blocks[p][...]) + mm(ref[rows, other], blocks[3 + p][...])
                gate, up, dm = both(a_ref, 0), both(a_ref, 1), both(e_ref, 2)
            sig = jax.nn.sigmoid(gate)
            act = gate * sig
            values = (low(dm * up * (sig * (1.0 + gate * (1.0 - sig)))), low(dm * act), low(act * up))
            for k, value in enumerate(values):
                kept[k][rows, :] = value
                if final:
                    outs[k][rows, :] = value
        du, dw, m = kept
        if own:
            back[...] += last(du[...], blocks[0][...]) + last(dw[...], blocks[1][...])
            out[...] += last(m[...], blocks[2][...])
        else:
            for where_to, p in ((core, 0), (other, 3)):
                back[:, where_to] += last(du[...], blocks[p][...]) + last(dw[...], blocks[p + 1][...])
                out[:, where_to] += last(m[...], blocks[p + 2][...])
        if not final:
            for k, left in enumerate((a_ref, a_ref, e_ref)):
                send, keep = halves(low(first(left[...], kept[k][...])), pieces, w[CORE])
                outs[0][:, k * wide:(k + 1) * wide] = send
                outs[1][:, k * wide:(k + 1) * wide] = keep

        @pl.when(step == steps - 1)
        def _():
            for c in copies:
                c.wait()
            if rest:
                back[...] += scratch[5][...].astype(f32)
                out[...] += scratch[6][...].astype(f32)
            if final:
                for k in range(group):
                    member = lax.rem(w[MEMBER] + (k + 1) % group, group)
                    rows = pl.ds(pl.multiple_of(member * share, share), share)
                    outs[3 + k][...] = low(back[rows, :])
                    outs[3 + group + k][...] = low(out[rows, :])
                outs[3 + 2 * group][...] = jnp.sum(back[...] * a_ref[...].astype(f32), axis=0, keepdims=True) / gain_ref[...]
            else:
                outs[2][...] = low(back[...])
                outs[3][...] = low(out[...])

    whole = lambda i, w: (0, 0)
    column = lambda i, w: (0, i)
    if own:
        parts = [(a, (model, wide), column) for a in weights]
    else:
        gm, gt, dm, dt = weights
        parts = [(a, (half, wide), lambda i, w, p=p: (0, p * steps + i))
                 for a, p in ((gm, 0), (gm, 1), (dm, 0), (gt, 0), (gt, 1), (dt, 0))]
    row_sum = once(shape((length, model), bf16), (length, model), whole)
    if final:
        outs = [(shape((length, hidden), bf16), (length, wide), column)] * 3
        outs += [once(shape((share, model), bf16), (share, model), whole)] * (2 * group)
        outs += [fixed_out((1, model), f32)]
    else:
        side = (shape((half, 3 * hidden), bf16), (half, 3 * wide), column)
        outs = [side, side, row_sum, row_sum]
    return run(
        "feed_forward", body, where, (steps,),
        [once(normed, (length, model), whole), once(cotangent, (length, model), lambda i, w: (w[ROW], 0)), fixed(gain)] + parts
        + [(a, None, None) for a in before],
        outs,
        [pltpu.VMEM((length, model), f32)] * 2 + [pltpu.VMEM((length, wide), bf16)] * 3
        + [pltpu.VMEM((length, model), bf16) for _ in before]
        + ([pltpu.SemaphoreType.DMA((len(before),))] if before else []),
        after,
    )


def weight_grads(name, where, lefts, groups, pieces, rows_of=False, row_of=(), mixed=0, after=()):
    length = groups[0][1][0].shape[0] if not rows_of else lefts[0].shape[0]
    half = lefts[0].shape[1] // 2
    widths = [sum(r.shape[1] for r in rights) for _, rights in groups]
    padded = [-(-n // 128) * 128 for n in widths]
    padded[-1] += -sum(padded) % 256
    parts, plan, loaded = [], [], {}
    row_at = (lambda w: w[MEMBER] * length) if rows_of else None
    for k, (s, rights) in enumerate(groups):
        if s not in loaded:
            loaded[s] = len(parts)
            parts.append(Part(lefts[s], length, (lambda w: w[ROW] * length) if s in row_of else None))
        at = []
        for r in rights:
            at.append(len(parts))
            parts.append(Part(r, length, row_at, r.shape[1]))
        plan.append((loaded[s], at, sum(padded[:k]), widths[k], padded[k]))

    def body(w, get, ready, put, rest):
        for k, (left, at, col, n, full) in enumerate(plan):
            left = get(left)[...]
            right = [get(k)[...] for k in at]
            value = low(first(left, right[0] if len(right) == 1 else jnp.concatenate(right, axis=1)))
            for which, part in enumerate(halves(value, pieces, w[CORE])):
                if mixed:
                    for b in range(n // mixed):
                        spot = (b * len(plan) + k) * mixed
                        ready[which][:, spot:spot + mixed] = part[:, b * mixed:(b + 1) * mixed]
                        put(which, col=spot, cols=mixed)
                    continue
                ready[which][:, col:col + n] = part
                if n < full:
                    ready[which][:, col + n:col + full] = jnp.zeros((half, full - n), bf16)
                put(which, col=col, cols=full)

    return stream(name, body, where, parts, [shape((half, sum(padded)), bf16)] * 2, (), after)


def fold(where, entries, after=()):
    keep, _, bits, _, _, width = entries[0]
    rows = keep.shape[0]
    count = len(bits)
    pieces = 1 << count
    piece = rows // pieces
    wide = next(n for n in (768, 512, 384, width) if width % n == 0)
    across = width // wide
    block = (piece, wide)
    ins, outs = [], []
    for keep, got, bits, bit_at, col, _ in entries:
        place = count - 1 - bits.index(bit_at)

        def index(mine, place=place, bit_at=bit_at, col=col):
            def at(i, c, w):
                own = lax.rem(w[CHIP] // (bit_at >> 1), 2)
                bit = own if mine else 1 - own
                low_part = lax.rem(i, 1 << place)
                high = i // (1 << place)
                return ((high * 2 + bit) * (1 << place) + low_part, col * across + c)
            return at

        for mine in (False, True):
            ins += [(keep, block, index(mine)), (got, block, index(mine))]
            outs.append((shape((rows // 2, width), bf16), block, lambda i, c, w: (i, c)))

    def body(w, ins_, outs_, scratch):
        for k, out in enumerate(outs_):
            out[...] = ins_[2 * k][...] + ins_[2 * k + 1][...]

    return run("fold", body, where, (pieces // 2, across), ins, outs, (), after, 10 ** 9)


def assemble(where, pieces, masks, after=()):
    count, extra = len(pieces), len(after)
    rows, width = pieces[0].shape

    def kernel(w, *refs):
        out, held, sems = refs[count + extra:]
        loads = [pltpu.make_async_copy(refs[k], held.at[k], sems.at[0, k]) for k in range(count)]
        for c in loads:
            c.start()
        stores = []
        for k in range(count):
            loads[k].wait()
            at = pl.multiple_of(jnp.bitwise_xor(w[CHIP], masks[k]) * rows, rows)
            stores.append(pltpu.make_async_copy(held.at[k], out.at[pl.ds(at, rows), :], sems.at[1, k]))
            stores[k].start()
        for c in stores:
            c.wait()

    return pl.pallas_call(
        kernel,
        grid_spec=pltpu.PrefetchScalarGridSpec(
            num_scalar_prefetch=1, grid=(),
            in_specs=[pl.BlockSpec(memory_space=pl.ANY)] * (count + extra),
            out_specs=pl.BlockSpec(memory_space=pl.ANY),
            scratch_shapes=[pltpu.VMEM((count, rows, width), bf16), pltpu.SemaphoreType.DMA((2, count))],
        ),
        out_shape=shape((count * rows, width), bf16),
        compiler_params=pltpu.CompilerParams(vmem_limit_bytes=56 << 20),
        cost_estimate=pl.CostEstimate(flops=STEP, bytes_accessed=1, transcendentals=0),
        name="assemble",
    )(where, *pieces, *after)


def back_rows(name, where, step, group, own_x, own_w, pair_terms, normed, gain, after=()):
    length, model = normed.shape
    half = model // 2
    share = length // group
    member = lambda w: lax.rem(w[MEMBER] + step, group)
    row_at = lambda w: member(w) * share
    parts, tails, cuts = [], [], []
    col = 0

    def lay(arrays, buffer, narrow):
        at = col
        for a in arrays:
            n = a.shape[1]
            rows, pick = (share, row_at) if buffer == 0 else (a.shape[0], None)
            if n % 128 == 0 and at % 128 == 0:
                parts.append(Part(a, rows, pick, n, None, (buffer, 0, at)))
            else:
                tails.append((len(parts), buffer, at, n))
                parts.append(Part(a, rows, pick, n))
            at += n
        return at

    if any(a.shape[1] % 128 for a in own_x[:-1]):
        own_x, own_w = [jnp.concatenate(own_x, axis=1)], [jnp.concatenate(own_w, axis=1)]
        pair_terms = [([jnp.concatenate(xs, axis=1)], mine, theirs) for xs, mine, theirs in pair_terms]
    lay(own_x, 0, True)
    end = lay(own_w, 1, True)
    full = -(-end // 128) * 128
    cuts.append((0, len(parts), 0, full))
    col = full
    for xs, mine, theirs in pair_terms:
        first_part = len(parts)
        lay(xs, 0, True)
        n = mine.shape[1]
        parts.append(Part(mine, into=(1, lambda w: pl.multiple_of(w[CORE] * half, half), col)))
        parts.append(Part(theirs, into=(1, lambda w: pl.multiple_of((1 - w[CORE]) * half, half), col)))
        cuts.append((first_part, len(parts), col, n))
        col += n
    unit_at = len(parts)
    parts.append(Part(normed, share, row_at))
    parts.append(Part(gain))

    def body(w, get, ready, put, rest):
        x_all, w_all = rest[:2]
        for low_part, high_part, at, n in cuts:
            for k in range(low_part, high_part):
                get(k)
            for k, buffer, spot, count in tails:
                if low_part <= k < high_part:
                    target = (x_all, w_all)[buffer]
                    last_col = at + n if spot + count <= at + n else spot + count
                    value = get(k)[...]
                    fill = jnp.zeros((value.shape[0], last_col - spot - count), bf16)
                    target[:, spot:last_col] = jnp.concatenate([value, fill], axis=1) if last_col > spot + count else value
            part = last(x_all[:, at:at + n], w_all[:, at:at + n])
            rest[2][...] = part if at == 0 else rest[2][...] + part
        total = rest[2][...]
        ready[0][...] = low(total)
        put(0)
        u = get(unit_at)[...].astype(f32)
        ready[1][...] = jnp.sum(total * u, axis=0, keepdims=True) / get(unit_at + 1)[...]
        put(1)

    return stream(
        name, body, where, parts, [shape((share, model), bf16), shape((1, model), f32)],
        [pltpu.VMEM((share, model), f32)], after, [(share, col), (model, col)],
    )


def close_feed_forward(where, share, group, part, got, hidden_row, inverse, gain, cotangent,
                       out_own, out_mine, out_theirs, after=()):
    model = part.shape[1]
    half = model // 2
    width = out_own.shape[1]
    filled = width + out_mine.shape[1]
    own_slots = filled // group

    def body(w, ins, outs, scratch):
        p_ref, h_ref, i_ref, gain_ref, e_ref, own_ref, m_ref, t_ref = ins[:8]
        dh_ref, low_ref, mine_out, peer_out = outs
        total = p_ref[...].astype(f32)
        for r in ins[8:]:
            total = total + r[...].astype(f32)
        unit = h_ref[...] * i_ref[...]
        scaled = total * gain_ref[...]
        dh = e_ref[...].astype(f32) + i_ref[...] * (scaled - unit * jnp.mean(scaled * unit, axis=1, keepdims=True))
        dh_ref[...] = dh
        d = low(dh)
        low_ref[...] = d
        dz = 0.0
        for d_half, ref, core in zip(core_halves(low_ref, w, half), (m_ref, t_ref), (w[CORE], 1 - w[CORE])):
            own = own_ref[pl.ds(pl.multiple_of(core * half, 128), half), :]
            dz = dz + mm(d_half, jnp.concatenate([own, ref[...]], axis=1))
        mine_out[...] = low(dz[:, :own_slots])
        peer_out[...] = low(dz[:, own_slots:])

    whole = lambda i, w: (0, 0)
    mine = lambda i, w: (w[MEMBER], 0)
    return run(
        "close_feed_forward", body, where, (1,),
        [fixed(part), (hidden_row, (share, model), mine), (inverse, (share, 1), mine), fixed(gain),
         (cotangent, (share, model), lambda i, w: (w[ROW] * group + w[MEMBER], 0)),
         fixed(out_own), fixed(out_mine), fixed(out_theirs)] + [fixed(a) for a in got],
        [(shape((share, model), f32), (share, model), whole), (shape((share, model), bf16), (share, model), whole),
         (shape((share, own_slots), bf16), (share, own_slots), whole),
         (shape((share, filled - own_slots), bf16), (share, filled - own_slots), whole)],
        (), after, 2 * share * model * filled,
    )


def close_block(where, share, group, part, got, inputs, inverse, gain, dh, after=()):
    model = part.shape[1]
    step_rows = min(BLK, share)
    blocks = share // step_rows
    row_blocks = group * blocks

    def body(w, ins, outs, scratch):
        p_ref, x_ref, i_ref, gain_ref, dh_ref = ins[:5]
        total = p_ref[...].astype(f32)
        for r in ins[5:]:
            total = total + r[...].astype(f32)
        unit = x_ref[...].astype(f32) * i_ref[...]
        scaled = total * gain_ref[...]
        outs[0][...] = dh_ref[...] + i_ref[...] * (scaled - unit * jnp.mean(scaled * unit, axis=1, keepdims=True))

    tokens = lambda i, w: (i, 0)
    return run(
        "close_block", body, where, (blocks,),
        [(part, (step_rows, model), tokens),
         (inputs, (step_rows, model), lambda i, w: (w[ROW] * row_blocks + w[MEMBER] * blocks + i, 0)),
         (inverse, (step_rows, 1), lambda i, w: (w[MEMBER] * blocks + i, 0)), fixed(gain),
         (dh, (step_rows, model), tokens)] + [(a, (step_rows, model), tokens) for a in got],
        [(shape((share, model), f32), (step_rows, model), tokens)], (), after,
    )[0]


def collect(where, arrays, pieces, unit=1, after=()):
    count = arrays[0].shape[0] // pieces
    filled = sum(a.shape[1] for a in arrays)
    total = -(-filled // unit) * unit

    def body(w, ins, outs, scratch):
        at = 0
        for r in ins:
            n = r.shape[1]
            outs[0][:, at:at + n] = r[...]
            at += n
        if at < total:
            outs[0][:, at:] = jnp.zeros((count, total - at), bf16)

    return run(
        "collect", body, where, (1,),
        [(a, (count, a.shape[1]), lambda i, w: (w[PIECE], 0)) for a in arrays],
        [(shape((count, total), bf16), (count, total), lambda i, w: (0, 0))], (), after,
    )[0]


class Place:
    def __init__(self, rows):
        self.tensor = lax.axis_size("tensor")
        self.dp = lax.axis_size("dp")
        self.rows = rows
        self.group = self.tensor // rows
        self.at = lax.axis_index("tensor")
        self.dp_at = lax.axis_index("dp")
        self.bits = [1 << b for b in reversed(range(1, self.dp.bit_length() - 1))]

    def owner(self, at, step, turn):
        row, member = at // self.group, at % self.group
        return ((row + turn) % self.rows) * self.group + (member + step) % self.group

    def fetch(self, value, step, turn):
        pairs = [(self.owner(i, step, turn), i) for i in range(self.tensor)]
        return lax.ppermute(value, "tensor", pairs)

    def deliver(self, value, step, turn):
        pairs = [(i, self.owner(i, step, turn)) for i in range(self.tensor)]
        return lax.ppermute(value, "tensor", pairs)

    def swap(self, value, bit):
        return lax.ppermute(value, "dp", [(i, i ^ bit) for i in range(self.dp)])


class Chain:
    def __init__(self, where):
        self.where = where
        self.behind = ()

    def __call__(self, make, *args, extra=(), **keys):
        made = make(self.where, *args, after=self.behind + tuple(extra), **keys)
        outs = made if isinstance(made, (list, tuple)) else [made]
        self.behind = (min(outs, key=lambda a: a.size),)
        return made

    def sync(self, *values):
        out = lax.optimization_barrier((*values, *self.behind))
        self.behind = tuple(out[len(values):])
        return out[:len(values)]


def on_device(
    inputs, gain_attn, w_query, w_key, w_value, w_outgate, w_forget, forget_bias, w_out,
    gain_mlp, w_gate, w_up, w_down, segment_ids, cotangent,
):
    rows, length = segment_ids.shape
    here = Place(rows)
    group, pieces = here.group, here.dp
    heads, width, hidden = w_forget.shape[1], w_query.shape[1], w_gate.shape[1]
    model = inputs.shape[1]
    share = length // group
    row, member = here.at // group, here.at % group
    core, chip = here.dp_at % 2, here.dp_at // 2
    where = jnp.stack([row, member, core, chip, core * (pieces // 2) + chip]).astype(jnp.int32)
    go = Chain(where)
    gain_attn, gain_mlp = gain_attn[None], gain_mlp[None]
    segment = lax.dynamic_index_in_dim(segment_ids, row, 0, keepdims=False)
    scol, srow = segment[:, None], segment[None, :]
    turns = range(1, rows)
    slots = [(s, j) for s in range(group) for j in range(rows)]

    def to_member(value, step):
        return lax.ppermute(value, "tensor", [
            (i, (i // group) * group + (i % group + step) % group) for i in range(here.tensor)])

    class Gather:
        def __init__(self, piece):
            others = range(1, here.dp // 2)
            self.masks = [0] + sorted(others, key=lambda k: bin(k).count("1"))
            self.held = [piece] + [here.swap(piece, 2 * k) for k in self.masks[1:]]

        def wait(self):
            self.held[1:] = go.sync(*self.held[1:])

        def close(self):
            self.mine = go(assemble, self.held, self.masks)
            self.theirs = here.swap(self.mine, 1)
            return self.mine, self.theirs

    class Reduce:
        def __init__(self, send, keep, orders):
            self.parts = None
            self.keep, self.got, self.orders = keep, here.swap(send, 1), orders

        def hop(self):
            if self.parts is None:
                n = self.keep.shape[1]
                split = len(self.orders) if n % (128 * len(self.orders)) == 0 else 1
                entries = [(self.keep, self.got, list(here.bits), self.orders[c][0], c, n // split) for c in range(split)]
                orders = [order[1:] for order in self.orders[:split]]
            else:
                entries = [(kept, got, left, order[0], 0, kept.shape[1]) for kept, got, left, order in self.parts]
                orders = [order[1:] for _, _, _, order in self.parts]
            outs = go(fold, entries)
            self.parts = [
                [outs[2 * c + 1], here.swap(outs[2 * c], e[3]), [b for b in e[2] if b != e[3]], orders[c]]
                for c, e in enumerate(entries)
            ]

        def close(self):
            while self.parts is None or self.parts[0][3]:
                self.hop()
            sums = [kept.astype(f32) + got.astype(f32) for kept, got, _, _ in self.parts]
            return sums[0] if len(sums) == 1 else jnp.concatenate(sums, axis=1)

        def wait(self):
            got = go.sync(*([self.got] if self.parts is None else [p[1] for p in self.parts]))
            if self.parts is None:
                self.got = got[0]
            else:
                for p, g in zip(self.parts, got):
                    p[1] = g

    both_ways = [here.bits, here.bits[::-1]]

    attn_cut = [[w_query, w_key], [w_value, w_outgate, w_forget]]
    attn_counts = [sum(a.shape[1] for a in cut) for cut in attn_cut]
    attn_pieces = [go(collect, cut, pieces, 128) for cut in attn_cut]
    attn_got = [here.fetch(attn_pieces[0], 0, j) for j in turns]
    bias_got = [here.fetch(forget_bias, 0, j) for j in turns]
    own = go(project_own, length, inputs, gain_attn,
             [w_query, w_key, w_value, w_outgate, w_forget], forget_bias[None])
    normed, inverse_attn = own[:2]
    mixed = {0: own[2:]}
    gated = {}
    logs = {}

    def attend(j):
        q, k, v, g, _, _, crow = mixed[j]
        z, logs[j] = go(attend_forward, q, k, v, g, crow, scol, srow)
        gated[0, j] = z
        for s in range(1, group):
            gated[s, j] = here.fetch(z, s, 0)

    def wait_gated(j):
        arrived = go.sync(*[gated[s, j] for s in range(1, group)])
        for s in range(1, group):
            gated[s, j] = arrived[s - 1]

    out_piece = go(collect, [w_out], pieces)
    arrived = go.sync(*attn_got, *bias_got, attn_pieces[1], out_piece)
    attn_got, bias_got = arrived[:rows - 1], arrived[rows - 1:-2]
    attn_later = [here.fetch(arrived[-2], 0, j) for j in turns]
    attn_gather = [[Gather(p)] for p in attn_got]
    attend(0)
    out_got = [here.fetch(arrived[-1], 0, j) for j in turns]
    for gathers, p in zip(attn_gather, go.sync(*attn_later)):
        gathers[0].wait()
        gathers.append(Gather(p))
    attn_w = [[gathers[0].close()] for gathers in attn_gather]
    gate_piece = go(collect, [w_gate, w_up], pieces)
    wait_gated(0)
    out_got = go.sync(*out_got)
    out_own = jnp.concatenate([out_piece, *out_got], axis=1)
    out_peers = [here.fetch(out_own, s, 0) for s in range(1, group)]
    for gathers in attn_gather:
        gathers[1].wait()
    for done, gathers in zip(attn_w, attn_gather):
        done.append(gathers[1].close())
    gate_piece = go.sync(gate_piece)[0]
    gate_got = [here.fetch(gate_piece, 0, j) for j in turns]
    for j in turns:
        mixed[j] = go(project_other, normed, attn_w[j - 1], attn_counts, width, heads, bias_got[j - 1][None])
    out_peers = go.sync(*out_peers)
    out_gather = Gather(jnp.concatenate([*out_got, *out_peers], axis=1))
    for j in turns:
        attend(j)
    out_gather.wait()
    out_mine, out_theirs = out_gather.close()
    gate_got = go.sync(*gate_got)
    gate_gather = [Gather(p) for p in gate_got]
    down_piece = go(collect, [w_down], pieces)
    for j in turns:
        wait_gated(j)
    down_piece, out_theirs = go.sync(down_piece, out_theirs)
    down_got = [here.fetch(down_piece, 0, j) for j in turns]
    hidden_row, mlp_normed, inverse_mlp = go(
        close_attention, length, inputs, [gated[slot] for slot in slots], w_out, out_mine, out_theirs, gain_mlp
    )
    for gather in gate_gather:
        gather.wait()
    down_got = go.sync(*down_got)
    down_gather = [Gather(p) for p in down_got]

    def ffn(weights, before, final):
        return go(feed_forward, mlp_normed, cotangent, weights, hidden, gain_mlp, group, pieces, before, final)

    wide = BLK if hidden % BLK == 0 else hidden
    mlp_sums = {}
    send, keep, *carried = ffn([w_gate, w_up, w_down], [], False)
    gate_w = [gather.close() for gather in gate_gather]
    down_w = [gather.close() for gather in down_gather]
    mlp_sums[0] = Reduce(send, keep, both_ways)
    mlp_w = {}
    for j in turns:
        mlp_w[j] = gate_w[j - 1] + down_w[j - 1]
        if j < rows - 1:
            send, keep, *carried = ffn(mlp_w[j], carried, False)
            mlp_sums[j] = Reduce(send, keep, both_ways)
    mlp_sums[0].hop()
    du, dw, m, *made = ffn(mlp_w[rows - 1], carried, True)
    peers = list(range(1, group))
    part, out_part_own, gain_mlp_part = made[group - 1], made[2 * group - 1], made[2 * group]
    out_send = made[group:2 * group - 1]
    got = [to_member(v, s) for v, s in zip(made, peers)]
    mlp_sums[0].hop()
    mlp_sums[rows - 1] = Reduce(*go(lambda w, after: weight_grads(
        "mlp_grads", w, [mlp_normed, cotangent], [(0, [du]), (0, [dw]), (1, [m])], pieces, row_of=(1,), mixed=wide, after=after)), both_ways)
    dh, dh_low, dz_mine, dz_peers = go(
        close_feed_forward, share, group, part, got, hidden_row, inverse_mlp, gain_mlp, cotangent,
        w_out, out_mine, out_theirs,
    )
    dz_parts = [dz_mine]
    own_slots = rows * width
    for s in peers:
        lo = (group - s - 1) * own_slots
        dz_parts.append(here.fetch(dz_peers if group == 2 else dz_peers[:, lo:lo + own_slots], s, 0))
    mlp_sums[0].wait()
    mlp_own = mlp_sums[0].close()
    for j in turns:
        mlp_sums[j].hop()
    out_sum = Reduce(*go(lambda w, after: weight_grads(
        "out_grads", w, [dh_low], [(0, [gated[slot] for slot in slots])], pieces, True, after=after)), both_ways)

    back = {}
    attn_sums = {}
    per_step = together(heads) * HEAD

    def attend_back(j):
        q, k, v, g, forget, ccol, _ = mixed[j]
        parts = [(d, j * width // per_step) for d in dz_parts]
        if width % 128:
            parts = [(a[:, o * per_step:(o + 1) * per_step], 0) for a, o in parts]
        back[j] = go(attend_backward, q, k, v, g, gated[0, j], parts, logs[j], ccol, forget, scol, srow)

    def attn_grads(j, orders):
        attn_sums[j] = Reduce(*go(lambda w, after: weight_grads(
            "attn_grads", w, [normed], [(0, back[j][:2]), (0, back[j][2:5])], pieces, after=after)), orders)

    arrived = go.sync(*dz_parts[1:], *out_send)
    dz_parts[1:], out_send = arrived[:group - 1], arrived[group - 1:]
    out_got = [to_member(v, s) for v, s in zip(out_send, peers)]
    for j in turns:
        attend_back(j)
    for j in turns:
        mlp_sums[j].hop()
    for j in turns:
        attn_grads(j, both_ways)
    out_got = go.sync(*out_got)
    out_sum.hop()
    for j in turns:
        mlp_sums[j].wait()
    mlp_other = [here.deliver(low(mlp_sums[j].close()), 0, j) for j in turns]
    for j in turns:
        attn_sums[j].hop()
    attend_back(0)
    out_sum.hop()
    for j in turns:
        attn_sums[j].hop()
    attn_grads(0, both_ways)
    own_w = [w_query, w_key, w_value, w_outgate, w_forget]
    pair_terms = [
        (list(back[j][lo:hi]), *attn_w[j - 1][k]) for j in turns for k, (lo, hi) in enumerate(((0, 2), (2, 5)))
    ]

    def attn_back(name, steps):
        outs = []
        for s in steps:
            outs.append(go(lambda w, after: back_rows(
                name, w, s, group, list(back[0][:5]), own_w, pair_terms, normed, gain_attn, after)))
        return [o[0] for o in outs] + [sum(o[1] for o in outs)]

    mlp_other = go.sync(*mlp_other)
    for j in turns:
        attn_sums[j].wait()
    attn_other = [here.deliver(low(attn_sums[j].close()), 0, j) for j in turns]
    out_sum.wait()
    made = attn_back("attn_back_send", peers)
    got = [to_member(v, s) for v, s in zip(made, peers)]
    attn_sums[0].hop()
    out_part = out_sum.close().reshape(-1, group, rows, width)
    out_part = go.sync(out_part)[0]
    out_turned = [here.deliver(low(out_part[:, :, j]).reshape(-1, group * width), 0, j) for j in turns]
    part, gained = attn_back("attn_back_own", [0])
    bias_full = jnp.zeros((here.tensor, heads), f32)
    for j in range(rows):
        bias_full = lax.dynamic_update_slice(bias_full, back[j][5], (here.owner(here.at, 0, j), 0))
    small = jnp.concatenate([made[-1] + gained, gain_mlp_part, bias_full.reshape(1, -1)], axis=1)
    small_hops = [lambda v, b=b: here.swap(v, b) for b in [1] + here.bits] + [
        lambda v, b=b: lax.ppermute(v, "tensor", [(i, i ^ b) for i in range(here.tensor)])
        for b in [1 << k for k in range(here.tensor.bit_length() - 1)]]
    flying = small_hops.pop(0)(small)

    def small_step():
        arrived = go.sync(flying)[0]
        total = small + arrived
        return total, (small_hops.pop(0)(total) if small_hops else None)

    attn_other = go.sync(*attn_other)
    attn_sums[0].hop()
    small, flying = small_step()
    out_own, *arrived = go.sync(out_part_own, *out_got)
    output = lax.dynamic_slice_in_dim(hidden_row, member * share, share, 0) + out_own.astype(f32)
    for v in arrived:
        output = output + v.astype(f32)
    out_turned = go.sync(*out_turned, output)
    output = out_turned[-1]
    out_part = out_part[:, :, 0].reshape(-1, group * width) + sum(v.astype(f32) for v in out_turned[:-1])
    grad_out = out_part[:, :width]
    out_rest = [here.deliver(low(out_part[:, s * width:(s + 1) * width]), s, 0) for s in peers]
    small, flying = small_step()
    mlp_own, *mlp_other = go.sync(mlp_own, *mlp_other)
    attn_sums[0].wait()
    attn = attn_sums[0].close()
    while small_hops:
        small, flying = small_step()
    out_rest = go.sync(*out_rest)
    grad_inputs = go(close_block, share, group, part, got, inputs, inverse_attn, gain_attn, dh)
    small, flying = small_step()
    mlp = mlp_own
    for v in mlp_other:
        mlp = mlp + v.astype(f32)

    def columns(kind):
        return jnp.concatenate([mlp[:, b + kind * wide:b + (kind + 1) * wide] for b in range(0, 3 * hidden, 3 * wide)], axis=1)

    for v in out_rest:
        grad_out = grad_out + v.astype(f32)
    for v in attn_other:
        attn = attn + v.astype(f32)
    bias_own = lax.dynamic_slice_in_dim(small[0, 2 * model:], here.at * heads, heads, 0)
    return (
        output,
        grad_inputs,
        small[0, :model],
        attn[:, :width],
        attn[:, width:2 * width],
        attn[:, 2 * width:3 * width],
        attn[:, 3 * width:4 * width],
        attn[:, 4 * width:4 * width + heads],
        bias_own,
        grad_out,
        small[0, model:2 * model],
        columns(0),
        columns(1),
        columns(2),
    )


def solution(mesh):
    placed = (
        P("dp", None), P(), P(None, "tensor"), P(None, "tensor"), P(None, "tensor"),
        P(None, "tensor"), P(None, "tensor"), P("tensor"), P(None, "tensor"), P(),
        P(None, "tensor"), P(None, "tensor"), P(None, "tensor"), P("dp", None), P("dp", None),
    )
    weight = P("dp", "tensor")
    tokens = P(("dp", "tensor"), None)
    return jax.shard_map(
        on_device,
        mesh=mesh,
        in_specs=placed,
        out_specs=(
            tokens, tokens, P(), weight, weight, weight, weight, weight, P("tensor"),
            weight, P(), weight, weight, weight,
        ),
        check_vma=False,
    )
```
